128 devices in a mesh: dp: 32 (over x, y, core), seq: 4 (over z).
Axes of the slice: x: 4, y: 4, z: 4, core: 2. Of those that a mesh axis runs over, the one named last changes fastest.
Arguments:
- tokens: bfloat16 [32768, 1024], P(('dp', 'seq')), may hold values from -6 to 6
- routes: int32 [32768, 8], P(('dp', 'seq')), may hold values from 0 to 31, all different within a row; in each aligned block of 256 rows (0 to 255, 256 to 511, ...) at most 96 rows name the same one
- lengths: int32 [32], P('dp'), may hold values from 769 to 1024, as said below
- out_grad: bfloat16 [32768, 1024], P(('dp', 'seq')), may hold values from -6 to 6
- query_weight: float32 [1024, 1024], P(('dp', 'seq')), may hold values from -0.1875 to 0.1875
- query_mean: float32 [1024, 1024], P(('dp', 'seq')), may hold values from -128 to 128
- query_square: float32 [1024, 1024], P(('dp', 'seq')), may hold values from 1736.704 to 6881.28
- keyval_weight: float32 [1024, 1024], P(('dp', 'seq')), may hold values from -0.1875 to 0.1875
- keyval_mean: float32 [1024, 1024], P(('dp', 'seq')), may hold values from -128 to 128
- keyval_square: float32 [1024, 1024], P(('dp', 'seq')), may hold values from 1736.704 to 6881.28
- output_weight: float32 [1024, 1024], P(('dp', 'seq')), may hold values from -4 to 4
- output_mean: float32 [1024, 1024], P(('dp', 'seq')), may hold values from -4 to 4
- output_square: float32 [1024, 1024], P(('dp', 'seq')), may hold values from 3.2 to 12.8
- router_weight: float32 [1024, 32], P(('dp', 'seq')), may hold values from -0.09375 to 0.09375
- router_mean: float32 [1024, 32], P(('dp', 'seq')), may hold values from -256 to 256
- router_square: float32 [1024, 32], P(('dp', 'seq')), may hold values from 6881.28 to 27525.12
- norm_gains: float32 [2, 1024], P(None, ('dp', 'seq')), may hold values from 0.5 to 1.5
- gains_mean: float32 [2, 1024], P(None, ('dp', 'seq')), may hold values from -256 to 256
- gains_square: float32 [2, 1024], P(None, ('dp', 'seq')), may hold values from 6881.28 to 27525.12
- gateup_weight: float32 [32, 1024, 1024], P('dp', 'seq'), may hold values from -0.1875 to 0.1875
- gateup_mean: float32 [32, 1024, 1024], P('dp', 'seq'), may hold values from -14 to 14
- gateup_square: float32 [32, 1024, 1024], P('dp', 'seq'), may hold values from 24.90368 to 98.304
- down_weight: float32 [32, 512, 1024], P('dp', 'seq'), may hold values from -0.75 to 0.75
- down_mean: float32 [32, 512, 1024], P('dp', 'seq'), may hold values from -4 to 4
- down_square: float32 [32, 512, 1024], P('dp', 'seq'), may hold values from 1.540096 to 6.22592
Outputs:
- layer_out: bfloat16 [32768, 1024], P(('dp', 'seq'))
- tokens_grad: float32 [32768, 1024], P(('dp', 'seq'))
- query_updated: float32 [1024, 1024], P(('dp', 'seq'))
- querymean_new: float32 [1024, 1024], P(('dp', 'seq'))
- querysquare_new: float32 [1024, 1024], P(('dp', 'seq'))
- keyval_updated: float32 [1024, 1024], P(('dp', 'seq'))
- keyvalmean_new: float32 [1024, 1024], P(('dp', 'seq'))
- keyvalsquare_new: float32 [1024, 1024], P(('dp', 'seq'))
- output_updated: float32 [1024, 1024], P(('dp', 'seq'))
- outputmean_new: float32 [1024, 1024], P(('dp', 'seq'))
- outputsquare_new: float32 [1024, 1024], P(('dp', 'seq'))
- router_updated: float32 [1024, 32], P(('dp', 'seq'))
- routermean_new: float32 [1024, 32], P(('dp', 'seq'))
- routersquare_new: float32 [1024, 32], P(('dp', 'seq'))
- gains_updated: float32 [2, 1024], P(None, ('dp', 'seq'))
- gainsmean_new: float32 [2, 1024], P(None, ('dp', 'seq'))
- gainssquare_new: float32 [2, 1024], P(None, ('dp', 'seq'))
- gateup_updated: float32 [32, 1024, 1024], P('dp', 'seq')
- gateupmean_new: float32 [32, 1024, 1024], P('dp', 'seq')
- gateupsquare_new: float32 [32, 1024, 1024], P('dp', 'seq')
- down_updated: float32 [32, 512, 1024], P('dp', 'seq')
- downmean_new: float32 [32, 512, 1024], P('dp', 'seq')
- downsquare_new: float32 [32, 512, 1024], P('dp', 'seq')
The draws below stay inside these ranges and needn't reach their ends.
Inputs may be any that keep to these rules, and one draw needn't show every extreme that they name: `routes`: in the rows of one device no expert is named by more than 96 rows. `lengths`: one sequence has length 1024.
All inputs are finite; a program needn't handle non-finite values.
Results may differ from the reference program's by a relative error of at most 0.029.
Values may be sent and summed in bfloat16 or wider, within the bound.
A program may use at most 256 MiB of HBM per device.

```python
import math
import jax
import jax.numpy as jnp
import numpy as np
from jax import lax

D = 1024
HEADS = 16
KV_HEADS = 8
HEAD_DIM = 64
EXPERTS = 32
TOP = 8
FF_E = 512
TOK_DEV = 256
STEP = 10
CAP = 96
SEQ_LEN = 1024
TOKENS = 32768
N_DP = 32
N_SEQ = 4


def draw_lengths(key, part):
    key = jax.random.fold_in(key, 11)
    first_key, second_key = jax.random.split(key)
    values = jax.random.randint(first_key, (N_DP,), 3 * SEQ_LEN // 4 + 1, SEQ_LEN + 1)
    longest = jax.random.randint(second_key, (), 0, N_DP)
    return jnp.where(jnp.arange(N_DP) == longest, SEQ_LEN, values).astype(jnp.int32)


def block_levels(key, shape, pieces, smallest, high):
    loudness = 1.0
    for dim, shards_of in pieces:
        steps = jax.random.uniform(jax.random.fold_in(jax.random.fold_in(key, 6), dim), (shards_of,), jnp.float32, smallest / len(pieces), high / len(pieces))
        loudness = loudness * jnp.repeat(jnp.exp(steps), shape[dim] // shards_of).reshape((-1,) + (1,) * (len(shape) - 1 - dim))
    return loudness


def deal_out(key, own, number, rows, count, top, bound, lean):
    ranking = jax.random.permutation(key, count)
    heavy_load, common = shares(count, rows * top, bound, lean, True), shares(count, rows * top, bound, lean, False)
    places = jnp.arange(count)

    def named(sizes, rotation):
        used = int((sizes > 0).sum())
        fixed = max(1, used // 4)
        passed = fixed + (places - fixed + rotation * (used - fixed)) % max(1, count - fixed)
        return jnp.zeros((count,), jnp.int32).at[ranking[jnp.where(places < fixed, places, passed)]].set(jnp.asarray(sizes, jnp.int32))

    sizes = jnp.where(number % 4 == 0, named(heavy_load, number // 4), named(common, number - number // 4 - 1))
    mixed = jax.random.permutation(jax.random.fold_in(own, 3), count)
    giver, sink = mixed[0:count // 2 * 2:2], mixed[1:count // 2 * 2:2]
    room = jnp.minimum(sizes[giver] - 1, bound - sizes[sink]) // 2
    room = jnp.where((giver == ranking[0]) | (sink == ranking[0]) | (sizes[sink] == 0), 0, jnp.maximum(room, 0))
    passed = jax.random.randint(jax.random.fold_in(own, 4), (count // 2,), 0, 1 << 20) % (room + 1)
    sizes = sizes.at[giver].add(-passed).at[sink].add(passed)
    items = jnp.searchsorted(jnp.cumsum(sizes), jnp.arange(rows * top), side="right").astype(jnp.int32)
    grid = items.reshape(top, rows).T
    grid = grid[jax.random.permutation(jax.random.fold_in(own, 1), rows)]
    rotation = jax.random.randint(jax.random.fold_in(own, 2), (rows, 1), 0, top)
    return jnp.take_along_axis(grid, (jnp.arange(top)[None, :] + rotation) % top, axis=1)


def shares(count, total, bound, slope, full):
    weights = [(1 << 20) // math.isqrt(standing ** slope) + 1 for standing in range(1, count + 1)]
    largest = bound if full else min(bound, max(-(-total // count), total * weights[0] // sum(weights)))
    least = 1 if total - largest >= count - 1 else 0
    counts, surplus = [largest] + [least] * (count - 1), total - largest - least * (count - 1)
    while surplus > 0:
        candidates = [i for i in range(1, count) if counts[i] < largest] or [i for i in range(1, count) if counts[i] < bound]
        mass, remaining = sum([weights[i] for i in candidates]), surplus
        for i in candidates:
            addition = min(bound - counts[i], max(1, remaining * weights[i] // mass), surplus)
            counts[i] = counts[i] + addition
            surplus = surplus - addition
    return np.array(counts)


def centred(key, dims, width, bound, pieces=(), kind=jnp.bfloat16):
    values = width * jax.random.normal(key, dims, jnp.float32)
    if pieces:
        values = values * block_levels(key, dims, pieces, -0.22, 0.18)
    return jnp.clip(values, -bound, bound).astype(kind)


def setup_inputs(seed: int = 0) -> dict:
    key_list = jax.random.split(jax.random.key(seed), 26)
    tokens = centred(key_list[0], (TOKENS, D), 1.0, 6.0, ((0, 128),))
    routes_keys = jax.random.split(jax.random.fold_in(key_list[1], 1), TOKENS // TOK_DEV)
    routes_turns = jax.random.permutation(jax.random.fold_in(key_list[1], 3), TOKENS // TOK_DEV)
    routes = jax.vmap(lambda own, number: deal_out(jax.random.fold_in(key_list[1], 2), own, number, TOK_DEV, EXPERTS, TOP, CAP, 1))(routes_keys, routes_turns).reshape((TOKENS, TOP))
    lengths = draw_lengths(jax.random.fold_in(key_list[25], 71), 0)
    out_grad = centred(key_list[3], (TOKENS, D), 1.0, 6.0, ((0, 128),))
    query_weight = centred(key_list[4], (D, HEADS * HEAD_DIM), D ** -0.5, 0.1875, ((0, 128),), jnp.float32)
    query_mean = centred(key_list[5], (D, HEADS * HEAD_DIM), (0.11 * TOKENS ** 0.5), 128.0, ((0, 128),), jnp.float32)
    query_square = jnp.clip(jnp.exp(math.log(6881.28) - 1.3768156 * jax.random.uniform(key_list[6], (D, HEADS * HEAD_DIM), jnp.float32) ** block_levels(key_list[6], (D, HEADS * HEAD_DIM), ((0, 128),), -0.2, 0.2)), 1736.704, 6881.28)
    keyval_weight = centred(key_list[7], (D, 2 * KV_HEADS * HEAD_DIM), D ** -0.5, 0.1875, ((0, 128),), jnp.float32)
    keyval_mean = centred(key_list[8], (D, 2 * KV_HEADS * HEAD_DIM), (0.11 * TOKENS ** 0.5), 128.0, ((0, 128),), jnp.float32)
    keyval_square = jnp.clip(jnp.exp(math.log(6881.28) - 1.3768156 * jax.random.uniform(key_list[9], (D, 2 * KV_HEADS * HEAD_DIM), jnp.float32) ** block_levels(key_list[9], (D, 2 * KV_HEADS * HEAD_DIM), ((0, 128),), -0.2, 0.2)), 1736.704, 6881.28)
    output_weight = centred(key_list[10], (HEADS * HEAD_DIM, D), (max(1, 2 * HEADS * HEAD_DIM // SEQ_LEN)) ** -0.5, 4.0, ((0, 128),), jnp.float32)
    output_mean = centred(key_list[11], (HEADS * HEAD_DIM, D), (0.16 * N_DP ** 0.5), 4.0, ((0, 128),), jnp.float32)
    output_square = jnp.clip(jnp.exp(math.log(12.8) - 1.3862944 * jax.random.uniform(key_list[12], (HEADS * HEAD_DIM, D), jnp.float32) ** block_levels(key_list[12], (HEADS * HEAD_DIM, D), ((0, 128),), -0.2, 0.2)), 3.2, 12.8)
    router_weight = centred(key_list[13], (D, EXPERTS), (4 * D) ** -0.5, 0.09375, ((0, 128),), jnp.float32)
    router_mean = centred(key_list[14], (D, EXPERTS), (0.22 * TOKENS ** 0.5), 256.0, ((0, 128),), jnp.float32)
    router_square = jnp.clip(jnp.exp(math.log(27525.12) - 1.3862944 * jax.random.uniform(key_list[15], (D, EXPERTS), jnp.float32) ** block_levels(key_list[15], (D, EXPERTS), ((0, 128),), -0.2, 0.2)), 6881.28, 27525.12)
    norm_gains = jnp.clip(1.0 + 0.1 * jax.random.normal(key_list[16], (2, D), jnp.float32), 0.5, 1.5)
    gains_mean = centred(key_list[17], (2, D), (0.22 * TOKENS ** 0.5), 256.0, ((1, 128),), jnp.float32)
    gains_square = jnp.clip(jnp.exp(math.log(27525.12) - 1.3862944 * jax.random.uniform(key_list[18], (2, D), jnp.float32) ** block_levels(key_list[18], (2, D), ((1, 128),), -0.2, 0.2)), 6881.28, 27525.12)
    gateup_weight = centred(key_list[19], (EXPERTS, D, 2 * FF_E), D ** -0.5, 0.1875, ((0, 32), (1, 4)), jnp.float32)
    gateup_mean = centred(key_list[20], (EXPERTS, D, 2 * FF_E), (0.013 * TOKENS ** 0.5), 14.0, ((0, 32), (1, 4)), jnp.float32)
    gateup_square = jnp.clip(jnp.exp(math.log(98.304) - 1.3730491 * jax.random.uniform(key_list[21], (EXPERTS, D, 2 * FF_E), jnp.float32) ** block_levels(key_list[21], (EXPERTS, D, 2 * FF_E), ((0, 32), (1, 4)), -0.2, 0.2)), 24.90368, 98.304)
    down_weight = centred(key_list[22], (EXPERTS, FF_E, D), (FF_E // 8) ** -0.5, 0.75, ((0, 32), (1, 4)), jnp.float32)
    down_mean = centred(key_list[23], (EXPERTS, FF_E, D), (0.0033 * TOKENS ** 0.5), 4.0, ((0, 32), (1, 4)), jnp.float32)
    down_square = jnp.clip(jnp.exp(math.log(6.22592) - 1.3968765 * jax.random.uniform(key_list[24], (EXPERTS, FF_E, D), jnp.float32) ** block_levels(key_list[24], (EXPERTS, FF_E, D), ((0, 32), (1, 4)), -0.2, 0.2)), 1.540096, 6.22592)
    return dict(tokens=tokens, routes=routes, lengths=lengths, out_grad=out_grad, query_weight=query_weight, query_mean=query_mean, query_square=query_square, keyval_weight=keyval_weight, keyval_mean=keyval_mean, keyval_square=keyval_square, output_weight=output_weight, output_mean=output_mean, output_square=output_square, router_weight=router_weight, router_mean=router_mean, router_square=router_square, norm_gains=norm_gains, gains_mean=gains_mean, gains_square=gains_square, gateup_weight=gateup_weight, gateup_mean=gateup_mean, gateup_square=gateup_square, down_weight=down_weight, down_mean=down_mean, down_square=down_square)


@jax.custom_vjp
def low(v):
    return lax.optimization_barrier(v.astype(jnp.bfloat16)).astype(jnp.float32)

@jax.custom_vjp
def low_back(v):
    return v

def low_keep(v):
    return (low(v), None)

def low_pass(kept, grad):
    return (grad,)

def back_keep(v):
    return (v, None)

def back_low(kept, grad):
    return (low(grad),)
low.defvjp(low_keep, low_pass)
low_back.defvjp(back_keep, back_low)
norm_epsilon = 1e-06
beta_first = 0.9
beta_second = 0.95
adam_epsilon = 1e-08
masked_score = -1e+30
highest = lax.Precision.HIGHEST

def rotary_tables(positions, half_width):
    freqs = 10000.0 ** (-jnp.arange(half_width, dtype=jnp.float32) / half_width)
    angles = positions.astype(jnp.float32)[:, None] * freqs[None, :]
    cosines = jnp.cos(angles)
    sines = jnp.sin(angles)
    return (jnp.concatenate([cosines, cosines], 1), jnp.concatenate([sines, sines], 1))

def rotate(values, cosines, sines):
    half_width = values.shape[-1] // 2
    turned = jnp.concatenate([-values[..., half_width:], values[..., :half_width]], -1)
    return values * cosines[:, None, :] + turned * sines[:, None, :]

def rms_normed(values, gain):
    return values * lax.rsqrt(lax.optimization_barrier(jnp.mean(values * values, axis=-1, keepdims=True)) + norm_epsilon) * gain

def lane_table(routes):
    blocks = routes.reshape(N_DP * N_SEQ, TOK_DEV * TOP)
    route_hits = (blocks[:, :, None] == jnp.arange(EXPERTS, dtype=jnp.int32)[None, None, :]).astype(jnp.int32)
    slot_ranks = lax.optimization_barrier(jnp.sum((jnp.cumsum(route_hits, axis=1) - 1) * route_hits, axis=2))
    offsets = jnp.arange(N_DP * N_SEQ, dtype=jnp.int32) % N_SEQ * CAP
    return (slot_ranks + offsets[:, None]).reshape(N_DP, SEQ_LEN, TOP)

def layer(weights, xgroup, length, route_group, lane_group):
    query_w, keyval_w, output_w, router_w, gains_w, gateup_w, down_w = weights
    positions = jnp.arange(SEQ_LEN, dtype=jnp.int32)
    cosines, sines = rotary_tables(positions, HEAD_DIM // 2)
    key_width = KV_HEADS * HEAD_DIM
    normed = low(rms_normed(xgroup, gains_w[0]))
    queries = low_back(jnp.dot(normed, query_w, precision=highest))
    keyvals = low_back(jnp.dot(normed, keyval_w, precision=highest))
    rotated_q = low(rotate(queries.reshape(SEQ_LEN, HEADS, HEAD_DIM), cosines, sines))
    rotated_k = low(rotate(keyvals[:, :key_width].reshape(SEQ_LEN, KV_HEADS, HEAD_DIM), cosines, sines))
    value_rows = low(keyvals[:, key_width:].reshape(SEQ_LEN, KV_HEADS, HEAD_DIM))
    grouped = rotated_q.reshape(SEQ_LEN, KV_HEADS, HEADS // KV_HEADS, HEAD_DIM)
    raw_scores = jnp.einsum('qkgd,pkd->kgqp', grouped, rotated_k, precision=highest) * HEAD_DIM ** (-0.5)
    scores = low_back(raw_scores)
    allowed = (positions[None, :] <= positions[:, None]) & (positions[None, :] < length)
    attention = jax.nn.softmax(jnp.where(allowed, scores, masked_score), axis=-1)
    mixed_heads = jnp.einsum('kgqp,pkd->qkgd', low(attention), value_rows, precision=highest)
    heads_out = low(low_back(mixed_heads.reshape(SEQ_LEN, HEADS * HEAD_DIM)))
    attended = low_back(jnp.dot(heads_out, output_w, precision=highest))
    residual = xgroup + attended
    normed_two = low(rms_normed(residual, gains_w[1]))
    logits = low_back(jnp.dot(normed_two, router_w, precision=highest))
    chosen = jnp.take_along_axis(logits, route_group, axis=1)
    gate_probs = jax.nn.softmax(chosen, axis=-1)
    token_ids = jnp.broadcast_to(jnp.arange(SEQ_LEN, dtype=jnp.int32)[:, None], route_group.shape)
    source = jnp.full((EXPERTS, N_SEQ * CAP), -1, jnp.int32).at[route_group, lane_group].set(token_ids)
    filled = source >= 0
    expert_rows = low_back(jnp.where(filled[:, :, None], normed_two[jnp.maximum(source, 0)], 0.0))
    gateup = low_back(jnp.einsum('erd,edf->erf', expert_rows, gateup_w, precision=highest))
    hidden = low(jax.nn.silu(gateup[..., :FF_E]) * gateup[..., FF_E:])
    expert_out = low(low_back(jnp.einsum('erf,efd->erd', hidden, down_w, precision=highest)))
    picked = expert_out[route_group, lane_group]
    return residual + lax.optimization_barrier(jnp.sum(gate_probs[:, :, None] * picked, axis=1))

def adamw(weight, grad, first, second, rate, decay):
    first_new = beta_first * first + (1.0 - beta_first) * grad
    second_new = beta_second * second + (1.0 - beta_second) * grad * grad
    update = first_new / (1.0 - beta_first ** STEP) / (jnp.sqrt(second_new / (1.0 - beta_second ** STEP)) + adam_epsilon)
    return (weight - rate * (update + decay * weight), first_new, second_new)

def reference(tokens, routes, lengths, out_grad, query_weight, query_mean, query_square, keyval_weight, keyval_mean, keyval_square, output_weight, output_mean, output_square, router_weight, router_mean, router_square, norm_gains, gains_mean, gains_square, gateup_weight, gateup_mean, gateup_square, down_weight, down_mean, down_square):
    lanes = lane_table(routes)
    route_groups = routes.reshape(N_DP, SEQ_LEN, TOP)

    def forward(inputs, *weights):
        rounded = tuple((low(weight) for weight in weights))

        def step(carry, item):
            xgroup, length, route_group, lane_group = item
            return (carry, jax.checkpoint(layer)(rounded, xgroup, length, route_group, lane_group))
        _, outputs = lax.scan(step, None, (inputs.reshape(N_DP, SEQ_LEN, D), lengths, route_groups, lanes))
        return outputs.reshape(N_DP * SEQ_LEN, D)
    weights = (query_weight, keyval_weight, output_weight, router_weight, norm_gains, gateup_weight, down_weight)
    result, pullback = jax.vjp(forward, tokens.astype(jnp.float32), *weights)
    grads = pullback(out_grad.astype(jnp.float32))
    base_rate = 0.5
    rates = (base_rate * D ** (-0.5), base_rate * D ** (-0.5), base_rate * max(1, 2 * HEADS * HEAD_DIM // SEQ_LEN) ** (-0.5), base_rate * (4 * D) ** (-0.5), 0.6, base_rate * D ** (-0.5), base_rate * (FF_E // 8) ** (-0.5))
    decays = (0.1, 0.1, 0.1, 0.1, 0.0, 0.1, 0.1)
    firsts = (query_mean, keyval_mean, output_mean, router_mean, gains_mean, gateup_mean, down_mean)
    seconds = (query_square, keyval_square, output_square, router_square, gains_square, gateup_square, down_square)
    updated = [adamw(weights[index], grads[index + 1], firsts[index], seconds[index], rates[index], decays[index]) for index in range(7)]
    return (result.astype(jnp.bfloat16), grads[0], updated[0][0], updated[0][1], updated[0][2], updated[1][0], updated[1][1], updated[1][2], updated[2][0], updated[2][1], updated[2][2], updated[3][0], updated[3][1], updated[3][2], updated[4][0], updated[4][1], updated[4][2], updated[5][0], updated[5][1], updated[5][2], updated[6][0], updated[6][1], updated[6][2])
```

```python
import jax
import jax.numpy as jnp
from jax import lax
from jax.experimental import pallas as pl
from jax.experimental.pallas import tpu as pltpu
from jax.sharding import PartitionSpec as P

MESH = pl.DeviceIdType.MESH
bf16 = jnp.bfloat16
f32 = jnp.float32
AXES = "xycz"


def place():
    dp = lax.axis_index("dp")
    return {"x": dp // 8, "y": (dp // 2) % 4, "c": dp % 2, "z": lax.axis_index("seq")}


def device(at):
    return ((at["x"] * 4 + at["y"]) * 2 + at["c"], at["z"])


def shift(at, axis, by):
    size = 2 if axis == "c" else 4
    return lax.rem(at[axis] + by, size)


def peer(at, axis, by):
    return device({**at, axis: shift(at, axis, by)})


def greet(at, axes):
    barrier = pltpu.get_barrier_semaphore()
    count = 0
    for axis in axes:
        for by in (1,) if axis == "c" else (1, 2, 3):
            pl.semaphore_signal(
                barrier, inc=1, device_id=peer(at, axis, by), device_id_type=MESH
            )
            count += 1
    pl.semaphore_wait(barrier, count)


class Wires:
    def __init__(self, send_sems, recv_sems, local_sems=None):
        self.send_sems, self.recv_sems, self.local_sems = send_sems, recv_sems, local_sems
        self.copies, self.local = [], 0

    def send(self, src, dst, target):
        at = len(self.copies)
        copy = pltpu.make_async_remote_copy(
            src_ref=src,
            dst_ref=dst,
            send_sem=self.send_sems.at[at],
            recv_sem=self.recv_sems.at[at],
            device_id=target,
            device_id_type=MESH,
        )
        copy.start()
        self.copies.append(copy)
        return copy

    def keep(self, src, dst):
        copy = pltpu.make_async_copy(src, dst, self.local_sems.at[self.local])
        copy.start()
        self.local += 1
        return copy

    def finish(self):
        for copy in self.copies:
            copy.wait_send()


def index(at, whole, **fixed):
    spots = {**at, **fixed}
    return tuple(slice(None) if axis in whole else spots[axis] for axis in AXES)


GATHER_ORDERS = ("zyx", "xzy", "yxz")


def gather_front_kernel(
    wq, wkv, wo, tok, oq, okv, oo, ot, send_sems, recv_sems, local_sems
):
    at = place()
    wires = Wires(send_sems, recv_sems, local_sems)
    parts = list(zip((wq, wkv, wo), (oq, okv, oo), GATHER_ORDERS))
    kept = [wires.keep(w, o.at[index(at, "")]) for w, o, _ in parts]
    kept.append(wires.keep(tok, ot.at[at["z"]]))
    greet(at, "xyzc")
    arrivals = {}
    for p, (w, o, order) in enumerate(parts):
        for by in (1, 3, 2):
            arrivals[p, by] = wires.send(w, o.at[index(at, "")], peer(at, order[0], by))
    half = tok.shape[0] // 2
    low, high = pl.ds(0, half), pl.ds(half, half)
    z = at["z"]
    from_left = wires.send(tok, ot.at[z], peer(at, "z", 1))
    from_right = wires.send(tok, ot.at[z], peer(at, "z", 3))
    for copy in kept:
        copy.wait()
    for stage in (1, 2):
        later = {}
        for p, (w, o, order) in enumerate(parts):
            for by in (1, 3, 2):
                arrivals[p, by].wait_recv()
            spot = index(at, order[:stage])
            for by in (1, 3, 2):
                later[p, by] = wires.send(o.at[spot], o.at[spot], peer(at, order[stage], by))
        arrivals = later
    sibling = peer(at, "c", 1)
    across = []
    for p, (w, o, order) in enumerate(parts):
        spot = index(at, order[:2])
        across.append(wires.send(o.at[spot], o.at[spot], sibling))
    from_left.wait_recv()
    left, right = shift(at, "z", 3), shift(at, "z", 1)
    far = [wires.send(ot.at[left, low], ot.at[left, low], peer(at, "z", 1))]
    from_right.wait_recv()
    far.append(wires.send(ot.at[right, high], ot.at[right, high], peer(at, "z", 3)))
    for by in (1, 3, 2):
        for p, (w, o, order) in enumerate(parts):
            arrivals[p, by].wait_recv()
            spot = index(at, order[:2], **{order[2]: shift(at, order[2], 4 - by)})
            across.append(wires.send(o.at[spot], o.at[spot], sibling))
    for copy in far + across:
        copy.wait_recv()
    wires.finish()


def gather_front(wq, wkv, wo, tok):
    shapes = [pltpu.HBM((4, 4, 2, 4) + w.shape, w.dtype) for w in (wq, wkv, wo)]
    shapes.append(pltpu.HBM((4,) + tok.shape, tok.dtype))
    count = 9 * 3 + 4 + 12
    return pl.pallas_call(
        gather_front_kernel,
        out_shape=shapes,
        in_specs=[pl.BlockSpec(memory_space=pltpu.HBM)] * 4,
        out_specs=[pl.BlockSpec(memory_space=pltpu.HBM)] * 4,
        scratch_shapes=[
            pltpu.SemaphoreType.DMA((count,)),
            pltpu.SemaphoreType.DMA((count,)),
            pltpu.SemaphoreType.DMA((4,)),
        ],
        compiler_params=pltpu.CompilerParams(collective_id=1, has_side_effects=True),
        name="gather_front",
    )(*(pltpu.with_memory_space_constraint(v, pltpu.HBM) for v in (wq, wkv, wo, tok)))


PLANE_ORDERS = ("xy", "yx")


def gather_plane_kernel(n, o, send_sems, recv_sems, local_sems):
    at = place()
    wires = Wires(send_sems, recv_sems, local_sems)
    half = n.shape[0] // 2
    rows = [pl.ds(0, half), pl.ds(half, half)]

    def spot(h, **fixed):
        where = {**at, **fixed}
        return o.at[where["x"], where["y"], where["c"], rows[h]]

    mine = o.at[at["x"], at["y"], at["c"]]
    kept = wires.keep(n, mine)
    greet(at, "xyc")
    sibling = peer(at, "c", 1)
    first, second, across = {}, {}, []
    for by in (1, 3, 2):
        for h in (0, 1):
            axis = PLANE_ORDERS[h][0]
            first[h, by] = wires.send(n.at[rows[h]], spot(h), peer(at, axis, by))
    for h in (0, 1):
        axis = PLANE_ORDERS[h][1]
        for to in (1, 3):
            second[h, 0, to] = wires.send(n.at[rows[h]], spot(h), peer(at, axis, to))
    across.append(wires.send(n, mine, sibling))
    for by in (1, 3, 2):
        for h in (0, 1):
            one, two = PLANE_ORDERS[h]
            first[h, by].wait_recv()
            unit = spot(h, **{one: shift(at, one, 4 - by)})
            for to in (1, 3):
                second[h, by, to] = wires.send(unit, unit, peer(at, two, to))
            across.append(wires.send(unit, unit, sibling))
    far = []
    for by in (0, 1, 3, 2):
        for h in (0, 1):
            one, two = PLANE_ORDERS[h]
            for to in (1, 3):
                second[h, by, to].wait_recv()
                unit = spot(
                    h, **{one: shift(at, one, (4 - by) % 4), two: shift(at, two, 4 - to)}
                )
                if (to == 1) == (by in (0, 3)):
                    far.append(((h, by, to), wires.send(unit, unit, peer(at, two, to))))
                across.append(wires.send(unit, unit, sibling))
    for (h, by, to), copy in far:
        one, two = PLANE_ORDERS[h]
        copy.wait_recv()
        unit = spot(h, **{one: shift(at, one, (4 - by) % 4), two: shift(at, two, 2)})
        across.append(wires.send(unit, unit, sibling))
    for copy in across:
        copy.wait_recv()
    kept.wait()
    wires.finish()


def gather_plane(n, collective_id):
    count = 6 + 16 + 8 + 31
    return pl.pallas_call(
        gather_plane_kernel,
        out_shape=pltpu.HBM((4, 4, 2) + n.shape, n.dtype),
        in_specs=[pl.BlockSpec(memory_space=pltpu.HBM)],
        out_specs=pl.BlockSpec(memory_space=pltpu.HBM),
        scratch_shapes=[
            pltpu.SemaphoreType.DMA((count,)),
            pltpu.SemaphoreType.DMA((count,)),
            pltpu.SemaphoreType.DMA((1,)),
        ],
        compiler_params=pltpu.CompilerParams(
            collective_id=collective_id, has_side_effects=True
        ),
        name="gather_plane",
    )(pltpu.with_memory_space_constraint(n, pltpu.HBM))


STRIP = 16


def add_rows(out, parts, rows):
    def strip(i, carry):
        span = pl.ds(pl.multiple_of(i * STRIP, STRIP), STRIP)
        total = parts[0][span].astype(f32)
        for part in parts[1:]:
            total = total + part[span].astype(f32)
        out[span] = total.astype(out.dtype)
        return carry

    lax.fori_loop(0, rows // STRIP, strip, 0)


def sum_plane_kernel(
    c_ref, out, held, crossed, near, mid, last, send_sems, recv_sems, local_sems
):
    at = place()
    wires = Wires(send_sems, recv_sems, local_sems)
    whole = out.shape[0]
    half = whole // 2
    rows = [pl.ds(0, half), pl.ds(half, half)]
    orders = ("yx", "xy")
    blocks = [(2, 2), (0, 2), (2, 0), (1, 2), (2, 1), (3, 2), (2, 3)]
    blocks += [(0, 1), (1, 0), (0, 3), (3, 0), (1, 1), (3, 3), (1, 3), (3, 1), (0, 0)]
    other = shift(at, "c", 1)

    def spot(dx, dy):
        return shift(at, "x", dx), shift(at, "y", dy)

    kept = [
        wires.keep(c_ref.at[spot(*b) + (at["c"],)], held.at[spot(*b)]) for b in blocks
    ]
    greet(at, "xyc")
    sibling = peer(at, "c", 1)
    crossing = {}
    for b in blocks:
        crossing[b] = wires.send(
            c_ref.at[spot(*b) + (other,)], crossed.at[spot(*b)], sibling
        )

    def unit(h, d1, d2):
        dx, dy = (d2, d1) if h == 0 else (d1, d2)
        return held.at[spot(dx, dy) + (rows[h],)]

    step1, step2 = {}, {}

    def settle(b, number):
        kept[number].wait()
        crossing[b].wait_recv()
        add_rows(held.at[spot(*b)], [held.at[spot(*b)], crossed.at[spot(*b)]], whole)

    for number, b in enumerate(blocks):
        settle(b, number)
        for h in (0, 1):
            d1, d2 = (b[1], b[0]) if h == 0 else (b[0], b[1])
            axis = orders[h][0]
            if d1 == 2:
                to = 1 if d2 < 2 else 3
                step1[h, d2] = wires.send(
                    unit(h, 2, d2), near.at[h, d2], peer(at, axis, to)
                )
            elif (d1 == 1 and d2 >= 2) or (d1 == 3 and d2 < 2):
                step2[h, d1, d2] = wires.send(
                    unit(h, d1, d2), mid.at[h, d1 // 2, d2], peer(at, axis, d1)
                )
    for d2 in (0, 2, 1, 3):
        for h in (0, 1):
            d1 = 1 if d2 < 2 else 3
            axis = orders[h][0]
            step1[h, d2].wait_recv()
            add_rows(unit(h, d1, d2), [unit(h, d1, d2), near.at[h, d2]], half)
            step2[h, d1, d2] = wires.send(
                unit(h, d1, d2), mid.at[h, d1 // 2, d2], peer(at, axis, d1)
            )
    ends = {}
    for d2 in (2, 1, 3, 0):
        for h in (0, 1):
            for d1 in (1, 3):
                step2[h, d1, d2].wait_recv()
            add_rows(
                unit(h, 0, d2), [unit(h, 0, d2), mid.at[h, 0, d2], mid.at[h, 1, d2]], half
            )
            if d2:
                ends[h, d2] = wires.send(
                    unit(h, 0, d2), last.at[h, d2 - 1], peer(at, orders[h][1], d2)
                )
    for h in (0, 1):
        for d2 in (1, 3, 2):
            ends[h, d2].wait_recv()
        add_rows(
            out.at[rows[h]],
            [unit(h, 0, 0), last.at[h, 0], last.at[h, 1], last.at[h, 2]],
            half,
        )
    wires.finish()


def sum_plane(c, collective_id, dtype):
    rows, width = c.shape[-2:]
    half = rows // 2
    count = 16 + 8 + 16 + 6
    return pl.pallas_call(
        sum_plane_kernel,
        out_shape=jax.ShapeDtypeStruct((rows, width), dtype),
        in_specs=[pl.BlockSpec(memory_space=pltpu.HBM)],
        out_specs=pl.BlockSpec(memory_space=pltpu.VMEM),
        scratch_shapes=[
            pltpu.VMEM((4, 4, rows, width), bf16),
            pltpu.VMEM((4, 4, rows, width), bf16),
            pltpu.VMEM((2, 4, half, width), bf16),
            pltpu.VMEM((2, 2, 4, half, width), bf16),
            pltpu.VMEM((2, 3, half, width), bf16),
            pltpu.SemaphoreType.DMA((count,)),
            pltpu.SemaphoreType.DMA((count,)),
            pltpu.SemaphoreType.DMA((16,)),
        ],
        compiler_params=pltpu.CompilerParams(
            collective_id=collective_id,
            has_side_effects=True,
            vmem_limit_bytes=56 * 1024 * 1024,
        ),
        name="sum_plane",
    )(pltpu.with_memory_space_constraint(c, pltpu.HBM))


SUM_ORDERS = ("xyz", "yzx", "zxy")


def pick(ref, axes, axis, mine):
    return ref.at[tuple(mine if a == axis else slice(None) for a in axes)]


def sum_back_kernel(*refs):
    mats, dn1 = refs[0:3], refs[3]
    outs, dn1_out = refs[4:7], refs[7]
    scratch = refs[8:-3]
    send_sems, recv_sems, local_sems = refs[-3:]
    crossed, held, one, two, three, sum1, sum2 = [scratch[i * 3 : i * 3 + 3] for i in range(7)]
    zmid, zlast, znear = scratch[21:24]
    at = place()
    wires = Wires(send_sems, recv_sems, local_sems)
    greet(at, "xyzc")
    sibling = peer(at, "c", 1)
    other = shift(at, "c", 1)
    crossing = [
        wires.send(mats[p].at[:, :, other], crossed[p], sibling) for p in range(3)
    ]
    half = dn1.shape[1] // 2
    low, high = pl.ds(0, half), pl.ds(half, half)
    z = at["z"]
    ahead, back, far = shift(at, "z", 1), shift(at, "z", 3), shift(at, "z", 2)
    up, down = peer(at, "z", 1), peer(at, "z", 3)
    znear_l = wires.send(dn1.at[far, low], znear.at[0], up)
    znear_r = wires.send(dn1.at[far, high], znear.at[1], down)
    zpure_l = wires.send(dn1.at[ahead, high], zlast.at[0, high], up)
    zpure_r = wires.send(dn1.at[back, low], zlast.at[1, low], down)

    def total(out, parts, count):
        def body(i, carry):
            value = parts[0][i].astype(f32)
            for part in parts[1:]:
                value = value + part[i].astype(f32)
            out[i] = value.astype(out.dtype)
            return carry

        lax.fori_loop(0, count, body, 0)

    stage1 = {}
    for p in range(3):
        crossing[p].wait_recv()

        def body(i, carry, p=p):
            mine = mats[p][i // 4, i % 4, at["c"]]
            held[p][i // 4, i % 4] = (
                mine.astype(f32) + crossed[p][i // 4, i % 4].astype(f32)
            ).astype(bf16)
            return carry

        lax.fori_loop(0, 16, body, 0)
        axis = SUM_ORDERS[p][0]
        for by in (2, 1, 3):
            stage1[p, by] = wires.send(
                pick(held[p], "xyz", axis, shift(at, axis, by)),
                one[p].at[by - 1],
                peer(at, axis, by),
            )
    znear_l.wait_recv()
    add_rows(zmid.at[0], [dn1.at[ahead, low], znear.at[0]], half)
    zsum_l = wires.send(zmid.at[0], zlast.at[0, low], up)
    znear_r.wait_recv()
    add_rows(zmid.at[1], [dn1.at[back, high], znear.at[1]], half)
    zsum_r = wires.send(zmid.at[1], zlast.at[1, high], down)
    stage2 = {}
    for p in range(3):
        axis, after = SUM_ORDERS[p][0], SUM_ORDERS[p][1]
        rest = "xyz".replace(axis, "")
        for by in (1, 3, 2):
            stage1[p, by].wait_recv()
        total(
            sum1[p],
            [pick(held[p], "xyz", axis, at[axis])] + [one[p].at[k] for k in range(3)],
            4,
        )
        for by in (2, 1, 3):
            stage2[p, by] = wires.send(
                pick(sum1[p], rest, after, shift(at, after, by)),
                two[p].at[by - 1],
                peer(at, after, by),
            )
    stage3 = {}
    for p in range(3):
        axis, after, end = SUM_ORDERS[p]
        rest = "xyz".replace(axis, "")
        for by in (1, 3, 2):
            stage2[p, by].wait_recv()
        total(
            sum2[p],
            [pick(sum1[p], rest, after, at[after])] + [two[p].at[k] for k in range(3)],
            4,
        )
        for by in (2, 1, 3):
            stage3[p, by] = wires.send(
                sum2[p].at[shift(at, end, by)], three[p].at[by - 1], peer(at, end, by)
            )
    for copy in (zpure_l, zsum_l, zpure_r, zsum_r):
        copy.wait_recv()
    add_rows(dn1_out, [dn1.at[z], zlast.at[0], zlast.at[1]], 2 * half)
    for p in range(3):
        for by in (1, 3, 2):
            stage3[p, by].wait_recv()
        value = sum2[p][at[SUM_ORDERS[p][2]]].astype(f32)
        for k in range(3):
            value = value + three[p][k].astype(f32)
        outs[p][...] = value
    wires.finish()


def sum_back(mats, dn1):
    widths = [m.shape[-1] for m in mats]
    rows, model = dn1.shape[1:]
    count = 3 * 10 + 6
    scratch = []
    for lead in ((4, 4, 4), (4, 4, 4), (3, 4, 4), (3, 4), (3,), (4, 4), (4,)):
        scratch += [pltpu.VMEM(lead + (16, w), bf16) for w in widths]
    scratch += [
        pltpu.VMEM((2, rows // 2, model), bf16),
        pltpu.VMEM((2, rows, model), bf16),
        pltpu.VMEM((2, rows // 2, model), bf16),
        pltpu.SemaphoreType.DMA((count,)),
        pltpu.SemaphoreType.DMA((count,)),
        pltpu.SemaphoreType.DMA((1,)),
    ]
    vmem = pl.BlockSpec(memory_space=pltpu.VMEM)
    return pl.pallas_call(
        sum_back_kernel,
        out_shape=[jax.ShapeDtypeStruct((16, w), f32) for w in widths]
        + [jax.ShapeDtypeStruct((rows, model), f32)],
        in_specs=[vmem] * 4,
        out_specs=[vmem] * 4,
        scratch_shapes=scratch,
        compiler_params=pltpu.CompilerParams(
            collective_id=4, has_side_effects=True, vmem_limit_bytes=56 * 1024 * 1024
        ),
        name="sum_back",
    )(*mats, dn1)


D = 1024
HEADS = 16
KV_HEADS = 8
HEAD_DIM = 64
EXPERTS = 32
FF_E = 512
STEP = 10
CAP = 96
TOK = 256


norm_epsilon = 1e-06
beta_first = 0.9
beta_second = 0.95
adam_epsilon = 1e-08
masked_score = -1e30


def rotary_tables(positions, half_width):
    freqs = 10000.0 ** (-jnp.arange(half_width, dtype=jnp.float32) / half_width)
    angles = positions.astype(jnp.float32)[:, None] * freqs[None, :]
    cosines = jnp.cos(angles)
    sines = jnp.sin(angles)
    return (jnp.concatenate([cosines, cosines], 1), jnp.concatenate([sines, sines], 1))


def rotate(values, cosines, sines):
    half_width = values.shape[-1] // 2
    turned = jnp.concatenate([-values[..., half_width:], values[..., :half_width]], -1)
    return values * cosines[:, None, :] + turned * sines[:, None, :]


def rotate_back(grads, cosines, sines):
    half_width = grads.shape[-1] // 2
    scaled = grads * sines[:, None, :]
    return grads * cosines[:, None, :] + jnp.concatenate(
        [scaled[..., half_width:], -scaled[..., :half_width]], -1
    )


def rms_scale(values):
    return lax.rsqrt(jnp.mean(values * values, axis=-1, keepdims=True) + norm_epsilon)


def norm_back(values, scale, gain, dnormed):
    scaled = values * scale
    dgain = jnp.sum(dnormed * scaled, axis=0)
    dscaled = dnormed * gain
    dvalues = scale * (dscaled - scaled * jnp.mean(dscaled * scaled, axis=-1, keepdims=True))
    return (dvalues, dgain)


def masked_scores(grouped, whole_kv, positions, length):
    key_count = whole_kv.shape[0]
    key_width = whole_kv.shape[1] // 2
    heads_kv = grouped.shape[1]
    head_size = grouped.shape[3]
    all_keys = whole_kv[:, :key_width].reshape(key_count, heads_kv, head_size)
    all_values = whole_kv[:, key_width:].reshape(key_count, heads_kv, head_size)
    raw_scores = jnp.einsum(
        "qkgd,pkd->kgqp", grouped, all_keys, preferred_element_type=jnp.float32
    ) * head_size ** (-0.5)
    key_pos = jnp.arange(key_count, dtype=jnp.int32)
    allowed = (key_pos[None, :] <= positions[:, None]) & (key_pos[None, :] < length)
    return (jnp.where(allowed, raw_scores, masked_score), all_keys, all_values)


def adamw(weight, grad, first, second, rate, decay):
    first_new = beta_first * first + (1.0 - beta_first) * grad
    second_new = beta_second * second + (1.0 - beta_second) * grad * grad
    update = (
        first_new
        / (1.0 - beta_first**STEP)
        / (jnp.sqrt(second_new / (1.0 - beta_second**STEP)) + adam_epsilon)
    )
    return (weight - rate * (update + decay * weight), first_new, second_new)


GROUP = 4


def matmul(a, b, contract):
    return lax.dot_general(
        a, b, (((contract[0],), (contract[1],)), ((), ())), preferred_element_type=f32
    )


def expert_kernel(n_ref, g_ref, w_ref, dn_ref, out_ref, dw_ref, xs, ds, dzs, gys, acc_gu, acc_d):
    step = pl.program_id(0)
    expert = lax.axis_index("dp")

    @pl.when(step == 0)
    def _():
        acc_gu[...] = jnp.zeros_like(acc_gu)
        acc_d[...] = jnp.zeros_like(acc_d)

    lane8 = lax.broadcasted_iota(jnp.int32, (8, 128), 1)
    sub8 = lax.broadcasted_iota(jnp.int32, (8, 128), 0)
    choose = (lane8 == expert + EXPERTS * sub8).astype(f32).astype(bf16)
    slot_row = lax.broadcasted_iota(jnp.int32, (CAP, TOK), 0).astype(f32)
    gates = []
    for b in range(GROUP):
        meta = n_ref[b, :, D:]
        fields = matmul(choose, meta, (1, 1))
        hot = slot_row == fields[0:1]
        pick_rows = jnp.where(hot, 1.0, 0.0).astype(bf16)
        gate_row = fields[1:2] + fields[2:3]
        gates.append(jnp.sum(jnp.where(hot, gate_row, 0.0), axis=1, keepdims=True))
        span = pl.ds(b * CAP, CAP)
        xs[span, :] = matmul(pick_rows, n_ref[b, :, :D], (1, 0)).astype(bf16)
        ds[span, :] = matmul(pick_rows, g_ref[b], (1, 0)).astype(bf16)
    gate = jnp.concatenate(gates, axis=0)
    w_gu = w_ref[:, : D // 4, :].reshape(D, 2 * FF_E)
    w_d = w_ref[:, D // 4 :, :].reshape(FF_E, D)
    x = xs[...]
    gu = matmul(x, w_gu, (1, 0))
    g_part, u_part = gu[:, :FF_E], gu[:, FF_E:]
    sig = 1.0 / (1.0 + jnp.exp(-g_part))
    act = g_part * sig
    hid = (act * u_part).astype(bf16)
    y = matmul(hid, w_d, (1, 0)).astype(bf16).astype(f32)
    dout = ds[...].astype(f32)
    dgate = jnp.sum(y * dout, axis=1, keepdims=True)
    gys[...] = (gate * y).astype(bf16)
    dy = (gate * dout).astype(bf16)
    dh = matmul(dy, w_d, (1, 1))
    da_g = dh * u_part * (sig * (1.0 + g_part * (1.0 - sig)))
    da = jnp.concatenate([da_g, dh * act], axis=1).astype(bf16)
    acc_d[...] += matmul(hid, dy, (0, 0))
    acc_gu[...] += matmul(x, da, (0, 0))
    dzs[:, :D] = matmul(da, w_gu, (1, 1)).astype(bf16)
    lane = lax.broadcasted_iota(jnp.int32, (GROUP * CAP, 128), 1)
    high = dgate.astype(bf16).astype(f32)
    fields = jnp.where(lane == expert, high, jnp.where(lane == expert + EXPERTS, dgate - high, 0.0))
    dzs[:, D:] = fields.astype(bf16)
    slot_lane = lax.broadcasted_iota(jnp.int32, (TOK, CAP), 1).astype(f32)
    lane_t = lax.broadcasted_iota(jnp.int32, (TOK, 128), 1)
    for b in range(GROUP):
        meta = n_ref[b, :, D:].astype(f32)
        rank = jnp.sum(jnp.where(lane_t == expert, meta, 0.0), axis=1, keepdims=True)
        spread = jnp.where(slot_lane == rank, 1.0, 0.0).astype(bf16)
        span = pl.ds(b * CAP, CAP)
        dn_ref[b] = matmul(spread, dzs[span, :], (1, 0)).astype(bf16)
        out_ref[b] = matmul(spread, gys[span, :], (1, 0)).astype(bf16)

    @pl.when(step == pl.num_programs(0) - 1)
    def _():
        dw_ref[:, : D // 4, :] = acc_gu[...].astype(bf16).reshape(4, D // 4, 2 * FF_E)
        dw_ref[:, D // 4 :, :] = acc_d[...].astype(bf16).reshape(4, FF_E // 4, D)


def experts(n_all, g_all, weights):
    sources = n_all.shape[0]
    wide = n_all.shape[2]
    rows = GROUP * CAP

    def block(width):
        return pl.BlockSpec((GROUP, TOK, width), lambda i: (i, 0, 0))

    def fixed(shape):
        return pl.BlockSpec(shape, lambda i: (0, 0, 0), pipeline_mode=pl.Buffered(1))

    return pl.pallas_call(
        expert_kernel,
        grid=(sources // GROUP,),
        out_shape=[
            jax.ShapeDtypeStruct(n_all.shape, bf16),
            jax.ShapeDtypeStruct(g_all.shape, bf16),
            jax.ShapeDtypeStruct(weights.shape, bf16),
        ],
        in_specs=[block(wide), block(D), fixed(weights.shape)],
        out_specs=[block(wide), block(D), fixed(weights.shape)],
        scratch_shapes=[
            pltpu.VMEM((rows, D), bf16),
            pltpu.VMEM((rows, D), bf16),
            pltpu.VMEM((rows, wide), bf16),
            pltpu.VMEM((rows, D), bf16),
            pltpu.VMEM((D, 2 * FF_E), f32),
            pltpu.VMEM((FF_E, D), f32),
        ],
        compiler_params=pltpu.CompilerParams(
            dimension_semantics=("arbitrary",), vmem_limit_bytes=58 * 1024 * 1024
        ),
        cost_estimate=pl.CostEstimate(
            flops=sources * CAP * D * FF_E * 18, bytes_accessed=75_000_000, transcendentals=0
        ),
        name="experts",
    )(n_all, g_all, weights)


def turned_rows(u, cos, sin, back):
    lane = lax.broadcasted_iota(jnp.int32, (1, 128), 1)
    first = lax.rem(lane, HEAD_DIM) < HEAD_DIM // 2
    pieces = []
    for j in range(u.shape[1] // 128):
        v = u[:, j * 128 : (j + 1) * 128]
        w = v * sin if back else v
        ahead = pltpu.roll(w, 128 - HEAD_DIM // 2, 1)
        behind = pltpu.roll(w, HEAD_DIM // 2, 1)
        if back:
            pieces.append(v * cos + jnp.where(first, ahead, -behind))
        else:
            pieces.append(v * cos + jnp.where(first, -ahead, behind) * sin)
    return jnp.concatenate(pieces, axis=1)


def unpack_into(out, packed):
    def chunk(i, carry):
        x = packed[pl.ds(i * 16, 16), :, :512].astype(f32)
        rows = pl.ds(pl.multiple_of(i * 128, 128), 128)
        out[rows, :512] = x[:, :8].reshape(128, 512).astype(bf16)
        out[rows, 512:] = x[:, 8:].reshape(128, 512).astype(bf16)
        return carry

    lax.fori_loop(0, 8, chunk, 0)


def gain_rows(small):
    lane = lax.broadcasted_iota(jnp.int32, (8, 128), 1)
    sub = lax.broadcasted_iota(jnp.int32, (8, 128), 0)
    choose = (lane == EXPERTS + sub).astype(f32).astype(bf16)
    return matmul(choose, small, (1, 1))


def fill_bias(bias, length, first_row):
    rows = lax.broadcasted_iota(jnp.int32, bias.shape, 0) + first_row
    keys = lax.broadcasted_iota(jnp.int32, bias.shape, 1)
    bias[...] = jnp.where((keys <= rows) & (keys < length), 0.0, masked_score)


def front_kernel(
    length, wq_p, wkv_p, wo_p, tok, routes, cos, sin,
    n_out, n1_out, q_out, kv_out, lse_out, ho_out, r_out, gate_out, wq, wkv, wo, small_out,
    bias,
):
    z = lax.axis_index("seq")
    unpack_into(wkv, wkv_p)
    unpack_into(wq, wq_p)

    def small_chunk(i, carry):
        x = wo_p[pl.ds(i * 16, 16), :, 512:].astype(f32)
        rows = pl.ds(pl.multiple_of(i * 128, 128), 128)
        small_out[rows, :] = x[:, :8].reshape(128, 128).astype(bf16)
        return carry

    lax.fori_loop(0, 8, small_chunk, 0)
    unpack_into(wo, wo_p)
    gains = gain_rows(small_out[...])
    fill_bias(bias, length[0], z * TOK)
    width = KV_HEADS * HEAD_DIM

    def block(b, carry):
        x = tok[b].astype(f32)
        n1 = (x * rms_scale(x) * gains[0:1]).astype(bf16)
        rows = pl.ds(pl.multiple_of(b * TOK, TOK), TOK)
        n1_out[rows, :] = n1
        kv = matmul(n1, wkv[...], (1, 0))
        kv_out[rows, :width] = turned_rows(
            kv[:, :width], cos[rows, :], sin[rows, :], False
        ).astype(bf16)
        kv_out[rows, width:] = kv[:, width:].astype(bf16)
        return carry

    lax.fori_loop(0, 4, block, 0)
    own = pl.ds(pl.multiple_of(z * TOK, TOK), TOK)
    q = matmul(n1_out[own, :], wq[...], (1, 0))
    q = turned_rows(q, cos[own, :], sin[own, :], False).astype(bf16)
    q_out[...] = q * jnp.asarray(HEAD_DIM ** (-0.5), bf16)
    lse_out[...] = jnp.zeros_like(lse_out)
    lane = lax.broadcasted_iota(jnp.int32, (TOK, 128), 1)

    def heads(j, carry):
        keys = kv_out[:, pl.ds(pl.multiple_of(j * 128, 128), 128)]
        values = kv_out[:, pl.ds(pl.multiple_of(width + j * 128, 128), 128)]
        for g in (0, 1):
            span = pl.ds(pl.multiple_of(j * 256 + g * 128, 128), 128)
            qs = q_out[:, span]
            key = keys[:, g * HEAD_DIM : (g + 1) * HEAD_DIM]
            value = values[:, g * HEAD_DIM : (g + 1) * HEAD_DIM]
            mixed = []
            for h in (0, 1):
                s = matmul(qs[:, h * HEAD_DIM : (h + 1) * HEAD_DIM], key, (1, 1)) + bias[...]
                top = jnp.max(s, axis=1, keepdims=True)
                p = jnp.exp(s - top)
                total = jnp.sum(p, axis=1, keepdims=True)
                p = (p * (1.0 / total)).astype(bf16)
                mixed.append(matmul(p, value, (1, 0)))
                head = j * 4 + g * 2 + h
                lse_out[...] = jnp.where(lane == head, top + jnp.log(total), lse_out[...])
            ho_out[:, span] = jnp.concatenate(mixed, axis=1).astype(bf16)
        return carry

    lax.fori_loop(0, 4, heads, 0)
    r = tok[z].astype(f32) + matmul(ho_out[...], wo[...], (1, 0))
    r_out[...] = r
    n2 = (r * rms_scale(r) * gains[1:2]).astype(bf16)
    n_out[:, :D] = n2
    logits = matmul(n2, small_out[...], (1, 0))
    hits = lane == routes[:, 0:1]
    for k in range(1, routes.shape[1]):
        hits = hits | (lane == routes[:, k : k + 1])
    lifted = jnp.where(hits, logits, masked_score)
    lifted = jnp.where(hits, jnp.exp(lifted - jnp.max(lifted, axis=1, keepdims=True)), 0.0)
    gate = lifted / jnp.sum(lifted, axis=1, keepdims=True)
    gate_out[...] = gate
    row = lax.broadcasted_iota(jnp.int32, (TOK, TOK), 0)
    col = lax.broadcasted_iota(jnp.int32, (TOK, TOK), 1)
    earlier = jnp.where(col < row, 1.0, 0.0).astype(bf16)
    ranks = matmul(earlier, jnp.where(hits, 1.0, 0.0).astype(bf16), (1, 0))
    high = gate.astype(bf16).astype(f32)
    meta = jnp.where(hits, ranks, jnp.where(lane < EXPERTS, -1.0, 0.0))
    meta = meta + pltpu.roll(high, EXPERTS, 1) + pltpu.roll(gate - high, 2 * EXPERTS, 1)
    n_out[:, D:] = meta.astype(bf16)


def front(length, w_q, w_kv, w_o, tok, routes, cos, sin):
    vmem = pl.BlockSpec(memory_space=pltpu.VMEM)
    square = jax.ShapeDtypeStruct((D, D), bf16)
    rows = jax.ShapeDtypeStruct((TOK, D), bf16)
    lanes = jax.ShapeDtypeStruct((TOK, 128), f32)
    return pl.pallas_call(
        front_kernel,
        out_shape=[
            jax.ShapeDtypeStruct((TOK, D + 128), bf16),
            square,
            rows,
            square,
            lanes,
            rows,
            jax.ShapeDtypeStruct((TOK, D), f32),
            lanes,
            square,
            square,
            square,
            jax.ShapeDtypeStruct((D, 128), bf16),
        ],
        in_specs=[pl.BlockSpec(memory_space=pltpu.SMEM)] + [vmem] * 7,
        out_specs=[vmem] * 12,
        scratch_shapes=[pltpu.VMEM((TOK, 4 * TOK), f32)],
        compiler_params=pltpu.CompilerParams(vmem_limit_bytes=56 * 1024 * 1024),
        cost_estimate=pl.CostEstimate(
            flops=10**10, bytes_accessed=30_000_000, transcendentals=5_000_000
        ),
        name="front",
    )(length, w_q, w_kv, w_o, tok, routes, cos, sin)


def rms_back(values, scale, gain, dnormed):
    scaled = values * scale
    dscaled = dnormed * gain
    dvalues = scale * (dscaled - scaled * jnp.mean(dscaled * scaled, axis=-1, keepdims=True))
    return dvalues, jnp.sum(dnormed * scaled, axis=0, keepdims=True)


def pack_into(out, value):
    def chunk(i, carry):
        rows = pl.ds(pl.multiple_of(i * 128, 128), 128)
        left = value[rows, :512].reshape(16, 8, 512)
        right = value[rows, 512:].reshape(16, 8, 512)
        out[pl.ds(i * 16, 16), :, :512] = jnp.concatenate([left, right], axis=1).astype(bf16)
        return carry

    lax.fori_loop(0, 8, chunk, 0)


def back_kernel(
    length, sums, dout, n_ext, r_ref, gate_ref, ho, q_ref, kv, lse, n1, tok, wq, wkv, wo, small,
    cos, sin, cos_t, sin_t,
    dwq_p, dwkv_p, dwo_p, dn1_out, dr_out,
    bias, square, dkv_t, dq_s, do_s, dkv_s,
):
    z = lax.axis_index("seq")
    own = pl.ds(pl.multiple_of(z * TOK, TOK), TOK)
    gains = gain_rows(small[...])
    lane = lax.broadcasted_iota(jnp.int32, (TOK, 128), 1)
    gate = gate_ref[...]
    fields = sums[:, D:]
    dgate = fields + pltpu.roll(fields, 128 - EXPERTS, 1)
    mean = jnp.sum(gate * dgate, axis=1, keepdims=True)
    dlogits = (gate * (dgate - mean)).astype(bf16)
    dn2 = sums[:, :D] + matmul(dlogits, small[...], (1, 1))
    d_router = matmul(n_ext[:, :D], dlogits, (0, 0))
    r = r_ref[...]
    dr, dg2 = rms_back(r, rms_scale(r), gains[1:2], dn2)
    dr = dr + dout[...].astype(f32)
    dr_out[...] = dr
    d_att = dr.astype(bf16)
    square[...] = matmul(ho[...], d_att, (0, 0))
    pack_into(dwo_p, square)
    do_s[...] = matmul(d_att, wo[...], (1, 1)).astype(bf16)
    fill_bias(bias, length[0], z * TOK)
    width = KV_HEADS * HEAD_DIM
    scale = HEAD_DIM ** (-0.5)

    def heads(j, carry):
        keys = kv[:, pl.ds(pl.multiple_of(j * 128, 128), 128)]
        values = kv[:, pl.ds(pl.multiple_of(width + j * 128, 128), 128)]
        for g in (0, 1):
            span = pl.ds(pl.multiple_of(j * 256 + g * 128, 128), 128)
            qs, dos = q_ref[:, span], do_s[:, span]
            prods = dos.astype(f32) * ho[:, span].astype(f32)
            key = keys[:, g * HEAD_DIM : (g + 1) * HEAD_DIM]
            value = values[:, g * HEAD_DIM : (g + 1) * HEAD_DIM]
            dqs = []
            dk_t, dv_t = 0.0, 0.0
            for h in (0, 1):
                part = slice(h * HEAD_DIM, (h + 1) * HEAD_DIM)
                head = j * 4 + g * 2 + h
                shift_by = jnp.sum(jnp.where(lane == head, lse[...], 0.0), axis=1, keepdims=True)
                mine = (lane >= h * HEAD_DIM) & (lane < (h + 1) * HEAD_DIM)
                delta = jnp.sum(jnp.where(mine, prods, 0.0), axis=1, keepdims=True)
                p = jnp.exp(matmul(qs[:, part], key, (1, 1)) + bias[...] - shift_by)
                dp = matmul(dos[:, part], value, (1, 1))
                ds = (p * (dp - delta)).astype(bf16)
                dqs.append(matmul(ds, key, (1, 0)) * scale)
                dk_t = dk_t + matmul(qs[:, part], ds, (0, 0))
                dv_t = dv_t + matmul(dos[:, part], p.astype(bf16), (0, 0))
            dq_s[:, span] = jnp.concatenate(dqs, axis=1)
            half = HEAD_DIM // 2
            wave = dk_t * sin_t[...]
            dk_t = dk_t * cos_t[...] + jnp.concatenate([wave[half:], -wave[:half]], axis=0)
            at = j * 128 + g * HEAD_DIM
            dkv_t[pl.ds(pl.multiple_of(at, HEAD_DIM), HEAD_DIM), :] = dk_t
            dkv_t[pl.ds(pl.multiple_of(width + at, HEAD_DIM), HEAD_DIM), :] = dv_t
        return carry

    lax.fori_loop(0, 4, heads, 0)

    def flip(i, carry):
        at = pl.ds(pl.multiple_of(i * 128, 128), 128)
        dkv_s[:, at] = jnp.transpose(dkv_t[at, :]).astype(bf16)
        return carry

    lax.fori_loop(0, 8, flip, 0)
    dq = turned_rows(dq_s[...], cos[own, :], sin[own, :], True).astype(bf16)
    square[...] = matmul(n1[own, :], dq, (0, 0))
    pack_into(dwq_p, square)
    square[...] = matmul(n1[...], dkv_s[...], (0, 0))
    pack_into(dwkv_p, square)
    square[...] = matmul(dkv_s[...], wkv[...], (1, 1))
    square[own, :] += matmul(dq, wq[...], (1, 1))
    dg1 = jnp.zeros((1, D), f32)
    for b in range(4):
        rows = slice(b * TOK, (b + 1) * TOK)
        x = tok[b].astype(f32)
        dn1 = square[rows, :]
        dg1 = dg1 + jnp.sum(dn1 * (x * rms_scale(x)), axis=0, keepdims=True)
        dn1_out[b] = dn1.astype(bf16)
    sub = lax.broadcasted_iota(jnp.int32, (8, D), 0)
    dgs = jnp.where(sub == 0, dg1, jnp.where(sub == 1, dg2, 0.0))
    high = dgs.astype(bf16)
    low = (dgs - high.astype(f32)).astype(bf16)
    place_lane = lax.broadcasted_iota(jnp.int32, (8, 128), 1)
    place_sub = lax.broadcasted_iota(jnp.int32, (8, 128), 0)
    spread = (place_lane == EXPERTS + place_sub).astype(f32).astype(bf16)
    d_small = d_router + matmul(high, spread, (0, 0)) + matmul(low, spread, (0, 0))
    d_small = d_small.reshape(128, 8, 128)
    dwo_p[:, :, 512:] = jnp.concatenate([d_small, jnp.zeros_like(d_small)], axis=1).astype(bf16)


def back(*args):
    vmem = pl.BlockSpec(memory_space=pltpu.VMEM)
    return pl.pallas_call(
        back_kernel,
        out_shape=[
            jax.ShapeDtypeStruct((128, 16, 512), bf16),
            jax.ShapeDtypeStruct((128, 16, 512), bf16),
            jax.ShapeDtypeStruct((128, 16, 640), bf16),
            jax.ShapeDtypeStruct((4, TOK, D), bf16),
            jax.ShapeDtypeStruct((TOK, D), f32),
        ],
        in_specs=[pl.BlockSpec(memory_space=pltpu.SMEM)] + [vmem] * 19,
        out_specs=[vmem] * 5,
        scratch_shapes=[
            pltpu.VMEM((TOK, 4 * TOK), f32),
            pltpu.VMEM((D, D), f32),
            pltpu.VMEM((D, D), f32),
            pltpu.VMEM((TOK, D), f32),
            pltpu.VMEM((TOK, D), bf16),
            pltpu.VMEM((D, D), bf16),
        ],
        compiler_params=pltpu.CompilerParams(vmem_limit_bytes=60 * 1024 * 1024),
        cost_estimate=pl.CostEstimate(
            flops=2 * 10**10, bytes_accessed=40_000_000, transcendentals=5_000_000
        ),
        name="back",
    )(*args)


def pack_matrix(shard):
    half = shard.shape[1] // 2
    return jnp.concatenate([shard[:, :half], shard[:, half:]], axis=0)


def unpack_matrix(packed):
    return jnp.concatenate([packed[:8], packed[8:]], axis=1)


def body(
    tokens, routes, lengths, out_grad,
    query_weight, query_mean, query_square,
    keyval_weight, keyval_mean, keyval_square,
    output_weight, output_mean, output_square,
    router_weight, router_mean, router_square,
    norm_gains, gains_mean, gains_square,
    gateup_weight, gateup_mean, gateup_square,
    down_weight, down_mean, down_square,
):
    row_count = tokens.shape[0]
    seq_len = row_count * 4
    query_width = HEADS * HEAD_DIM

    small = jnp.concatenate(
        [router_weight, norm_gains.T, jnp.zeros((8, 128 - EXPERTS - 2), f32)], axis=1
    )
    small = jnp.concatenate([small, jnp.zeros((8, 128), f32)], axis=0)
    w_q, w_kv, w_o, all_tokens = gather_front(
        pack_matrix(query_weight).astype(bf16),
        pack_matrix(keyval_weight).astype(bf16),
        jnp.concatenate([pack_matrix(output_weight), small], axis=1).astype(bf16),
        tokens,
    )
    expert_b = lax.all_gather(
        jnp.concatenate([gateup_weight[0], down_weight[0]], axis=0).astype(bf16), "seq", axis=0
    )
    dout_all = lax.all_gather(out_grad, "dp", axis=0)

    cos, sin = rotary_tables(jnp.arange(seq_len, dtype=jnp.int32), HEAD_DIM // 2)
    cos2, sin2 = jnp.tile(cos, (1, 2)), jnp.tile(sin, (1, 2))
    n_ext, n1, q, kv, lse, ho, residual, gate, query_b, keyval_b, output_b, small_b = front(
        lengths,
        w_q.reshape(128, 16, 512),
        w_kv.reshape(128, 16, 512),
        w_o.reshape(128, 16, 640),
        all_tokens,
        routes,
        cos2,
        sin2,
    )
    n_all = gather_plane(n_ext, 2)
    wide = n_all.shape[-1]
    dn_parts, out_parts, d_expert = experts(
        n_all.reshape(EXPERTS, row_count, wide), dout_all, expert_b
    )
    grad_expert = lax.psum_scatter(d_expert, "seq", scatter_dimension=0, tiled=False).astype(f32)
    sums = sum_plane(dn_parts.reshape(4, 4, 2, row_count, wide), 3, f32)
    mixed_out = sum_plane(out_parts.reshape(4, 4, 2, row_count, D), 5, f32)
    layer_out = (residual + mixed_out).astype(bf16)
    d_query, d_keyval, d_last, dn1, dresidual = back(
        lengths, sums, out_grad, n_ext, residual, gate, ho, q, kv, lse, n1, all_tokens,
        query_b, keyval_b, output_b, small_b, cos2, sin2, cos.T, sin.T,
    )
    g_query, g_keyval, g_last, dn1_sum = sum_back(
        (
            d_query.reshape(4, 4, 2, 4, 16, 512),
            d_keyval.reshape(4, 4, 2, 4, 16, 512),
            d_last.reshape(4, 4, 2, 4, 16, 640),
        ),
        dn1,
    )
    grad_query, grad_keyval, grad_output = (
        unpack_matrix(g) for g in (g_query, g_keyval, g_last[:, :512])
    )
    grad_router = g_last[:8, 512 : 512 + EXPERTS]
    grad_gains = g_last[:8, 512 + EXPERTS : 512 + EXPERTS + 2].T
    inputs = tokens.astype(f32)
    gain_one = small_b[:, EXPERTS].astype(f32)
    dnorm_one, _ = norm_back(inputs, rms_scale(inputs), gain_one, dn1_sum)
    tokens_grad = dresidual + dnorm_one

    rate = 0.5
    query_new = adamw(query_weight, grad_query, query_mean, query_square, rate * D ** (-0.5), 0.1)
    keyval_new = adamw(
        keyval_weight, grad_keyval, keyval_mean, keyval_square, rate * D ** (-0.5), 0.1
    )
    output_new = adamw(
        output_weight,
        grad_output,
        output_mean,
        output_square,
        rate * max(1, 2 * query_width // seq_len) ** (-0.5),
        0.1,
    )
    router_new = adamw(
        router_weight, grad_router, router_mean, router_square, rate * (4 * D) ** (-0.5), 0.1
    )
    gains_new = adamw(norm_gains, grad_gains, gains_mean, gains_square, 0.6, 0.0)
    gateup_new = adamw(
        gateup_weight,
        grad_expert[None, : D // 4],
        gateup_mean,
        gateup_square,
        rate * D ** (-0.5),
        0.1,
    )
    down_new = adamw(
        down_weight,
        grad_expert[None, D // 4 :],
        down_mean,
        down_square,
        rate * (FF_E // 8) ** (-0.5),
        0.1,
    )
    return (
        (layer_out, tokens_grad)
        + query_new
        + keyval_new
        + output_new
        + router_new
        + gains_new
        + gateup_new
        + down_new
    )


def solution(mesh):
    rows = P(("dp", "seq"), None)
    gains = P(None, ("dp", "seq"))
    shard = P("dp", "seq", None)
    return jax.shard_map(
        body,
        mesh=mesh,
        in_specs=(rows, rows, P("dp"), rows) + (rows,) * 12 + (gains,) * 3 + (shard,) * 6,
        out_specs=(rows, rows) + (rows,) * 12 + (gains,) * 3 + (shard,) * 6,
        check_vma=False,
    )
```

```python
import jax
import jax.numpy as jnp
from jax import lax
from jax.experimental import pallas as pl
from jax.experimental.pallas import tpu as pltpu
from jax.sharding import PartitionSpec as P

MESH = pl.DeviceIdType.MESH
bf16 = jnp.bfloat16
f32 = jnp.float32
AXES = "xycz"
STRIP = 16


def place():
    return {a: lax.axis_index(a) for a in AXES}


def device(at):
    return tuple(at[a] for a in AXES)


def shift(at, axis, by):
    size = 2 if axis == "c" else 4
    return lax.rem(at[axis] + by, size)


def peer(at, axis, by):
    return device({**at, axis: shift(at, axis, by)})


def greet(at, axes):
    barrier = pltpu.get_barrier_semaphore()
    count = 0
    for axis in axes:
        for by in (1,) if axis == "c" else (1, 2, 3):
            pl.semaphore_signal(
                barrier, inc=1, device_id=peer(at, axis, by), device_id_type=MESH
            )
            count += 1
    pl.semaphore_wait(barrier, count)


class Wires:
    def __init__(self, send_sems, recv_sems, local_sems):
        self.send_sems, self.recv_sems, self.local_sems = send_sems, recv_sems, local_sems
        self.copies, self.local = [], 0

    def send(self, src, dst, target):
        at = len(self.copies)
        copy = pltpu.make_async_remote_copy(
            src_ref=src,
            dst_ref=dst,
            send_sem=self.send_sems.at[at],
            recv_sem=self.recv_sems.at[at],
            device_id=target,
            device_id_type=MESH,
        )
        copy.start()
        self.copies.append(copy)
        return copy

    def keep(self, src, dst):
        copy = pltpu.make_async_copy(src, dst, self.local_sems.at[self.local])
        copy.start()
        self.local += 1
        return copy

    def finish(self):
        for copy in self.copies:
            copy.wait_send()


def wire_sems(copies, kept):
    return [
        pltpu.SemaphoreType.DMA((copies,)),
        pltpu.SemaphoreType.DMA((copies,)),
        pltpu.SemaphoreType.DMA((kept,)),
    ]


def in_order(order, **steps):
    for letter in order:
        next(steps[letter], None)
    for step in steps.values():
        for _ in step:
            pass


def hbm(*arrays):
    return [pltpu.with_memory_space_constraint(v, pltpu.HBM) for v in arrays]


def ring_steps(wires, at, axis, spot, hand_on):
    right, left = peer(at, axis, 1), peer(at, axis, 3)
    to_right = {k: wires.send(spot(0, k), spot(0, k), right) for k in (0, 1)}
    to_left = {k: wires.send(spot(0, k), spot(0, k), left) for k in (1, 0)}
    for k in (0, 1):
        hand_on(0, k)
    yield
    to_right[0].wait_recv()
    far_right = wires.send(spot(3, 0), spot(3, 0), right)
    hand_on(3, 0)
    to_left[1].wait_recv()
    far_left = wires.send(spot(1, 1), spot(1, 1), left)
    hand_on(1, 1)
    yield
    to_right[1].wait_recv()
    hand_on(3, 1)
    to_left[0].wait_recv()
    hand_on(1, 0)
    yield
    far_right.wait_recv()
    hand_on(2, 0)
    far_left.wait_recv()
    hand_on(2, 1)


def row_steps(wires, at, src, out):
    half = src.shape[0] // 2
    own = out.at[at["x"], at["c"]]
    kept = wires.keep(src, own)
    sibling = peer(at, "c", 1)
    across = []

    def spot(by, part):
        return out.at[shift(at, "x", by), at["c"], pl.ds(part * half, half)]

    def hand_on(by, part):
        across.append(wires.send(spot(by, part), spot(by, part), sibling))

    kept.wait()
    yield from ring_steps(wires, at, "x", spot, hand_on)
    yield
    for copy in across:
        copy.wait_recv()


ROW_COPIES = 6 + 8


def token_steps(wires, at, src, out):
    half = src.shape[0] // 2
    kept = wires.keep(src, out.at[at["z"]])

    def spot(by, part):
        return out.at[shift(at, "z", by), pl.ds(part * half, half)]

    kept.wait()
    yield from ring_steps(wires, at, "z", spot, lambda by, part: None)


TOKEN_COPIES = 6


def index(at, whole, **fixed):
    spots = {**at, **{a: slice(None) for a in whole}, **fixed}
    return tuple(spots[axis] for axis in AXES)


def weight_steps(wires, at, parts):
    kept = [wires.keep(w, o.at[index(at, "")]) for w, o, _ in parts]
    arrivals = {}
    for p, (w, o, order) in enumerate(parts):
        for by in (1, 3, 2):
            arrivals[p, by] = wires.send(w, o.at[index(at, "")], peer(at, order[0], by))
    yield
    for copy in kept:
        copy.wait()
    later = {}
    for p, (w, o, order) in enumerate(parts):
        for by in (1, 3, 2):
            arrivals[p, by].wait_recv()
        spot = index(at, order[0])
        for by in (1, 3, 2):
            later[p, by] = wires.send(o.at[spot], o.at[spot], peer(at, order[1], by))
    yield
    sibling = peer(at, "c", 1)
    across, rings = [], []
    for p, (w, o, order) in enumerate(parts):
        for by in (1, 3, 2):
            later[p, by].wait_recv()

        def spot(by, part, o=o, order=order):
            pieces = {order[1]: pl.ds(2 * part, 2), order[2]: shift(at, order[2], by)}
            return o.at[index(at, order[0], **pieces)]

        def hand_on(by, part, spot=spot):
            across.append(wires.send(spot(by, part), spot(by, part), sibling))

        ring = ring_steps(wires, at, order[2], spot, hand_on)
        next(ring)
        rings.append(ring)
    yield
    for _ in range(3):
        for ring in rings:
            next(ring, None)
        yield
    for copy in across:
        copy.wait_recv()


WEIGHT_COPIES = 3 * (3 + 3 + 6 + 8)


GATHER_ORDERS = ("zyx", "zxy", "zyx")
GATHER_SCHEDULE = "wtdwwdtwdwtd"


def gather_front_kernel(wq, wkv, wo, tok, dout, oq, okv, oo, ot, od, *sems):
    at = place()
    wires = Wires(*sems)
    greet(at, "xyzc")
    in_order(
        GATHER_SCHEDULE,
        w=weight_steps(wires, at, list(zip((wq, wkv, wo), (oq, okv, oo), GATHER_ORDERS))),
        t=token_steps(wires, at, tok, ot),
        d=row_steps(wires, at, dout, od),
    )
    wires.finish()


def gather_front(wq, wkv, wo, tok, dout):
    shapes = [pltpu.HBM((4, 4, 2, 4) + w.shape, w.dtype) for w in (wq, wkv, wo)]
    shapes.append(pltpu.HBM((4,) + tok.shape, tok.dtype))
    shapes.append(pltpu.HBM((4, 2) + dout.shape, dout.dtype))
    far = pl.BlockSpec(memory_space=pltpu.HBM)
    return pl.pallas_call(
        gather_front_kernel,
        out_shape=shapes,
        in_specs=[far] * 5,
        out_specs=[far] * 5,
        scratch_shapes=wire_sems(WEIGHT_COPIES + TOKEN_COPIES + ROW_COPIES, 5),
        compiler_params=pltpu.CompilerParams(collective_id=1, has_side_effects=True),
        name="gather_front",
    )(*hbm(wq, wkv, wo, tok, dout))


def gather_rows_kernel(n, o, *sems):
    at = place()
    wires = Wires(*sems)
    greet(at, "xc")
    in_order("", d=row_steps(wires, at, n, o))
    wires.finish()


def gather_rows(n):
    far = pl.BlockSpec(memory_space=pltpu.HBM)
    return pl.pallas_call(
        gather_rows_kernel,
        out_shape=pltpu.HBM((4, 2) + n.shape, n.dtype),
        in_specs=[far],
        out_specs=far,
        scratch_shapes=wire_sems(ROW_COPIES, 1),
        compiler_params=pltpu.CompilerParams(collective_id=2, has_side_effects=True),
        name="gather_rows",
    )(*hbm(n))


def add_rows(out, parts, rows):
    def strip(i, carry):
        span = pl.ds(pl.multiple_of(i * STRIP, STRIP), STRIP)
        total = parts[0][span].astype(f32)
        for part in parts[1:]:
            total = total + part[span].astype(f32)
        out[span] = total.astype(out.dtype)
        return carry

    lax.fori_loop(0, rows // STRIP, strip, 0)


def ring_sum_steps(wires, at, axis, blocks, out, mid, last, near):
    half = out.shape[0] // 2
    low, high = pl.ds(0, half), pl.ds(half, half)
    ahead, back, far = (blocks.at[shift(at, axis, by)] for by in (1, 3, 2))
    right, left = peer(at, axis, 1), peer(at, axis, 3)
    near_l = wires.send(far.at[low], near.at[0], right)
    near_r = wires.send(far.at[high], near.at[1], left)
    pure_l = wires.send(ahead.at[high], last.at[0, high], right)
    pure_r = wires.send(back.at[low], last.at[1, low], left)
    yield
    near_l.wait_recv()
    add_rows(mid.at[0], [ahead.at[low], near.at[0]], half)
    sum_l = wires.send(mid.at[0], last.at[0, low], right)
    near_r.wait_recv()
    add_rows(mid.at[1], [back.at[high], near.at[1]], half)
    sum_r = wires.send(mid.at[1], last.at[1, high], left)
    yield
    for copy in (pure_l, sum_l, pure_r, sum_r):
        copy.wait_recv()
    add_rows(out, [blocks.at[at[axis]], last.at[0], last.at[1]], 2 * half)


def ring_sum_scratch(rows, width):
    return [
        pltpu.VMEM((2, rows // 2, width), bf16),
        pltpu.VMEM((2, rows, width), bf16),
        pltpu.VMEM((2, rows // 2, width), bf16),
    ]


def row_sum_steps(wires, at, c_ref, out, held, crossed, mid, last, near):
    other = shift(at, "c", 1)
    sibling = peer(at, "c", 1)
    rows = out.shape[0]
    crossing, kept = {}, {}
    for by in (2, 1, 3, 0):
        i = shift(at, "x", by)
        crossing[by] = wires.send(c_ref.at[i, other], crossed.at[i], sibling)
        kept[by] = wires.keep(c_ref.at[i, at["c"]], held.at[i])
    yield
    for by in (2, 1, 3, 0):
        i = shift(at, "x", by)
        kept[by].wait()
        crossing[by].wait_recv()
        add_rows(held.at[i], [held.at[i], crossed.at[i]], rows)
        if by == 3:
            ring = ring_sum_steps(wires, at, "x", held, out, mid, last, near)
            next(ring)
    yield
    yield from ring


ROW_SUM_COPIES = 4 + 6


def row_sum_scratch(rows, width):
    return [pltpu.VMEM((4, rows, width), bf16)] * 2 + ring_sum_scratch(rows, width)


def sum_rows_kernel(c_ref, out, *refs):
    at = place()
    wires = Wires(*refs[-3:])
    greet(at, "xc")
    in_order("", p=row_sum_steps(wires, at, c_ref, out, *refs[:5]))
    wires.finish()


def sum_rows(c):
    rows, width = c.shape[-2:]
    return pl.pallas_call(
        sum_rows_kernel,
        out_shape=jax.ShapeDtypeStruct((rows, width), f32),
        in_specs=[pl.BlockSpec(memory_space=pltpu.HBM)],
        out_specs=pl.BlockSpec(memory_space=pltpu.VMEM),
        scratch_shapes=row_sum_scratch(rows, width) + wire_sems(ROW_SUM_COPIES, 4),
        compiler_params=pltpu.CompilerParams(
            collective_id=3, has_side_effects=True, vmem_limit_bytes=56 * 1024 * 1024
        ),
        name="sum_rows",
    )(*hbm(c))


SUM_ORDERS = ("yxz", "xyz", "zxy")
SUM_SCHEDULE = "mnpmmmpnpmmmmmm"


def pick(ref, axes, axis, mine):
    return ref.at[tuple(mine if a == axis else slice(None) for a in axes)]


def mat_steps(wires, at, mats, outs, crossed, held, one, two, three, sum1, sum2):
    sibling = peer(at, "c", 1)
    other = shift(at, "c", 1)
    crossing = [
        wires.send(mats[p].at[:, :, other], crossed[p], sibling) for p in range(3)
    ]

    def total(out, parts, count):
        def body(i, carry):
            value = parts[0][i].astype(f32)
            for part in parts[1:]:
                value = value + part[i].astype(f32)
            out[i] = value.astype(out.dtype)
            return carry

        lax.fori_loop(0, count, body, 0)

    stage1 = {}
    yield
    for p in range(3):
        crossing[p].wait_recv()

        def body(i, carry, p=p):
            mine = mats[p][i // 4, i % 4, at["c"]]
            held[p][i // 4, i % 4] = (
                mine.astype(f32) + crossed[p][i // 4, i % 4].astype(f32)
            ).astype(bf16)
            return carry

        lax.fori_loop(0, 16, body, 0)
        axis = SUM_ORDERS[p][0]
        for by in (2, 1, 3):
            stage1[p, by] = wires.send(
                pick(held[p], "xyz", axis, shift(at, axis, by)),
                one[p].at[by - 1],
                peer(at, axis, by),
            )
        yield
    stage2 = {}
    for p in range(3):
        axis, after = SUM_ORDERS[p][0], SUM_ORDERS[p][1]
        rest = "xyz".replace(axis, "")
        for by in (1, 3, 2):
            stage1[p, by].wait_recv()
        total(
            sum1[p],
            [pick(held[p], "xyz", axis, at[axis])] + [one[p].at[k] for k in range(3)],
            4,
        )
        for by in (2, 1, 3):
            stage2[p, by] = wires.send(
                pick(sum1[p], rest, after, shift(at, after, by)),
                two[p].at[by - 1],
                peer(at, after, by),
            )
        yield
    stage3 = {}
    for p in range(3):
        axis, after, end = SUM_ORDERS[p]
        rest = "xyz".replace(axis, "")
        for by in (1, 3, 2):
            stage2[p, by].wait_recv()
        total(
            sum2[p],
            [pick(sum1[p], rest, after, at[after])] + [two[p].at[k] for k in range(3)],
            4,
        )
        for by in (2, 1, 3):
            stage3[p, by] = wires.send(
                sum2[p].at[shift(at, end, by)], three[p].at[by - 1], peer(at, end, by)
            )
        yield
    for p in range(3):
        for by in (1, 3, 2):
            stage3[p, by].wait_recv()
        value = sum2[p][at[SUM_ORDERS[p][2]]].astype(f32)
        for k in range(3):
            value = value + three[p][k].astype(f32)
        outs[p][...] = value


def sum_back_kernel(*refs):
    mats, dn1, c_ref = refs[0:3], refs[3], refs[4]
    outs, dn1_out, mixed_out = refs[5:8], refs[8], refs[9]
    scratch = refs[10:-3]
    groups = [scratch[i * 3 : i * 3 + 3] for i in range(7)]
    at = place()
    wires = Wires(*refs[-3:])
    greet(at, "xyzc")
    in_order(
        SUM_SCHEDULE,
        p=row_sum_steps(wires, at, c_ref, mixed_out, *scratch[24:29]),
        m=mat_steps(wires, at, mats, outs, *groups),
        n=ring_sum_steps(wires, at, "z", dn1, dn1_out, *scratch[21:24]),
    )
    wires.finish()


def sum_back(mats, dn1, c):
    widths = [m.shape[-1] for m in mats]
    rows, model = dn1.shape[1:]
    scratch = []
    for lead in ((4, 4, 4), (4, 4, 4), (3, 4, 4), (3, 4), (3,), (4, 4), (4,)):
        scratch += [pltpu.VMEM(lead + (16, w), bf16) for w in widths]
    scratch += ring_sum_scratch(rows, model) + row_sum_scratch(rows, model)
    vmem = pl.BlockSpec(memory_space=pltpu.VMEM)
    return pl.pallas_call(
        sum_back_kernel,
        out_shape=[jax.ShapeDtypeStruct((16, w), f32) for w in widths]
        + [jax.ShapeDtypeStruct((rows, model), f32)] * 2,
        in_specs=[vmem] * 4 + [pl.BlockSpec(memory_space=pltpu.HBM)],
        out_specs=[vmem] * 5,
        scratch_shapes=scratch + wire_sems(3 * 10 + 6 + ROW_SUM_COPIES, 4),
        compiler_params=pltpu.CompilerParams(
            collective_id=4, has_side_effects=True, vmem_limit_bytes=60 * 1024 * 1024
        ),
        name="sum_back",
    )(*mats, dn1, *hbm(c))


D = 1024
HEADS = 16
KV_HEADS = 8
HEAD_DIM = 64
EXPERTS = 32
FF_E = 512
STEP = 10
CAP = 96
TOK = 256


norm_epsilon = 1e-06
beta_first = 0.9
beta_second = 0.95
adam_epsilon = 1e-08
masked_score = -1e30


def rotary_tables(positions, half_width):
    freqs = 10000.0 ** (-jnp.arange(half_width, dtype=jnp.float32) / half_width)
    angles = positions.astype(jnp.float32)[:, None] * freqs[None, :]
    cosines = jnp.cos(angles)
    sines = jnp.sin(angles)
    return (jnp.concatenate([cosines, cosines], 1), jnp.concatenate([sines, sines], 1))


def rotate(values, cosines, sines):
    half_width = values.shape[-1] // 2
    turned = jnp.concatenate([-values[..., half_width:], values[..., :half_width]], -1)
    return values * cosines[:, None, :] + turned * sines[:, None, :]


def rotate_back(grads, cosines, sines):
    half_width = grads.shape[-1] // 2
    scaled = grads * sines[:, None, :]
    return grads * cosines[:, None, :] + jnp.concatenate(
        [scaled[..., half_width:], -scaled[..., :half_width]], -1
    )


def rms_scale(values):
    return lax.rsqrt(jnp.mean(values * values, axis=-1, keepdims=True) + norm_epsilon)


def norm_back(values, scale, gain, dnormed):
    scaled = values * scale
    dgain = jnp.sum(dnormed * scaled, axis=0)
    dscaled = dnormed * gain
    dvalues = scale * (dscaled - scaled * jnp.mean(dscaled * scaled, axis=-1, keepdims=True))
    return (dvalues, dgain)


def masked_scores(grouped, whole_kv, positions, length):
    key_count = whole_kv.shape[0]
    key_width = whole_kv.shape[1] // 2
    heads_kv = grouped.shape[1]
    head_size = grouped.shape[3]
    all_keys = whole_kv[:, :key_width].reshape(key_count, heads_kv, head_size)
    all_values = whole_kv[:, key_width:].reshape(key_count, heads_kv, head_size)
    raw_scores = jnp.einsum(
        "qkgd,pkd->kgqp", grouped, all_keys, preferred_element_type=jnp.float32
    ) * head_size ** (-0.5)
    key_pos = jnp.arange(key_count, dtype=jnp.int32)
    allowed = (key_pos[None, :] <= positions[:, None]) & (key_pos[None, :] < length)
    return (jnp.where(allowed, raw_scores, masked_score), all_keys, all_values)


def adamw(weight, grad, first, second, rate, decay):
    first_new = beta_first * first + (1.0 - beta_first) * grad
    second_new = beta_second * second + (1.0 - beta_second) * grad * grad
    update = (
        first_new
        / (1.0 - beta_first**STEP)
        / (jnp.sqrt(second_new / (1.0 - beta_second**STEP)) + adam_epsilon)
    )
    return (weight - rate * (update + decay * weight), first_new, second_new)


SOURCES = 8
HOSTED = 4
SLOTS = SOURCES * CAP
OUT_BLOCKS = 2


def matmul(a, b, contract):
    return lax.dot_general(
        a, b, (((contract[0],), (contract[1],)), ((), ())), preferred_element_type=f32
    )


def expert_kernel(n_ref, g_ref, w_ref, dn_ref, out_ref, dw_ref, xs, ds, zs, gates):
    step = pl.program_id(0)
    base = lax.axis_index("x") * 8 + lax.axis_index("c")

    @pl.when(step == 0)
    def _():
        lane = lax.broadcasted_iota(jnp.int32, (16, 128), 1)
        sub = lax.broadcasted_iota(jnp.int32, (16, 128), 0)
        wanted = base + 2 * lax.rem(sub, HOSTED) + EXPERTS * (sub // HOSTED)
        choose = jnp.where((lane == wanted) & (sub < 3 * HOSTED), 1.0, 0.0).astype(bf16)
        slot = lax.broadcasted_iota(jnp.int32, (CAP, TOK), 0).astype(f32)

        def source(b, carry):
            fields = matmul(choose, n_ref[b, :, D:], (1, 1))
            hots = []
            for j in range(HOSTED):
                hot = slot == fields[j : j + 1]
                gate = fields[HOSTED + j : HOSTED + j + 1] + fields[2 * HOSTED + j : 2 * HOSTED + j + 1]
                span = pl.ds(pl.multiple_of(j * SLOTS + b * CAP, CAP), CAP)
                gates[span, :] = jnp.broadcast_to(
                    jnp.sum(jnp.where(hot, gate, 0.0), axis=1, keepdims=True), (CAP, 128)
                )
                hots.append(jnp.where(hot, 1.0, 0.0).astype(bf16))
            hots = jnp.concatenate(hots, axis=0)
            x = matmul(hots, n_ref[b, :, :D], (1, 0)).astype(bf16)
            d = matmul(hots, g_ref[b], (1, 0)).astype(bf16)
            for j in range(HOSTED):
                span = pl.ds(pl.multiple_of(j * SLOTS + b * CAP, CAP), CAP)
                xs[span, :] = x[j * CAP : (j + 1) * CAP]
                ds[span, :] = d[j * CAP : (j + 1) * CAP]
            return carry

        lax.fori_loop(0, SOURCES, source, 0)

    @pl.when(step < HOSTED)
    def _():
        expert = base + 2 * step
        rows = pl.ds(pl.multiple_of(step * SLOTS, SLOTS), SLOTS)
        gate = gates[rows, :][:, :1]
        w_gu = w_ref[0, :, : D // 4, :].reshape(D, 2 * FF_E)
        w_d = w_ref[0, :, D // 4 :, :].reshape(FF_E, D)
        gu = matmul(xs[rows, :], w_gu, (1, 0))
        g_part, u_part = gu[:, :FF_E], gu[:, FF_E:]
        sig = 1.0 / (1.0 + jnp.exp(-g_part))
        act = g_part * sig
        hid = (act * u_part).astype(bf16)
        y = matmul(hid, w_d, (1, 0)).astype(bf16).astype(f32)
        dout = ds[rows, :].astype(f32)
        dgate = jnp.sum(y * dout, axis=1, keepdims=True)
        dy = (gate * dout).astype(bf16)
        ds[rows, :] = (gate * y).astype(bf16)
        dh = matmul(dy, w_d, (1, 1))
        da_g = dh * u_part * (sig * (1.0 + g_part * (1.0 - sig)))
        da = jnp.concatenate([da_g, dh * act], axis=1).astype(bf16)
        dw_ref[0, :, D // 4 :, :] = (
            matmul(hid, dy, (0, 0)).astype(bf16).reshape(4, FF_E // 4, D)
        )
        dw_ref[0, :, : D // 4, :] = (
            matmul(xs[rows, :], da, (0, 0)).astype(bf16).reshape(4, D // 4, 2 * FF_E)
        )
        xs[rows, :] = matmul(da, w_gu, (1, 1)).astype(bf16)
        lane = lax.broadcasted_iota(jnp.int32, (SLOTS, 128), 1)
        high = dgate.astype(bf16).astype(f32)
        fields = jnp.where(lane == expert + EXPERTS, dgate - high, 0.0)
        zs[rows, :] = jnp.where(lane == expert, high, fields).astype(bf16)

    @pl.when(step >= HOSTED)
    def _():
        slot = lax.broadcasted_iota(jnp.int32, (TOK, HOSTED * CAP), 1)
        lane = lax.broadcasted_iota(jnp.int32, (TOK, 128), 1)
        for i in range(OUT_BLOCKS):
            b = (step - HOSTED) * OUT_BLOCKS + i
            meta = n_ref[b, :, D:].astype(f32)
            target = jnp.full((TOK, HOSTED * CAP), -1.0, f32)
            for j in reversed(range(HOSTED)):
                mine = lane == base + 2 * j
                rank = jnp.sum(jnp.where(mine, meta, 0.0), axis=1, keepdims=True)
                rank = jnp.where(rank < 0.0, -1.0, rank + j * CAP)
                target = jnp.where(slot < (j + 1) * CAP, rank, target)
            spread = jnp.where(slot.astype(f32) == target, 1.0, 0.0).astype(bf16)
            spans = [pl.ds(pl.multiple_of(j * SLOTS + b * CAP, CAP), CAP) for j in range(HOSTED)]
            for ref, out in ((xs, dn_ref.at[i, :, :D]), (zs, dn_ref.at[i, :, D:]), (ds, out_ref.at[i])):
                rows = jnp.concatenate([ref[span, :] for span in spans], axis=0)
                out[...] = matmul(spread, rows, (1, 0)).astype(bf16)


def experts(n_all, g_all, weights):
    wide = n_all.shape[2]
    slots = HOSTED * SLOTS

    def block(width):
        return pl.BlockSpec(
            (OUT_BLOCKS, TOK, width), lambda i: (jnp.maximum(i - HOSTED, 0), 0, 0)
        )

    def fixed(shape):
        return pl.BlockSpec(shape, lambda i: (0, 0, 0), pipeline_mode=pl.Buffered(1))

    def one(shape):
        return pl.BlockSpec((1,) + shape[1:], lambda i: (jnp.minimum(i, HOSTED - 1), 0, 0, 0))

    return pl.pallas_call(
        expert_kernel,
        grid=(HOSTED + SOURCES // OUT_BLOCKS,),
        out_shape=[
            jax.ShapeDtypeStruct(n_all.shape, bf16),
            jax.ShapeDtypeStruct(g_all.shape, bf16),
            jax.ShapeDtypeStruct(weights.shape, bf16),
        ],
        in_specs=[fixed(n_all.shape), fixed(g_all.shape), one(weights.shape)],
        out_specs=[block(wide), block(D), one(weights.shape)],
        scratch_shapes=[
            pltpu.VMEM((slots, D), bf16),
            pltpu.VMEM((slots, D), bf16),
            pltpu.VMEM((slots, 128), bf16),
            pltpu.VMEM((slots, 128), f32),
        ],
        compiler_params=pltpu.CompilerParams(
            dimension_semantics=("arbitrary",), vmem_limit_bytes=62 * 1024 * 1024
        ),
        cost_estimate=pl.CostEstimate(
            flops=slots * D * FF_E * 18, bytes_accessed=45_000_000, transcendentals=0
        ),
        name="experts",
    )(n_all, g_all, weights)


def turned_rows(u, cos, sin, back):
    lane = lax.broadcasted_iota(jnp.int32, (1, 128), 1)
    first = lax.rem(lane, HEAD_DIM) < HEAD_DIM // 2
    pieces = []
    for j in range(u.shape[1] // 128):
        v = u[:, j * 128 : (j + 1) * 128]
        w = v * sin if back else v
        ahead = pltpu.roll(w, 128 - HEAD_DIM // 2, 1)
        behind = pltpu.roll(w, HEAD_DIM // 2, 1)
        if back:
            pieces.append(v * cos + jnp.where(first, ahead, -behind))
        else:
            pieces.append(v * cos + jnp.where(first, -ahead, behind) * sin)
    return jnp.concatenate(pieces, axis=1)


def unpack_into(out, packed):
    def chunk(i, carry):
        x = packed[pl.ds(i * 16, 16), :, :512].astype(f32)
        rows = pl.ds(pl.multiple_of(i * 128, 128), 128)
        out[rows, :512] = x[:, :8].reshape(128, 512).astype(bf16)
        out[rows, 512:] = x[:, 8:].reshape(128, 512).astype(bf16)
        return carry

    lax.fori_loop(0, 8, chunk, 0)


def gain_rows(small):
    lane = lax.broadcasted_iota(jnp.int32, (8, 128), 1)
    sub = lax.broadcasted_iota(jnp.int32, (8, 128), 0)
    choose = (lane == EXPERTS + sub).astype(f32).astype(bf16)
    return matmul(choose, small, (1, 1))


def fill_bias(bias, length, first_row):
    rows = lax.broadcasted_iota(jnp.int32, bias.shape, 0) + first_row
    keys = lax.broadcasted_iota(jnp.int32, bias.shape, 1)
    bias[...] = jnp.where((keys <= rows) & (keys < length), 0.0, masked_score)


def front_kernel(
    length, wq_p, wkv_p, wo_p, tok, routes, cos, sin,
    n_out, n1_out, q_out, kv_out, lse_out, ho_out, r_out, gate_out, wq, wkv, wo, small_out,
    bias,
):
    z = lax.axis_index("z")
    unpack_into(wkv, wkv_p)
    unpack_into(wq, wq_p)

    def small_chunk(i, carry):
        x = wo_p[pl.ds(i * 16, 16), :, 512:].astype(f32)
        rows = pl.ds(pl.multiple_of(i * 128, 128), 128)
        small_out[rows, :] = x[:, :8].reshape(128, 128).astype(bf16)
        return carry

    lax.fori_loop(0, 8, small_chunk, 0)
    unpack_into(wo, wo_p)
    gains = gain_rows(small_out[...])
    fill_bias(bias, length[0], z * TOK)
    width = KV_HEADS * HEAD_DIM

    def block(b, carry):
        x = tok[b].astype(f32)
        n1 = (x * rms_scale(x) * gains[0:1]).astype(bf16)
        rows = pl.ds(pl.multiple_of(b * TOK, TOK), TOK)
        n1_out[rows, :] = n1
        kv = matmul(n1, wkv[...], (1, 0))
        kv_out[rows, :width] = turned_rows(
            kv[:, :width], cos[rows, :], sin[rows, :], False
        ).astype(bf16)
        kv_out[rows, width:] = kv[:, width:].astype(bf16)
        return carry

    lax.fori_loop(0, 4, block, 0)
    own = pl.ds(pl.multiple_of(z * TOK, TOK), TOK)
    q = matmul(n1_out[own, :], wq[...], (1, 0))
    q = turned_rows(q, cos[own, :], sin[own, :], False).astype(bf16)
    q_out[...] = q * jnp.asarray(HEAD_DIM ** (-0.5), bf16)
    lse_out[...] = jnp.zeros_like(lse_out)
    lane = lax.broadcasted_iota(jnp.int32, (TOK, 128), 1)

    def heads(j, carry):
        keys = kv_out[:, pl.ds(pl.multiple_of(j * 128, 128), 128)]
        values = kv_out[:, pl.ds(pl.multiple_of(width + j * 128, 128), 128)]
        for g in (0, 1):
            span = pl.ds(pl.multiple_of(j * 256 + g * 128, 128), 128)
            qs = q_out[:, span]
            key = keys[:, g * HEAD_DIM : (g + 1) * HEAD_DIM]
            value = values[:, g * HEAD_DIM : (g + 1) * HEAD_DIM]
            mixed = []
            for h in (0, 1):
                s = matmul(qs[:, h * HEAD_DIM : (h + 1) * HEAD_DIM], key, (1, 1)) + bias[...]
                top = jnp.max(s, axis=1, keepdims=True)
                p = jnp.exp(s - top)
                total = jnp.sum(p, axis=1, keepdims=True)
                p = (p * (1.0 / total)).astype(bf16)
                mixed.append(matmul(p, value, (1, 0)))
                head = j * 4 + g * 2 + h
                lse_out[...] = jnp.where(lane == head, top + jnp.log(total), lse_out[...])
            ho_out[:, span] = jnp.concatenate(mixed, axis=1).astype(bf16)
        return carry

    lax.fori_loop(0, 4, heads, 0)
    r = tok[z].astype(f32) + matmul(ho_out[...], wo[...], (1, 0))
    r_out[...] = r
    n2 = (r * rms_scale(r) * gains[1:2]).astype(bf16)
    n_out[:, :D] = n2
    logits = matmul(n2, small_out[...], (1, 0))
    hits = lane == routes[:, 0:1]
    for k in range(1, routes.shape[1]):
        hits = hits | (lane == routes[:, k : k + 1])
    lifted = jnp.where(hits, logits, masked_score)
    lifted = jnp.where(hits, jnp.exp(lifted - jnp.max(lifted, axis=1, keepdims=True)), 0.0)
    gate = lifted / jnp.sum(lifted, axis=1, keepdims=True)
    gate_out[...] = gate
    row = lax.broadcasted_iota(jnp.int32, (TOK, TOK), 0)
    col = lax.broadcasted_iota(jnp.int32, (TOK, TOK), 1)
    earlier = jnp.where(col < row, 1.0, 0.0).astype(bf16)
    ranks = matmul(earlier, jnp.where(hits, 1.0, 0.0).astype(bf16), (1, 0))
    high = gate.astype(bf16).astype(f32)
    meta = jnp.where(hits, ranks, jnp.where(lane < EXPERTS, -1.0, 0.0))
    meta = meta + pltpu.roll(high, EXPERTS, 1) + pltpu.roll(gate - high, 2 * EXPERTS, 1)
    n_out[:, D:] = meta.astype(bf16)


def front(length, w_q, w_kv, w_o, tok, routes, cos, sin):
    vmem = pl.BlockSpec(memory_space=pltpu.VMEM)
    square = jax.ShapeDtypeStruct((D, D), bf16)
    rows = jax.ShapeDtypeStruct((TOK, D), bf16)
    lanes = jax.ShapeDtypeStruct((TOK, 128), f32)
    return pl.pallas_call(
        front_kernel,
        out_shape=[
            jax.ShapeDtypeStruct((TOK, D + 128), bf16),
            square,
            rows,
            square,
            lanes,
            rows,
            jax.ShapeDtypeStruct((TOK, D), f32),
            lanes,
            square,
            square,
            square,
            jax.ShapeDtypeStruct((D, 128), bf16),
        ],
        in_specs=[pl.BlockSpec(memory_space=pltpu.SMEM)] + [vmem] * 7,
        out_specs=[vmem] * 12,
        scratch_shapes=[pltpu.VMEM((TOK, 4 * TOK), f32)],
        compiler_params=pltpu.CompilerParams(vmem_limit_bytes=56 * 1024 * 1024),
        cost_estimate=pl.CostEstimate(
            flops=10**10, bytes_accessed=30_000_000, transcendentals=5_000_000
        ),
        name="front",
    )(length, w_q, w_kv, w_o, tok, routes, cos, sin)


def rms_back(values, scale, gain, dnormed):
    scaled = values * scale
    dscaled = dnormed * gain
    dvalues = scale * (dscaled - scaled * jnp.mean(dscaled * scaled, axis=-1, keepdims=True))
    return dvalues, jnp.sum(dnormed * scaled, axis=0, keepdims=True)


def pack_into(out, value):
    def chunk(i, carry):
        rows = pl.ds(pl.multiple_of(i * 128, 128), 128)
        left = value[rows, :512].reshape(16, 8, 512)
        right = value[rows, 512:].reshape(16, 8, 512)
        out[pl.ds(i * 16, 16), :, :512] = jnp.concatenate([left, right], axis=1).astype(bf16)
        return carry

    lax.fori_loop(0, 8, chunk, 0)


def back_kernel(
    length, sums, dout, n_ext, r_ref, gate_ref, ho, q_ref, kv, lse, n1, tok, wq, wkv, wo, small,
    cos, sin, cos_t, sin_t,
    dwq_p, dwkv_p, dwo_p, dn1_out, dr_out,
    bias, square, dkv_t, dq_s, do_s, dkv_s,
):
    z = lax.axis_index("z")
    own = pl.ds(pl.multiple_of(z * TOK, TOK), TOK)
    gains = gain_rows(small[...])
    lane = lax.broadcasted_iota(jnp.int32, (TOK, 128), 1)
    gate = gate_ref[...]
    fields = sums[:, D:]
    dgate = fields + pltpu.roll(fields, 128 - EXPERTS, 1)
    mean = jnp.sum(gate * dgate, axis=1, keepdims=True)
    dlogits = (gate * (dgate - mean)).astype(bf16)
    dn2 = sums[:, :D] + matmul(dlogits, small[...], (1, 1))
    d_router = matmul(n_ext[:, :D], dlogits, (0, 0))
    r = r_ref[...]
    dr, dg2 = rms_back(r, rms_scale(r), gains[1:2], dn2)
    dr = dr + dout[...].astype(f32)
    dr_out[...] = dr
    d_att = dr.astype(bf16)
    square[...] = matmul(ho[...], d_att, (0, 0))
    pack_into(dwo_p, square)
    do_s[...] = matmul(d_att, wo[...], (1, 1)).astype(bf16)
    fill_bias(bias, length[0], z * TOK)
    width = KV_HEADS * HEAD_DIM
    scale = HEAD_DIM ** (-0.5)

    def heads(j, carry):
        keys = kv[:, pl.ds(pl.multiple_of(j * 128, 128), 128)]
        values = kv[:, pl.ds(pl.multiple_of(width + j * 128, 128), 128)]
        for g in (0, 1):
            span = pl.ds(pl.multiple_of(j * 256 + g * 128, 128), 128)
            qs, dos = q_ref[:, span], do_s[:, span]
            prods = dos.astype(f32) * ho[:, span].astype(f32)
            key = keys[:, g * HEAD_DIM : (g + 1) * HEAD_DIM]
            value = values[:, g * HEAD_DIM : (g + 1) * HEAD_DIM]
            dqs = []
            dk_t, dv_t = 0.0, 0.0
            for h in (0, 1):
                part = slice(h * HEAD_DIM, (h + 1) * HEAD_DIM)
                head = j * 4 + g * 2 + h
                shift_by = jnp.sum(jnp.where(lane == head, lse[...], 0.0), axis=1, keepdims=True)
                mine = (lane >= h * HEAD_DIM) & (lane < (h + 1) * HEAD_DIM)
                delta = jnp.sum(jnp.where(mine, prods, 0.0), axis=1, keepdims=True)
                p = jnp.exp(matmul(qs[:, part], key, (1, 1)) + bias[...] - shift_by)
                dp = matmul(dos[:, part], value, (1, 1))
                ds = (p * (dp - delta)).astype(bf16)
                dqs.append(matmul(ds, key, (1, 0)) * scale)
                dk_t = dk_t + matmul(qs[:, part], ds, (0, 0))
                dv_t = dv_t + matmul(dos[:, part], p.astype(bf16), (0, 0))
            dq_s[:, span] = jnp.concatenate(dqs, axis=1)
            half = HEAD_DIM // 2
            wave = dk_t * sin_t[...]
            dk_t = dk_t * cos_t[...] + jnp.concatenate([wave[half:], -wave[:half]], axis=0)
            at = j * 128 + g * HEAD_DIM
            dkv_t[pl.ds(pl.multiple_of(at, HEAD_DIM), HEAD_DIM), :] = dk_t
            dkv_t[pl.ds(pl.multiple_of(width + at, HEAD_DIM), HEAD_DIM), :] = dv_t
        return carry

    lax.fori_loop(0, 4, heads, 0)

    def flip(i, carry):
        at = pl.ds(pl.multiple_of(i * 128, 128), 128)
        dkv_s[:, at] = jnp.transpose(dkv_t[at, :]).astype(bf16)
        return carry

    lax.fori_loop(0, 8, flip, 0)
    dq = turned_rows(dq_s[...], cos[own, :], sin[own, :], True).astype(bf16)
    square[...] = matmul(n1[own, :], dq, (0, 0))
    pack_into(dwq_p, square)
    square[...] = matmul(n1[...], dkv_s[...], (0, 0))
    pack_into(dwkv_p, square)
    square[...] = matmul(dkv_s[...], wkv[...], (1, 1))
    square[own, :] += matmul(dq, wq[...], (1, 1))
    dg1 = jnp.zeros((1, D), f32)
    for b in range(4):
        rows = slice(b * TOK, (b + 1) * TOK)
        x = tok[b].astype(f32)
        dn1 = square[rows, :]
        dg1 = dg1 + jnp.sum(dn1 * (x * rms_scale(x)), axis=0, keepdims=True)
        dn1_out[b] = dn1.astype(bf16)
    sub = lax.broadcasted_iota(jnp.int32, (8, D), 0)
    dgs = jnp.where(sub == 0, dg1, jnp.where(sub == 1, dg2, 0.0))
    high = dgs.astype(bf16)
    low = (dgs - high.astype(f32)).astype(bf16)
    place_lane = lax.broadcasted_iota(jnp.int32, (8, 128), 1)
    place_sub = lax.broadcasted_iota(jnp.int32, (8, 128), 0)
    spread = (place_lane == EXPERTS + place_sub).astype(f32).astype(bf16)
    d_small = d_router + matmul(high, spread, (0, 0)) + matmul(low, spread, (0, 0))
    d_small = d_small.reshape(128, 8, 128)
    dwo_p[:, :, 512:] = jnp.concatenate([d_small, jnp.zeros_like(d_small)], axis=1).astype(bf16)


def back(*args):
    vmem = pl.BlockSpec(memory_space=pltpu.VMEM)
    return pl.pallas_call(
        back_kernel,
        out_shape=[
            jax.ShapeDtypeStruct((128, 16, 512), bf16),
            jax.ShapeDtypeStruct((128, 16, 512), bf16),
            jax.ShapeDtypeStruct((128, 16, 640), bf16),
            jax.ShapeDtypeStruct((4, TOK, D), bf16),
            jax.ShapeDtypeStruct((TOK, D), f32),
        ],
        in_specs=[pl.BlockSpec(memory_space=pltpu.SMEM)] + [vmem] * 19,
        out_specs=[vmem] * 5,
        scratch_shapes=[
            pltpu.VMEM((TOK, 4 * TOK), f32),
            pltpu.VMEM((D, D), f32),
            pltpu.VMEM((D, D), f32),
            pltpu.VMEM((TOK, D), f32),
            pltpu.VMEM((TOK, D), bf16),
            pltpu.VMEM((D, D), bf16),
        ],
        compiler_params=pltpu.CompilerParams(vmem_limit_bytes=60 * 1024 * 1024),
        cost_estimate=pl.CostEstimate(
            flops=2 * 10**10, bytes_accessed=40_000_000, transcendentals=5_000_000
        ),
        name="back",
    )(*args)


def pack_matrix(shard):
    half = shard.shape[1] // 2
    return jnp.concatenate([shard[:, :half], shard[:, half:]], axis=0)


def unpack_matrix(packed):
    return jnp.concatenate([packed[:8], packed[8:]], axis=1)


def body(
    tokens, routes, lengths, out_grad,
    query_weight, query_mean, query_square,
    keyval_weight, keyval_mean, keyval_square,
    output_weight, output_mean, output_square,
    router_weight, router_mean, router_square,
    norm_gains, gains_mean, gains_square,
    gateup_weight, gateup_mean, gateup_square,
    down_weight, down_mean, down_square,
):
    row_count = tokens.shape[0]
    seq_len = row_count * 4
    query_width = HEADS * HEAD_DIM

    small = jnp.concatenate(
        [router_weight, norm_gains.T, jnp.zeros((8, 128 - EXPERTS - 2), f32)], axis=1
    )
    small = jnp.concatenate([small, jnp.zeros((8, 128), f32)], axis=0)
    expert_b = lax.all_gather(
        jnp.concatenate([gateup_weight[0], down_weight[0]], axis=0).astype(bf16),
        ("y", "z"),
        axis=0,
    )
    w_q, w_kv, w_o, all_tokens, dout_all = gather_front(
        pack_matrix(query_weight).astype(bf16),
        pack_matrix(keyval_weight).astype(bf16),
        jnp.concatenate([pack_matrix(output_weight), small], axis=1).astype(bf16),
        tokens,
        out_grad,
    )
    cos, sin = rotary_tables(jnp.arange(seq_len, dtype=jnp.int32), HEAD_DIM // 2)
    cos2, sin2 = jnp.tile(cos, (1, 2)), jnp.tile(sin, (1, 2))
    n_ext, n1, q, kv, lse, ho, residual, gate, query_b, keyval_b, output_b, small_b = front(
        lengths,
        w_q.reshape(128, 16, 512),
        w_kv.reshape(128, 16, 512),
        w_o.reshape(128, 16, 640),
        all_tokens,
        routes,
        cos2,
        sin2,
    )
    n_all = gather_rows(n_ext)
    wide = n_all.shape[-1]
    dn_parts, out_parts, d_expert = experts(
        n_all.reshape(SOURCES, row_count, wide),
        dout_all.reshape(SOURCES, row_count, D),
        expert_b.reshape((4,) + (4, D // 4 + FF_E // 4, D)),
    )
    grad_expert = lax.psum_scatter(
        d_expert.reshape((16,) + d_expert.shape[2:]),
        ("y", "z"),
        scatter_dimension=0,
        tiled=False,
    ).astype(f32)
    sums = sum_rows(dn_parts.reshape(4, 2, row_count, wide))
    d_query, d_keyval, d_last, dn1, dresidual = back(
        lengths, sums, out_grad, n_ext, residual, gate, ho, q, kv, lse, n1, all_tokens,
        query_b, keyval_b, output_b, small_b, cos2, sin2, cos.T, sin.T,
    )
    g_query, g_keyval, g_last, dn1_sum, mixed_out = sum_back(
        (
            d_query.reshape(4, 4, 2, 4, 16, 512),
            d_keyval.reshape(4, 4, 2, 4, 16, 512),
            d_last.reshape(4, 4, 2, 4, 16, 640),
        ),
        dn1,
        out_parts.reshape(4, 2, row_count, D),
    )
    layer_out = (residual + mixed_out).astype(bf16)
    grad_query, grad_keyval, grad_output = (
        unpack_matrix(g) for g in (g_query, g_keyval, g_last[:, :512])
    )
    grad_router = g_last[:8, 512 : 512 + EXPERTS]
    grad_gains = g_last[:8, 512 + EXPERTS : 512 + EXPERTS + 2].T
    inputs = tokens.astype(f32)
    gain_one = small_b[:, EXPERTS].astype(f32)
    dnorm_one, _ = norm_back(inputs, rms_scale(inputs), gain_one, dn1_sum)
    tokens_grad = dresidual + dnorm_one

    rate = 0.5
    query_new = adamw(query_weight, grad_query, query_mean, query_square, rate * D ** (-0.5), 0.1)
    keyval_new = adamw(
        keyval_weight, grad_keyval, keyval_mean, keyval_square, rate * D ** (-0.5), 0.1
    )
    output_new = adamw(
        output_weight,
        grad_output,
        output_mean,
        output_square,
        rate * max(1, 2 * query_width // seq_len) ** (-0.5),
        0.1,
    )
    router_new = adamw(
        router_weight, grad_router, router_mean, router_square, rate * (4 * D) ** (-0.5), 0.1
    )
    gains_new = adamw(norm_gains, grad_gains, gains_mean, gains_square, 0.6, 0.0)
    gateup_new = adamw(
        gateup_weight,
        grad_expert[None, : D // 4],
        gateup_mean,
        gateup_square,
        rate * D ** (-0.5),
        0.1,
    )
    down_new = adamw(
        down_weight,
        grad_expert[None, D // 4 :],
        down_mean,
        down_square,
        rate * (FF_E // 8) ** (-0.5),
        0.1,
    )
    return (
        (layer_out, tokens_grad)
        + query_new
        + keyval_new
        + output_new
        + router_new
        + gains_new
        + gateup_new
        + down_new
    )


def solution(mesh):
    devices = jax.sharding.Mesh(mesh.devices.reshape(4, 4, 2, 4), ("x", "y", "c", "z"))
    every = ("x", "y", "c", "z")
    rows = P(every, None)
    gains = P(None, every)
    shard = P(("x", "y", "c"), "z", None)
    return jax.shard_map(
        body,
        mesh=devices,
        in_specs=(rows, rows, P(("x", "y", "c")), rows)
        + (rows,) * 12
        + (gains,) * 3
        + (shard,) * 6,
        out_specs=(rows, rows) + (rows,) * 12 + (gains,) * 3 + (shard,) * 6,
        check_vma=False,
    )
```

```python
import jax
import jax.numpy as jnp
from jax import lax
from jax.experimental import pallas as pl
from jax.experimental.pallas import tpu as pltpu
from jax.sharding import PartitionSpec as P

MESH = pl.DeviceIdType.MESH
bf16 = jnp.bfloat16
f32 = jnp.float32
AXES = "xycz"
STRIP = 16


def place():
    return {a: lax.axis_index(a) for a in AXES}


def device(at):
    return tuple(at[a] for a in AXES)


def shift(at, axis, by):
    size = 2 if axis == "c" else 4
    return lax.rem(at[axis] + by, size)


def peer(at, axis, by):
    return device({**at, axis: shift(at, axis, by)})


def greet(at, axes):
    barrier = pltpu.get_barrier_semaphore()
    count = 0
    for axis in axes:
        for by in (1,) if axis == "c" else (1, 2, 3):
            pl.semaphore_signal(
                barrier, inc=1, device_id=peer(at, axis, by), device_id_type=MESH
            )
            count += 1
    pl.semaphore_wait(barrier, count)


class Wires:
    def __init__(self, send_sems, recv_sems, local_sems):
        self.send_sems, self.recv_sems, self.local_sems = send_sems, recv_sems, local_sems
        self.copies, self.local = [], 0

    def send(self, src, dst, target):
        at = len(self.copies)
        copy = pltpu.make_async_remote_copy(
            src_ref=src,
            dst_ref=dst,
            send_sem=self.send_sems.at[at],
            recv_sem=self.recv_sems.at[at],
            device_id=target,
            device_id_type=MESH,
        )
        copy.start()
        self.copies.append(copy)
        return copy

    def keep(self, src, dst):
        copy = pltpu.make_async_copy(src, dst, self.local_sems.at[self.local])
        copy.start()
        self.local += 1
        return copy

    def finish(self):
        for copy in self.copies:
            copy.wait_send()


def wire_sems(copies, kept):
    return [
        pltpu.SemaphoreType.DMA((copies,)),
        pltpu.SemaphoreType.DMA((copies,)),
        pltpu.SemaphoreType.DMA((kept,)),
    ]


def in_order(order, **steps):
    for letter in order:
        next(steps[letter], None)
    for step in steps.values():
        for _ in step:
            pass


def hbm(*arrays):
    return [pltpu.with_memory_space_constraint(v, pltpu.HBM) for v in arrays]


def ring_steps(wires, at, axis, spot, hand_on):
    right, left = peer(at, axis, 1), peer(at, axis, 3)
    to_right = {k: wires.send(spot(0, k), spot(0, k), right) for k in (0, 1)}
    to_left = {k: wires.send(spot(0, k), spot(0, k), left) for k in (1, 0)}
    for k in (0, 1):
        hand_on(0, k)
    yield
    to_right[0].wait_recv()
    far_right = wires.send(spot(3, 0), spot(3, 0), right)
    hand_on(3, 0)
    to_left[1].wait_recv()
    far_left = wires.send(spot(1, 1), spot(1, 1), left)
    hand_on(1, 1)
    yield
    to_right[1].wait_recv()
    hand_on(3, 1)
    to_left[0].wait_recv()
    hand_on(1, 0)
    yield
    far_right.wait_recv()
    hand_on(2, 0)
    far_left.wait_recv()
    hand_on(2, 1)


def row_steps(wires, at, held, out):
    half = held.shape[2] // 2
    sibling = peer(at, "c", 1)
    other = shift(at, "c", 1)
    across, kept = [], []

    def hand_on(by, part):
        rows = pl.ds(part * half, half)
        unit, theirs = (
            (shift(at, "x", by), c, rows) for c in (at["c"], other)
        )
        across.append((theirs, wires.send(held.at[unit], held.at[unit], sibling)))
        kept.append(wires.keep(held.at[unit], out.at[unit]))

    def spot(by, part):
        return held.at[shift(at, "x", by), at["c"], pl.ds(part * half, half)]

    yield from ring_steps(wires, at, "x", spot, hand_on)
    yield
    for unit, copy in across:
        copy.wait_recv()
        kept.append(wires.keep(held.at[unit], out.at[unit]))
    for copy in kept:
        copy.wait()


ROW_KEPT = 16
ROW_COPIES = 6 + 8


def token_steps(wires, at, held):
    half = held.shape[1] // 2

    def spot(by, part):
        return held.at[shift(at, "z", by), pl.ds(part * half, half)]

    yield from ring_steps(wires, at, "z", spot, lambda by, part: None)


TOKEN_COPIES = 6


def index(at, whole, **fixed):
    spots = {**at, **{a: slice(None) for a in whole}, **fixed}
    return tuple(spots[axis] for axis in AXES)


def weight_steps(wires, at, parts):
    kept = [wires.keep(w, o.at[index(at, "")]) for w, o, _ in parts]
    arrivals = {}
    for p, (w, o, order) in enumerate(parts):
        for by in (1, 3, 2):
            arrivals[p, by] = wires.send(w, o.at[index(at, "")], peer(at, order[0], by))
    yield
    for copy in kept:
        copy.wait()
    later = {}
    for p, (w, o, order) in enumerate(parts):
        for by in (1, 3, 2):
            arrivals[p, by].wait_recv()
        spot = index(at, order[0])
        for by in (1, 3, 2):
            later[p, by] = wires.send(o.at[spot], o.at[spot], peer(at, order[1], by))
    yield
    sibling = peer(at, "c", 1)
    across, rings = [], []
    for p, (w, o, order) in enumerate(parts):
        for by in (1, 3, 2):
            later[p, by].wait_recv()

        def spot(by, part, o=o, order=order):
            pieces = {order[1]: pl.ds(2 * part, 2), order[2]: shift(at, order[2], by)}
            return o.at[index(at, order[0], **pieces)]

        def hand_on(by, part, spot=spot):
            across.append(wires.send(spot(by, part), spot(by, part), sibling))

        ring = ring_steps(wires, at, order[2], spot, hand_on)
        next(ring)
        rings.append(ring)
    yield
    for _ in range(3):
        for ring in rings:
            next(ring, None)
        yield
    for copy in across:
        copy.wait_recv()


WEIGHT_COPIES = 3 * (3 + 3 + 6 + 8)


def add_rows(out, parts, rows):
    def strip(i, carry):
        span = pl.ds(pl.multiple_of(i * STRIP, STRIP), STRIP)
        total = parts[0][span].astype(f32)
        for part in parts[1:]:
            total = total + part[span].astype(f32)
        out[span] = total.astype(out.dtype)
        return carry

    lax.fori_loop(0, rows // STRIP, strip, 0)


def ring_sum_steps(wires, at, axis, blocks, out, mid, last, near):
    half = out.shape[0] // 2
    low, high = pl.ds(0, half), pl.ds(half, half)
    ahead, back, far = (blocks.at[shift(at, axis, by)] for by in (1, 3, 2))
    right, left = peer(at, axis, 1), peer(at, axis, 3)
    near_l = wires.send(far.at[low], near.at[0], right)
    near_r = wires.send(far.at[high], near.at[1], left)
    pure_l = wires.send(ahead.at[high], last.at[0, high], right)
    pure_r = wires.send(back.at[low], last.at[1, low], left)
    yield
    near_l.wait_recv()
    add_rows(mid.at[0], [ahead.at[low], near.at[0]], half)
    sum_l = wires.send(mid.at[0], last.at[0, low], right)
    near_r.wait_recv()
    add_rows(mid.at[1], [back.at[high], near.at[1]], half)
    sum_r = wires.send(mid.at[1], last.at[1, high], left)
    yield
    for copy in (pure_l, sum_l, pure_r, sum_r):
        copy.wait_recv()
    add_rows(out, [blocks.at[at[axis]], last.at[0], last.at[1]], 2 * half)


def ring_sum_scratch(rows, width):
    return [
        pltpu.VMEM((2, rows // 2, width), bf16),
        pltpu.VMEM((2, rows, width), bf16),
        pltpu.VMEM((2, rows // 2, width), bf16),
    ]


def row_sum_steps(wires, at, c_ref, out, held, crossed, mid, last, near):
    other = shift(at, "c", 1)
    sibling = peer(at, "c", 1)
    rows = out.shape[0]
    crossing, kept = {}, {}
    for by in (2, 1, 3, 0):
        i = shift(at, "x", by)
        crossing[by] = wires.send(c_ref.at[i, other], crossed.at[i], sibling)
        kept[by] = wires.keep(c_ref.at[i, at["c"]], held.at[i])
    yield
    for by in (2, 1, 3, 0):
        i = shift(at, "x", by)
        kept[by].wait()
        crossing[by].wait_recv()
        add_rows(held.at[i], [held.at[i], crossed.at[i]], rows)
        if by == 3:
            ring = ring_sum_steps(wires, at, "x", held, out, mid, last, near)
            next(ring)
    yield
    yield from ring


ROW_SUM_COPIES = 4 + 6


def row_sum_scratch(rows, width):
    return [pltpu.VMEM((4, rows, width), bf16)] * 2 + ring_sum_scratch(rows, width)


def sum_rows_kernel(c_ref, out, *refs):
    at = place()
    wires = Wires(*refs[-3:])
    greet(at, "xc")
    in_order("", p=row_sum_steps(wires, at, c_ref, out, *refs[:5]))
    wires.finish()


def sum_rows(c):
    rows, width = c.shape[-2:]
    return pl.pallas_call(
        sum_rows_kernel,
        out_shape=jax.ShapeDtypeStruct((rows, width), f32),
        in_specs=[pl.BlockSpec(memory_space=pltpu.HBM)],
        out_specs=pl.BlockSpec(memory_space=pltpu.VMEM),
        scratch_shapes=row_sum_scratch(rows, width) + wire_sems(ROW_SUM_COPIES, 4),
        compiler_params=pltpu.CompilerParams(
            collective_id=3, has_side_effects=True, vmem_limit_bytes=56 * 1024 * 1024
        ),
        name="sum_rows",
    )(*hbm(c))


SUM_ORDERS = ("yxz", "xyz", "zxy")
SUM_SCHEDULE = "mnpmmmpnpmmmmmm"


def pick(ref, axes, axis, mine):
    return ref.at[tuple(mine if a == axis else slice(None) for a in axes)]


def mat_steps(wires, at, mats, outs, crossed, held, one, two, three, sum1, sum2):
    sibling = peer(at, "c", 1)
    other = shift(at, "c", 1)
    crossing = [
        wires.send(mats[p].at[:, :, other], crossed[p], sibling) for p in range(3)
    ]

    def total(out, parts, count):
        def body(i, carry):
            value = parts[0][i].astype(f32)
            for part in parts[1:]:
                value = value + part[i].astype(f32)
            out[i] = value.astype(out.dtype)
            return carry

        lax.fori_loop(0, count, body, 0)

    stage1 = {}
    yield
    for p in range(3):
        crossing[p].wait_recv()

        def body(i, carry, p=p):
            mine = mats[p][i // 4, i % 4, at["c"]]
            held[p][i // 4, i % 4] = (
                mine.astype(f32) + crossed[p][i // 4, i % 4].astype(f32)
            ).astype(bf16)
            return carry

        lax.fori_loop(0, 16, body, 0)
        axis = SUM_ORDERS[p][0]
        for by in (2, 1, 3):
            stage1[p, by] = wires.send(
                pick(held[p], "xyz", axis, shift(at, axis, by)),
                one[p].at[by - 1],
                peer(at, axis, by),
            )
        yield
    stage2 = {}
    for p in range(3):
        axis, after = SUM_ORDERS[p][0], SUM_ORDERS[p][1]
        rest = "xyz".replace(axis, "")
        for by in (1, 3, 2):
            stage1[p, by].wait_recv()
        total(
            sum1[p],
            [pick(held[p], "xyz", axis, at[axis])] + [one[p].at[k] for k in range(3)],
            4,
        )
        for by in (2, 1, 3):
            stage2[p, by] = wires.send(
                pick(sum1[p], rest, after, shift(at, after, by)),
                two[p].at[by - 1],
                peer(at, after, by),
            )
        yield
    stage3 = {}
    for p in range(3):
        axis, after, end = SUM_ORDERS[p]
        rest = "xyz".replace(axis, "")
        for by in (1, 3, 2):
            stage2[p, by].wait_recv()
        total(
            sum2[p],
            [pick(sum1[p], rest, after, at[after])] + [two[p].at[k] for k in range(3)],
            4,
        )
        for by in (2, 1, 3):
            stage3[p, by] = wires.send(
                sum2[p].at[shift(at, end, by)], three[p].at[by - 1], peer(at, end, by)
            )
        yield
    for p in range(3):
        for by in (1, 3, 2):
            stage3[p, by].wait_recv()
        value = sum2[p][at[SUM_ORDERS[p][2]]].astype(f32)
        for k in range(3):
            value = value + three[p][k].astype(f32)
        outs[p][...] = value


def sum_back_kernel(*refs):
    mats, dn1, c_ref = refs[0:3], refs[3], refs[4]
    outs, dn1_out, mixed_out = refs[5:8], refs[8], refs[9]
    scratch = refs[10:-3]
    groups = [scratch[i * 3 : i * 3 + 3] for i in range(7)]
    at = place()
    wires = Wires(*refs[-3:])
    greet(at, "xyzc")
    in_order(
        SUM_SCHEDULE,
        p=row_sum_steps(wires, at, c_ref, mixed_out, *scratch[24:29]),
        m=mat_steps(wires, at, mats, outs, *groups),
        n=ring_sum_steps(wires, at, "z", dn1, dn1_out, *scratch[21:24]),
    )
    wires.finish()


def sum_back(mats, dn1, c):
    widths = [m.shape[-1] for m in mats]
    rows, model = dn1.shape[1:]
    scratch = []
    for lead in ((4, 4, 4), (4, 4, 4), (3, 4, 4), (3, 4), (3,), (4, 4), (4,)):
        scratch += [pltpu.VMEM(lead + (16, w), bf16) for w in widths]
    scratch += ring_sum_scratch(rows, model) + row_sum_scratch(rows, model)
    vmem = pl.BlockSpec(memory_space=pltpu.VMEM)
    return pl.pallas_call(
        sum_back_kernel,
        out_shape=[jax.ShapeDtypeStruct((16, w), f32) for w in widths]
        + [jax.ShapeDtypeStruct((rows, model), f32)] * 2,
        in_specs=[vmem] * 4 + [pl.BlockSpec(memory_space=pltpu.HBM)],
        out_specs=[vmem] * 5,
        scratch_shapes=scratch + wire_sems(3 * 10 + 6 + ROW_SUM_COPIES, 4),
        compiler_params=pltpu.CompilerParams(
            collective_id=4, has_side_effects=True, vmem_limit_bytes=60 * 1024 * 1024
        ),
        name="sum_back",
    )(*mats, dn1, *hbm(c))


D = 1024
HEADS = 16
KV_HEADS = 8
HEAD_DIM = 64
EXPERTS = 32
FF_E = 512
STEP = 10
CAP = 96
TOK = 256


norm_epsilon = 1e-06
beta_first = 0.9
beta_second = 0.95
adam_epsilon = 1e-08
masked_score = -1e30


def rotary_tables(positions, half_width):
    freqs = 10000.0 ** (-jnp.arange(half_width, dtype=jnp.float32) / half_width)
    angles = positions.astype(jnp.float32)[:, None] * freqs[None, :]
    cosines = jnp.cos(angles)
    sines = jnp.sin(angles)
    return (jnp.concatenate([cosines, cosines], 1), jnp.concatenate([sines, sines], 1))


def rotate(values, cosines, sines):
    half_width = values.shape[-1] // 2
    turned = jnp.concatenate([-values[..., half_width:], values[..., :half_width]], -1)
    return values * cosines[:, None, :] + turned * sines[:, None, :]


def rotate_back(grads, cosines, sines):
    half_width = grads.shape[-1] // 2
    scaled = grads * sines[:, None, :]
    return grads * cosines[:, None, :] + jnp.concatenate(
        [scaled[..., half_width:], -scaled[..., :half_width]], -1
    )


def rms_scale(values):
    return lax.rsqrt(jnp.mean(values * values, axis=-1, keepdims=True) + norm_epsilon)


def norm_back(values, scale, gain, dnormed):
    scaled = values * scale
    dgain = jnp.sum(dnormed * scaled, axis=0)
    dscaled = dnormed * gain
    dvalues = scale * (dscaled - scaled * jnp.mean(dscaled * scaled, axis=-1, keepdims=True))
    return (dvalues, dgain)


def masked_scores(grouped, whole_kv, positions, length):
    key_count = whole_kv.shape[0]
    key_width = whole_kv.shape[1] // 2
    heads_kv = grouped.shape[1]
    head_size = grouped.shape[3]
    all_keys = whole_kv[:, :key_width].reshape(key_count, heads_kv, head_size)
    all_values = whole_kv[:, key_width:].reshape(key_count, heads_kv, head_size)
    raw_scores = jnp.einsum(
        "qkgd,pkd->kgqp", grouped, all_keys, preferred_element_type=jnp.float32
    ) * head_size ** (-0.5)
    key_pos = jnp.arange(key_count, dtype=jnp.int32)
    allowed = (key_pos[None, :] <= positions[:, None]) & (key_pos[None, :] < length)
    return (jnp.where(allowed, raw_scores, masked_score), all_keys, all_values)


def adamw(weight, grad, first, second, rate, decay):
    first_new = beta_first * first + (1.0 - beta_first) * grad
    second_new = beta_second * second + (1.0 - beta_second) * grad * grad
    update = (
        first_new
        / (1.0 - beta_first**STEP)
        / (jnp.sqrt(second_new / (1.0 - beta_second**STEP)) + adam_epsilon)
    )
    return (weight - rate * (update + decay * weight), first_new, second_new)


SOURCES = 8
HOSTED = 4
SLOTS = SOURCES * CAP
OUT_BLOCKS = 2


def matmul(a, b, contract):
    return lax.dot_general(
        a, b, (((contract[0],), (contract[1],)), ((), ())), preferred_element_type=f32
    )


def expert_kernel(n_ref, g_ref, w_ref, dn_ref, out_ref, dw_ref, xs, ds, zs, gates):
    step = pl.program_id(0)
    base = lax.axis_index("x") * 8 + lax.axis_index("c")

    @pl.when(step == 0)
    def _():
        lane = lax.broadcasted_iota(jnp.int32, (16, 128), 1)
        sub = lax.broadcasted_iota(jnp.int32, (16, 128), 0)
        wanted = base + 2 * lax.rem(sub, HOSTED) + EXPERTS * (sub // HOSTED)
        choose = jnp.where((lane == wanted) & (sub < 3 * HOSTED), 1.0, 0.0).astype(bf16)
        slot = lax.broadcasted_iota(jnp.int32, (CAP, TOK), 0).astype(f32)

        def source(b, carry):
            fields = matmul(choose, n_ref[b, :, D:], (1, 1))
            hots = []
            for j in range(HOSTED):
                hot = slot == fields[j : j + 1]
                gate = fields[HOSTED + j : HOSTED + j + 1] + fields[2 * HOSTED + j : 2 * HOSTED + j + 1]
                span = pl.ds(pl.multiple_of(j * SLOTS + b * CAP, CAP), CAP)
                gates[span, :] = jnp.broadcast_to(
                    jnp.sum(jnp.where(hot, gate, 0.0), axis=1, keepdims=True), (CAP, 128)
                )
                hots.append(jnp.where(hot, 1.0, 0.0).astype(bf16))
            hots = jnp.concatenate(hots, axis=0)
            x = matmul(hots, n_ref[b, :, :D], (1, 0)).astype(bf16)
            d = matmul(hots, g_ref[b], (1, 0)).astype(bf16)
            for j in range(HOSTED):
                span = pl.ds(pl.multiple_of(j * SLOTS + b * CAP, CAP), CAP)
                xs[span, :] = x[j * CAP : (j + 1) * CAP]
                ds[span, :] = d[j * CAP : (j + 1) * CAP]
            return carry

        lax.fori_loop(0, SOURCES, source, 0)

    @pl.when(step < HOSTED)
    def _():
        expert = base + 2 * step
        rows = pl.ds(pl.multiple_of(step * SLOTS, SLOTS), SLOTS)
        gate = gates[rows, :][:, :1]
        w_gu = w_ref[0, :, : D // 4, :].reshape(D, 2 * FF_E)
        w_d = w_ref[0, :, D // 4 :, :].reshape(FF_E, D)
        gu = matmul(xs[rows, :], w_gu, (1, 0))
        g_part, u_part = gu[:, :FF_E], gu[:, FF_E:]
        sig = 1.0 / (1.0 + jnp.exp(-g_part))
        act = g_part * sig
        hid = (act * u_part).astype(bf16)
        y = matmul(hid, w_d, (1, 0)).astype(bf16).astype(f32)
        dout = ds[rows, :].astype(f32)
        dgate = jnp.sum(y * dout, axis=1, keepdims=True)
        dy = (gate * dout).astype(bf16)
        ds[rows, :] = (gate * y).astype(bf16)
        dh = matmul(dy, w_d, (1, 1))
        da_g = dh * u_part * (sig * (1.0 + g_part * (1.0 - sig)))
        da = jnp.concatenate([da_g, dh * act], axis=1).astype(bf16)
        dw_ref[0, :, D // 4 :, :] = (
            matmul(hid, dy, (0, 0)).astype(bf16).reshape(4, FF_E // 4, D)
        )
        dw_ref[0, :, : D // 4, :] = (
            matmul(xs[rows, :], da, (0, 0)).astype(bf16).reshape(4, D // 4, 2 * FF_E)
        )
        xs[rows, :] = matmul(da, w_gu, (1, 1)).astype(bf16)
        lane = lax.broadcasted_iota(jnp.int32, (SLOTS, 128), 1)
        high = dgate.astype(bf16).astype(f32)
        fields = jnp.where(lane == expert + EXPERTS, dgate - high, 0.0)
        zs[rows, :] = jnp.where(lane == expert, high, fields).astype(bf16)

    @pl.when(step >= HOSTED)
    def _():
        slot = lax.broadcasted_iota(jnp.int32, (TOK, HOSTED * CAP), 1)
        lane = lax.broadcasted_iota(jnp.int32, (TOK, 128), 1)
        for i in range(OUT_BLOCKS):
            b = (step - HOSTED) * OUT_BLOCKS + i
            meta = n_ref[b, :, D:].astype(f32)
            target = jnp.full((TOK, HOSTED * CAP), -1.0, f32)
            for j in reversed(range(HOSTED)):
                mine = lane == base + 2 * j
                rank = jnp.sum(jnp.where(mine, meta, 0.0), axis=1, keepdims=True)
                rank = jnp.where(rank < 0.0, -1.0, rank + j * CAP)
                target = jnp.where(slot < (j + 1) * CAP, rank, target)
            spread = jnp.where(slot.astype(f32) == target, 1.0, 0.0).astype(bf16)
            spans = [pl.ds(pl.multiple_of(j * SLOTS + b * CAP, CAP), CAP) for j in range(HOSTED)]
            for ref, out in ((xs, dn_ref.at[i, :, :D]), (zs, dn_ref.at[i, :, D:]), (ds, out_ref.at[i])):
                rows = jnp.concatenate([ref[span, :] for span in spans], axis=0)
                out[...] = matmul(spread, rows, (1, 0)).astype(bf16)


def experts(n_all, g_all, weights):
    wide = n_all.shape[2]
    slots = HOSTED * SLOTS

    def block(width):
        return pl.BlockSpec(
            (OUT_BLOCKS, TOK, width), lambda i: (jnp.maximum(i - HOSTED, 0), 0, 0)
        )

    def fixed(shape):
        return pl.BlockSpec(shape, lambda i: (0, 0, 0), pipeline_mode=pl.Buffered(1))

    def one(shape):
        return pl.BlockSpec((1,) + shape[1:], lambda i: (jnp.minimum(i, HOSTED - 1), 0, 0, 0))

    return pl.pallas_call(
        expert_kernel,
        grid=(HOSTED + SOURCES // OUT_BLOCKS,),
        out_shape=[
            jax.ShapeDtypeStruct(n_all.shape, bf16),
            jax.ShapeDtypeStruct(g_all.shape, bf16),
            jax.ShapeDtypeStruct(weights.shape, bf16),
        ],
        in_specs=[fixed(n_all.shape), fixed(g_all.shape), one(weights.shape)],
        out_specs=[block(wide), block(D), one(weights.shape)],
        scratch_shapes=[
            pltpu.VMEM((slots, D), bf16),
            pltpu.VMEM((slots, D), bf16),
            pltpu.VMEM((slots, 128), bf16),
            pltpu.VMEM((slots, 128), f32),
        ],
        compiler_params=pltpu.CompilerParams(
            dimension_semantics=("arbitrary",), vmem_limit_bytes=62 * 1024 * 1024
        ),
        cost_estimate=pl.CostEstimate(
            flops=slots * D * FF_E * 18, bytes_accessed=45_000_000, transcendentals=0
        ),
        name="experts",
    )(n_all, g_all, weights)


def turned_rows(u, cos, sin, back):
    lane = lax.broadcasted_iota(jnp.int32, (1, 128), 1)
    first = lax.rem(lane, HEAD_DIM) < HEAD_DIM // 2
    pieces = []
    for j in range(u.shape[1] // 128):
        v = u[:, j * 128 : (j + 1) * 128]
        w = v * sin if back else v
        ahead = pltpu.roll(w, 128 - HEAD_DIM // 2, 1)
        behind = pltpu.roll(w, HEAD_DIM // 2, 1)
        if back:
            pieces.append(v * cos + jnp.where(first, ahead, -behind))
        else:
            pieces.append(v * cos + jnp.where(first, -ahead, behind) * sin)
    return jnp.concatenate(pieces, axis=1)


def unpack_into(out, packed):
    def chunk(i, carry):
        x = packed[pl.ds(i * 16, 16), :, :512].astype(f32)
        rows = pl.ds(pl.multiple_of(i * 128, 128), 128)
        out[rows, :512] = x[:, :8].reshape(128, 512).astype(bf16)
        out[rows, 512:] = x[:, 8:].reshape(128, 512).astype(bf16)
        return carry

    lax.fori_loop(0, 8, chunk, 0)


def gain_rows(small):
    lane = lax.broadcasted_iota(jnp.int32, (8, 128), 1)
    sub = lax.broadcasted_iota(jnp.int32, (8, 128), 0)
    choose = (lane == EXPERTS + sub).astype(f32).astype(bf16)
    return matmul(choose, small, (1, 1))


def fill_bias(bias, length, first_row):
    rows = lax.broadcasted_iota(jnp.int32, bias.shape, 0) + first_row
    keys = lax.broadcasted_iota(jnp.int32, bias.shape, 1)
    bias[...] = jnp.where((keys <= rows) & (keys < length), 0.0, masked_score)


def front_steps(z, length, wq_p, wkv_p, wo_p, tok, routes, cos, sin, outs, n_held, bias):
    n_out, n1_out, q_out, kv_out, lse_out, ho_out, r_out, gate_out, wq, wkv, wo, small_out = outs
    width = KV_HEADS * HEAD_DIM
    unpack_into(wkv, wkv_p)

    def small_chunk(i, carry):
        x = wo_p[pl.ds(i * 16, 16), :, 512:].astype(f32)
        rows = pl.ds(pl.multiple_of(i * 128, 128), 128)
        small_out[rows, :] = x[:, :8].reshape(128, 128).astype(bf16)
        return carry

    lax.fori_loop(0, 8, small_chunk, 0)
    gains = gain_rows(small_out[...])
    yield
    for b in range(4):
        x = tok[b].astype(f32)
        n1 = (x * rms_scale(x) * gains[0:1]).astype(bf16)
        rows = pl.ds(b * TOK, TOK)
        n1_out[rows, :] = n1
        kv = matmul(n1, wkv[...], (1, 0))
        kv_out[rows, :width] = turned_rows(
            kv[:, :width], cos[rows, :], sin[rows, :], False
        ).astype(bf16)
        kv_out[rows, width:] = kv[:, width:].astype(bf16)
        yield
    unpack_into(wq, wq_p)
    own = pl.ds(pl.multiple_of(z * TOK, TOK), TOK)
    q = matmul(n1_out[own, :], wq[...], (1, 0))
    q = turned_rows(q, cos[own, :], sin[own, :], False).astype(bf16)
    q_out[...] = q * jnp.asarray(HEAD_DIM ** (-0.5), bf16)
    lse_out[...] = jnp.zeros_like(lse_out)
    fill_bias(bias, length[0], z * TOK)
    lane = lax.broadcasted_iota(jnp.int32, (TOK, 128), 1)
    yield

    def heads(j):
        keys = kv_out[:, pl.ds(j * 128, 128)]
        values = kv_out[:, pl.ds(width + j * 128, 128)]
        for g in (0, 1):
            span = pl.ds(j * 256 + g * 128, 128)
            qs = q_out[:, span]
            key = keys[:, g * HEAD_DIM : (g + 1) * HEAD_DIM]
            value = values[:, g * HEAD_DIM : (g + 1) * HEAD_DIM]
            mixed = []
            for h in (0, 1):
                s = matmul(qs[:, h * HEAD_DIM : (h + 1) * HEAD_DIM], key, (1, 1)) + bias[...]
                top = jnp.max(s, axis=1, keepdims=True)
                p = jnp.exp(s - top)
                total = jnp.sum(p, axis=1, keepdims=True)
                p = (p * (1.0 / total)).astype(bf16)
                mixed.append(matmul(p, value, (1, 0)))
                head = j * 4 + g * 2 + h
                lse_out[...] = jnp.where(lane == head, top + jnp.log(total), lse_out[...])
            ho_out[:, span] = jnp.concatenate(mixed, axis=1).astype(bf16)

    for j in range(4):
        heads(j)
        yield
    unpack_into(wo, wo_p)
    r = tok[z].astype(f32) + matmul(ho_out[...], wo[...], (1, 0))
    r_out[...] = r
    n2 = (r * rms_scale(r) * gains[1:2]).astype(bf16)
    n_out[:, :D] = n2
    n_held[:, :D] = n2
    logits = matmul(n2, small_out[...], (1, 0))
    hits = lane == routes[:, 0:1]
    for k in range(1, routes.shape[1]):
        hits = hits | (lane == routes[:, k : k + 1])
    lifted = jnp.where(hits, logits, masked_score)
    lifted = jnp.where(hits, jnp.exp(lifted - jnp.max(lifted, axis=1, keepdims=True)), 0.0)
    gate = lifted / jnp.sum(lifted, axis=1, keepdims=True)
    gate_out[...] = gate
    row = lax.broadcasted_iota(jnp.int32, (TOK, TOK), 0)
    col = lax.broadcasted_iota(jnp.int32, (TOK, TOK), 1)
    earlier = jnp.where(col < row, 1.0, 0.0).astype(bf16)
    ranks = matmul(earlier, jnp.where(hits, 1.0, 0.0).astype(bf16), (1, 0))
    high = gate.astype(bf16).astype(f32)
    meta = jnp.where(hits, ranks, jnp.where(lane < EXPERTS, -1.0, 0.0))
    meta = meta + pltpu.roll(high, EXPERTS, 1) + pltpu.roll(gate - high, 2 * EXPERTS, 1)
    meta = meta.astype(bf16)
    n_out[:, D:] = meta
    n_held[:, D:] = meta


GATHER_ORDERS = ("zyx", "yzx", "zyx")
FRONT_SCHEDULE = "wtwwtwdtwwt" + "fd" * 6 + "f" * 12


def front_kernel(
    length, w_kv, w_q, w_o, tok, dout, routes, cos, sin,
    n_out, n1_out, q_out, kv_out, lse_out, ho_out, r_out, gate_out, wq, wkv, wo, small_out,
    tok_out, dout_out, n_all,
    wkv_p, wq_p, wo_p, tok_held, dout_held, n_held, bias, *sems,
):
    at = place()
    wires = Wires(*sems)
    own_tok = wires.keep(tok, tok_held.at[at["z"]])
    own_dout = wires.keep(dout, dout_held.at[at["x"], at["c"]])
    weights = weight_steps(
        wires, at, list(zip((w_kv, w_q, w_o), (wkv_p, wq_p, wo_p), GATHER_ORDERS))
    )
    tokens = token_steps(wires, at, tok_held)
    flat = [p.reshape(128, *p.shape[-2:]) for p in (wq_p, wkv_p, wo_p)]
    outs = (
        n_out, n1_out, q_out, kv_out, lse_out, ho_out, r_out, gate_out, wq, wkv, wo, small_out
    )

    def forward():
        for _ in weights:
            pass
        for _ in tokens:
            pass
        kept = wires.keep(tok_held, tok_out)
        yield from front_steps(
            at["z"], length, *flat, tok_held, routes, cos, sin, outs,
            n_held.at[at["x"], at["c"]], bias,
        )
        kept.wait()

    greet(at, "xyzc")
    own_tok.wait()
    own_dout.wait()
    in_order(
        FRONT_SCHEDULE,
        w=weights,
        t=tokens,
        d=row_steps(wires, at, dout_held, dout_out),
        f=forward(),
    )
    in_order("", n=row_steps(wires, at, n_held, n_all))
    wires.finish()


def front(length, w_q, w_kv, w_o, tok, dout, routes, cos, sin):
    vmem = pl.BlockSpec(memory_space=pltpu.VMEM)
    far = pl.BlockSpec(memory_space=pltpu.HBM)
    square = jax.ShapeDtypeStruct((D, D), bf16)
    rows = jax.ShapeDtypeStruct((TOK, D), bf16)
    lanes = jax.ShapeDtypeStruct((TOK, 128), f32)
    lead = (4, 4, 2, 4)
    copies = WEIGHT_COPIES + TOKEN_COPIES + 2 * ROW_COPIES
    return pl.pallas_call(
        front_kernel,
        out_shape=[
            jax.ShapeDtypeStruct((TOK, D + 128), bf16),
            square,
            rows,
            square,
            lanes,
            rows,
            jax.ShapeDtypeStruct((TOK, D), f32),
            lanes,
            square,
            square,
            square,
            jax.ShapeDtypeStruct((D, 128), bf16),
            pltpu.HBM((4, TOK, D), bf16),
            pltpu.HBM((4, 2, TOK, D), bf16),
            pltpu.HBM((4, 2, TOK, D + 128), bf16),
        ],
        in_specs=[pl.BlockSpec(memory_space=pltpu.SMEM)] + [far] * 5 + [vmem] * 3,
        out_specs=[vmem] * 12 + [far] * 3,
        scratch_shapes=[
            pltpu.VMEM(lead + w_kv.shape, bf16),
            pltpu.VMEM(lead + w_q.shape, bf16),
            pltpu.VMEM(lead + w_o.shape, bf16),
            pltpu.VMEM((4, TOK, D), bf16),
            pltpu.VMEM((4, 2, TOK, D), bf16),
            pltpu.VMEM((4, 2, TOK, D + 128), bf16),
            pltpu.VMEM((TOK, 4 * TOK), f32),
        ]
        + wire_sems(copies, 2 + 3 + 1 + 2 * ROW_KEPT),
        compiler_params=pltpu.CompilerParams(
            collective_id=1, has_side_effects=True, vmem_limit_bytes=60 * 1024 * 1024
        ),
        cost_estimate=pl.CostEstimate(
            flops=10**10, bytes_accessed=30_000_000, transcendentals=5_000_000
        ),
        name="front",
    )(length, *hbm(w_kv, w_q, w_o, tok, dout), routes, cos, sin)


def rms_back(values, scale, gain, dnormed):
    scaled = values * scale
    dscaled = dnormed * gain
    dvalues = scale * (dscaled - scaled * jnp.mean(dscaled * scaled, axis=-1, keepdims=True))
    return dvalues, jnp.sum(dnormed * scaled, axis=0, keepdims=True)


def pack_into(out, value):
    def chunk(i, carry):
        rows = pl.ds(pl.multiple_of(i * 128, 128), 128)
        left = value[rows, :512].reshape(16, 8, 512)
        right = value[rows, 512:].reshape(16, 8, 512)
        out[pl.ds(i * 16, 16), :, :512] = jnp.concatenate([left, right], axis=1).astype(bf16)
        return carry

    lax.fori_loop(0, 8, chunk, 0)


def back_kernel(
    length, sums, dout, n_ext, r_ref, gate_ref, ho, q_ref, kv, lse, n1, tok, wq, wkv, wo, small,
    cos, sin, cos_t, sin_t,
    dwq_p, dwkv_p, dwo_p, dn1_out, dr_out,
    bias, square, dkv_t, dq_s, do_s, dkv_s,
):
    z = lax.axis_index("z")
    own = pl.ds(pl.multiple_of(z * TOK, TOK), TOK)
    gains = gain_rows(small[...])
    lane = lax.broadcasted_iota(jnp.int32, (TOK, 128), 1)
    gate = gate_ref[...]
    fields = sums[:, D:]
    dgate = fields + pltpu.roll(fields, 128 - EXPERTS, 1)
    mean = jnp.sum(gate * dgate, axis=1, keepdims=True)
    dlogits = (gate * (dgate - mean)).astype(bf16)
    dn2 = sums[:, :D] + matmul(dlogits, small[...], (1, 1))
    d_router = matmul(n_ext[:, :D], dlogits, (0, 0))
    r = r_ref[...]
    dr, dg2 = rms_back(r, rms_scale(r), gains[1:2], dn2)
    dr = dr + dout[...].astype(f32)
    dr_out[...] = dr
    d_att = dr.astype(bf16)
    square[...] = matmul(ho[...], d_att, (0, 0))
    pack_into(dwo_p, square)
    do_s[...] = matmul(d_att, wo[...], (1, 1)).astype(bf16)
    fill_bias(bias, length[0], z * TOK)
    width = KV_HEADS * HEAD_DIM
    scale = HEAD_DIM ** (-0.5)

    def heads(j, carry):
        keys = kv[:, pl.ds(pl.multiple_of(j * 128, 128), 128)]
        values = kv[:, pl.ds(pl.multiple_of(width + j * 128, 128), 128)]
        for g in (0, 1):
            span = pl.ds(pl.multiple_of(j * 256 + g * 128, 128), 128)
            qs, dos = q_ref[:, span], do_s[:, span]
            prods = dos.astype(f32) * ho[:, span].astype(f32)
            key = keys[:, g * HEAD_DIM : (g + 1) * HEAD_DIM]
            value = values[:, g * HEAD_DIM : (g + 1) * HEAD_DIM]
            dqs = []
            dk_t, dv_t = 0.0, 0.0
            for h in (0, 1):
                part = slice(h * HEAD_DIM, (h + 1) * HEAD_DIM)
                head = j * 4 + g * 2 + h
                shift_by = jnp.sum(jnp.where(lane == head, lse[...], 0.0), axis=1, keepdims=True)
                mine = (lane >= h * HEAD_DIM) & (lane < (h + 1) * HEAD_DIM)
                delta = jnp.sum(jnp.where(mine, prods, 0.0), axis=1, keepdims=True)
                p = jnp.exp(matmul(qs[:, part], key, (1, 1)) + bias[...] - shift_by)
                dp = matmul(dos[:, part], value, (1, 1))
                ds = (p * (dp - delta)).astype(bf16)
                dqs.append(matmul(ds, key, (1, 0)) * scale)
                dk_t = dk_t + matmul(qs[:, part], ds, (0, 0))
                dv_t = dv_t + matmul(dos[:, part], p.astype(bf16), (0, 0))
            dq_s[:, span] = jnp.concatenate(dqs, axis=1)
            half = HEAD_DIM // 2
            wave = dk_t * sin_t[...]
            dk_t = dk_t * cos_t[...] + jnp.concatenate([wave[half:], -wave[:half]], axis=0)
            at = j * 128 + g * HEAD_DIM
            dkv_t[pl.ds(pl.multiple_of(at, HEAD_DIM), HEAD_DIM), :] = dk_t
            dkv_t[pl.ds(pl.multiple_of(width + at, HEAD_DIM), HEAD_DIM), :] = dv_t
        return carry

    lax.fori_loop(0, 4, heads, 0)

    def flip(i, carry):
        at = pl.ds(pl.multiple_of(i * 128, 128), 128)
        dkv_s[:, at] = jnp.transpose(dkv_t[at, :]).astype(bf16)
        return carry

    lax.fori_loop(0, 8, flip, 0)
    dq = turned_rows(dq_s[...], cos[own, :], sin[own, :], True).astype(bf16)
    square[...] = matmul(n1[own, :], dq, (0, 0))
    pack_into(dwq_p, square)
    square[...] = matmul(n1[...], dkv_s[...], (0, 0))
    pack_into(dwkv_p, square)
    square[...] = matmul(dkv_s[...], wkv[...], (1, 1))
    square[own, :] += matmul(dq, wq[...], (1, 1))
    dg1 = jnp.zeros((1, D), f32)
    for b in range(4):
        rows = slice(b * TOK, (b + 1) * TOK)
        x = tok[b].astype(f32)
        dn1 = square[rows, :]
        dg1 = dg1 + jnp.sum(dn1 * (x * rms_scale(x)), axis=0, keepdims=True)
        dn1_out[b] = dn1.astype(bf16)
    sub = lax.broadcasted_iota(jnp.int32, (8, D), 0)
    dgs = jnp.where(sub == 0, dg1, jnp.where(sub == 1, dg2, 0.0))
    high = dgs.astype(bf16)
    low = (dgs - high.astype(f32)).astype(bf16)
    place_lane = lax.broadcasted_iota(jnp.int32, (8, 128), 1)
    place_sub = lax.broadcasted_iota(jnp.int32, (8, 128), 0)
    spread = (place_lane == EXPERTS + place_sub).astype(f32).astype(bf16)
    d_small = d_router + matmul(high, spread, (0, 0)) + matmul(low, spread, (0, 0))
    d_small = d_small.reshape(128, 8, 128)
    dwo_p[:, :, 512:] = jnp.concatenate([d_small, jnp.zeros_like(d_small)], axis=1).astype(bf16)


def back(*args):
    vmem = pl.BlockSpec(memory_space=pltpu.VMEM)
    return pl.pallas_call(
        back_kernel,
        out_shape=[
            jax.ShapeDtypeStruct((128, 16, 512), bf16),
            jax.ShapeDtypeStruct((128, 16, 512), bf16),
            jax.ShapeDtypeStruct((128, 16, 640), bf16),
            jax.ShapeDtypeStruct((4, TOK, D), bf16),
            jax.ShapeDtypeStruct((TOK, D), f32),
        ],
        in_specs=[pl.BlockSpec(memory_space=pltpu.SMEM)] + [vmem] * 19,
        out_specs=[vmem] * 5,
        scratch_shapes=[
            pltpu.VMEM((TOK, 4 * TOK), f32),
            pltpu.VMEM((D, D), f32),
            pltpu.VMEM((D, D), f32),
            pltpu.VMEM((TOK, D), f32),
            pltpu.VMEM((TOK, D), bf16),
            pltpu.VMEM((D, D), bf16),
        ],
        compiler_params=pltpu.CompilerParams(vmem_limit_bytes=60 * 1024 * 1024),
        cost_estimate=pl.CostEstimate(
            flops=2 * 10**10, bytes_accessed=40_000_000, transcendentals=5_000_000
        ),
        name="back",
    )(*args)


def pack_matrix(shard):
    half = shard.shape[1] // 2
    return jnp.concatenate([shard[:, :half], shard[:, half:]], axis=0)


def unpack_matrix(packed):
    return jnp.concatenate([packed[:8], packed[8:]], axis=1)


def body(
    tokens, routes, lengths, out_grad,
    query_weight, query_mean, query_square,
    keyval_weight, keyval_mean, keyval_square,
    output_weight, output_mean, output_square,
    router_weight, router_mean, router_square,
    norm_gains, gains_mean, gains_square,
    gateup_weight, gateup_mean, gateup_square,
    down_weight, down_mean, down_square,
):
    row_count = tokens.shape[0]
    seq_len = row_count * 4
    query_width = HEADS * HEAD_DIM

    small = jnp.concatenate(
        [router_weight, norm_gains.T, jnp.zeros((8, 128 - EXPERTS - 2), f32)], axis=1
    )
    small = jnp.concatenate([small, jnp.zeros((8, 128), f32)], axis=0)
    expert_b = lax.all_gather(
        jnp.concatenate([gateup_weight[0], down_weight[0]], axis=0).astype(bf16),
        ("y", "z"),
        axis=0,
    )
    cos, sin = rotary_tables(jnp.arange(seq_len, dtype=jnp.int32), HEAD_DIM // 2)
    cos2, sin2 = jnp.tile(cos, (1, 2)), jnp.tile(sin, (1, 2))
    (
        n_ext, n1, q, kv, lse, ho, residual, gate, query_b, keyval_b, output_b, small_b,
        all_tokens, dout_all, n_all,
    ) = front(
        lengths,
        pack_matrix(query_weight).astype(bf16),
        pack_matrix(keyval_weight).astype(bf16),
        jnp.concatenate([pack_matrix(output_weight), small], axis=1).astype(bf16),
        tokens,
        out_grad,
        routes,
        cos2,
        sin2,
    )
    wide = n_all.shape[-1]
    dn_parts, out_parts, d_expert = experts(
        n_all.reshape(SOURCES, row_count, wide),
        dout_all.reshape(SOURCES, row_count, D),
        expert_b.reshape((4,) + (4, D // 4 + FF_E // 4, D)),
    )
    grad_expert = lax.psum_scatter(
        d_expert.reshape((16,) + d_expert.shape[2:]),
        ("y", "z"),
        scatter_dimension=0,
        tiled=False,
    ).astype(f32)
    sums = sum_rows(dn_parts.reshape(4, 2, row_count, wide))
    d_query, d_keyval, d_last, dn1, dresidual = back(
        lengths, sums, out_grad, n_ext, residual, gate, ho, q, kv, lse, n1, all_tokens,
        query_b, keyval_b, output_b, small_b, cos2, sin2, cos.T, sin.T,
    )
    g_query, g_keyval, g_last, dn1_sum, mixed_out = sum_back(
        (
            d_query.reshape(4, 4, 2, 4, 16, 512),
            d_keyval.reshape(4, 4, 2, 4, 16, 512),
            d_last.reshape(4, 4, 2, 4, 16, 640),
        ),
        dn1,
        out_parts.reshape(4, 2, row_count, D),
    )
    layer_out = (residual + mixed_out).astype(bf16)
    grad_query, grad_keyval, grad_output = (
        unpack_matrix(g) for g in (g_query, g_keyval, g_last[:, :512])
    )
    grad_router = g_last[:8, 512 : 512 + EXPERTS]
    grad_gains = g_last[:8, 512 + EXPERTS : 512 + EXPERTS + 2].T
    inputs = tokens.astype(f32)
    gain_one = small_b[:, EXPERTS].astype(f32)
    dnorm_one, _ = norm_back(inputs, rms_scale(inputs), gain_one, dn1_sum)
    tokens_grad = dresidual + dnorm_one

    rate = 0.5
    query_new = adamw(query_weight, grad_query, query_mean, query_square, rate * D ** (-0.5), 0.1)
    keyval_new = adamw(
        keyval_weight, grad_keyval, keyval_mean, keyval_square, rate * D ** (-0.5), 0.1
    )
    output_new = adamw(
        output_weight,
        grad_output,
        output_mean,
        output_square,
        rate * max(1, 2 * query_width // seq_len) ** (-0.5),
        0.1,
    )
    router_new = adamw(
        router_weight, grad_router, router_mean, router_square, rate * (4 * D) ** (-0.5), 0.1
    )
    gains_new = adamw(norm_gains, grad_gains, gains_mean, gains_square, 0.6, 0.0)
    gateup_new = adamw(
        gateup_weight,
        grad_expert[None, : D // 4],
        gateup_mean,
        gateup_square,
        rate * D ** (-0.5),
        0.1,
    )
    down_new = adamw(
        down_weight,
        grad_expert[None, D // 4 :],
        down_mean,
        down_square,
        rate * (FF_E // 8) ** (-0.5),
        0.1,
    )
    return (
        (layer_out, tokens_grad)
        + query_new
        + keyval_new
        + output_new
        + router_new
        + gains_new
        + gateup_new
        + down_new
    )


def solution(mesh):
    devices = jax.sharding.Mesh(mesh.devices.reshape(4, 4, 2, 4), ("x", "y", "c", "z"))
    every = ("x", "y", "c", "z")
    rows = P(every, None)
    gains = P(None, every)
    shard = P(("x", "y", "c"), "z", None)
    return jax.shard_map(
        body,
        mesh=devices,
        in_specs=(rows, rows, P(("x", "y", "c")), rows)
        + (rows,) * 12
        + (gains,) * 3
        + (shard,) * 6,
        out_specs=(rows, rows) + (rows,) * 12 + (gains,) * 3 + (shard,) * 6,
        check_vma=False,
    )
```

```python
import jax
import jax.numpy as jnp
import numpy as np
from jax import lax
from jax.experimental import pallas as pl
from jax.experimental.pallas import tpu as pltpu
from jax.sharding import PartitionSpec as P

MESH = pl.DeviceIdType.MESH
bf16 = jnp.bfloat16
f32 = jnp.float32
AXES = "xycz"
STRIP = 16


def place():
    return {a: lax.axis_index(a) for a in AXES}


def device(at):
    return tuple(at[a] for a in AXES)


def shift(at, axis, by):
    size = 2 if axis == "c" else 4
    return lax.rem(at[axis] + by, size)


def peer(at, axis, by):
    return device({**at, axis: shift(at, axis, by)})


def greet(at, axes):
    barrier = pltpu.get_barrier_semaphore()
    count = 0
    for axis in axes:
        for by in (1,) if axis == "c" else (1, 2, 3):
            pl.semaphore_signal(
                barrier, inc=1, device_id=peer(at, axis, by), device_id_type=MESH
            )
            count += 1
    pl.semaphore_wait(barrier, count)


class Wires:
    def __init__(self, send_sems, recv_sems, local_sems):
        self.send_sems, self.recv_sems, self.local_sems = send_sems, recv_sems, local_sems
        self.copies, self.sent, self.local = [], 0, 0

    def send(self, src, dst, target):
        at = self.sent
        self.sent += 1
        copy = pltpu.make_async_remote_copy(
            src_ref=src,
            dst_ref=dst,
            send_sem=self.send_sems.at[at],
            recv_sem=self.recv_sems.at[at],
            device_id=target,
            device_id_type=MESH,
        )
        copy.start()
        self.copies.append(copy)
        return copy

    def keep(self, src, dst):
        copy = pltpu.make_async_copy(src, dst, self.local_sems.at[self.local])
        copy.start()
        self.local += 1
        return copy

    def finish(self):
        for copy in self.copies:
            copy.wait_send()
        self.copies = []


def wire_sems(copies, kept):
    return [
        pltpu.SemaphoreType.DMA((copies,)),
        pltpu.SemaphoreType.DMA((copies,)),
        pltpu.SemaphoreType.DMA((kept,)),
    ]


def in_order(order, **steps):
    for letter in order:
        next(steps[letter], None)
    for step in steps.values():
        for _ in step:
            pass


def hbm(*arrays):
    return [pltpu.with_memory_space_constraint(v, pltpu.HBM) for v in arrays]


def ring_steps(wires, at, axis, spot, hand_on):
    right, left = peer(at, axis, 1), peer(at, axis, 3)
    to_right = {k: wires.send(spot(0, k), spot(0, k), right) for k in (0, 1)}
    to_left = {k: wires.send(spot(0, k), spot(0, k), left) for k in (1, 0)}
    for k in (0, 1):
        hand_on(0, k)
    yield
    to_right[0].wait_recv()
    far_right = wires.send(spot(3, 0), spot(3, 0), right)
    hand_on(3, 0)
    to_left[1].wait_recv()
    far_left = wires.send(spot(1, 1), spot(1, 1), left)
    hand_on(1, 1)
    yield
    to_right[1].wait_recv()
    hand_on(3, 1)
    to_left[0].wait_recv()
    hand_on(1, 0)
    yield
    far_right.wait_recv()
    hand_on(2, 0)
    far_left.wait_recv()
    hand_on(2, 1)


def row_steps(wires, at, held, out):
    half = held.shape[2] // 2
    sibling = peer(at, "c", 1)
    other = shift(at, "c", 1)
    across, kept = [], []

    def hand_on(by, part):
        rows = pl.ds(part * half, half)
        unit, theirs = (
            (shift(at, "x", by), c, rows) for c in (at["c"], other)
        )
        across.append((theirs, wires.send(held.at[unit], held.at[unit], sibling)))
        kept.append(wires.keep(held.at[unit], out.at[unit]))

    def spot(by, part):
        return held.at[shift(at, "x", by), at["c"], pl.ds(part * half, half)]

    yield from ring_steps(wires, at, "x", spot, hand_on)
    yield
    for unit, copy in across:
        copy.wait_recv()
        kept.append(wires.keep(held.at[unit], out.at[unit]))
    for copy in kept:
        copy.wait()


ROW_KEPT = 16
ROW_COPIES = 6 + 8


def token_steps(wires, at, held):
    half = held.shape[1] // 2

    def spot(by, part):
        return held.at[shift(at, "z", by), pl.ds(part * half, half)]

    yield from ring_steps(wires, at, "z", spot, lambda by, part: None)


TOKEN_COPIES = 6


def index(at, whole, **fixed):
    spots = {**at, **{a: slice(None) for a in whole}, **fixed}
    return tuple(spots[axis] for axis in AXES)


def weight_steps(wires, at, parts):
    arrivals = {}
    for p, (o, order) in enumerate(parts):
        own = o.at[index(at, "")]
        for by in (1, 3, 2):
            arrivals[p, by] = wires.send(own, own, peer(at, order[0], by))
    yield
    later = {}
    for p, (o, order) in enumerate(parts):
        for by in (1, 3, 2):
            arrivals[p, by].wait_recv()
        spot = index(at, order[0])
        for by in (1, 3, 2):
            later[p, by] = wires.send(o.at[spot], o.at[spot], peer(at, order[1], by))
    yield
    sibling = peer(at, "c", 1)
    across, rings = [], []
    for p, (o, order) in enumerate(parts):
        for by in (1, 3, 2):
            later[p, by].wait_recv()

        def spot(by, part, o=o, order=order):
            pieces = {order[1]: pl.ds(2 * part, 2), order[2]: shift(at, order[2], by)}
            return o.at[index(at, order[0], **pieces)]

        def hand_on(by, part, spot=spot):
            across.append(wires.send(spot(by, part), spot(by, part), sibling))

        ring = ring_steps(wires, at, order[2], spot, hand_on)
        next(ring)
        rings.append(ring)
    yield
    for _ in range(3):
        for ring in rings:
            next(ring, None)
        yield
    for copy in across:
        copy.wait_recv()


WEIGHT_COPIES = 3 * (3 + 3 + 6 + 8)


def add_rows(out, parts, rows):
    def strip(i, carry):
        span = pl.ds(pl.multiple_of(i * STRIP, STRIP), STRIP)
        total = parts[0][span].astype(f32)
        for part in parts[1:]:
            total = total + part[span].astype(f32)
        out[span] = total.astype(out.dtype)
        return carry

    lax.fori_loop(0, rows // STRIP, strip, 0)


def ring_sum_steps(wires, at, axis, blocks, out, mid, last, near):
    half = out.shape[0] // 2
    low, high = pl.ds(0, half), pl.ds(half, half)
    ahead, back, far = (blocks.at[shift(at, axis, by)] for by in (1, 3, 2))
    right, left = peer(at, axis, 1), peer(at, axis, 3)
    near_l = wires.send(far.at[low], near.at[0], right)
    near_r = wires.send(far.at[high], near.at[1], left)
    pure_l = wires.send(ahead.at[high], last.at[0, high], right)
    pure_r = wires.send(back.at[low], last.at[1, low], left)
    yield
    near_l.wait_recv()
    add_rows(mid.at[0], [ahead.at[low], near.at[0]], half)
    sum_l = wires.send(mid.at[0], last.at[0, low], right)
    near_r.wait_recv()
    add_rows(mid.at[1], [back.at[high], near.at[1]], half)
    sum_r = wires.send(mid.at[1], last.at[1, high], left)
    yield
    for copy in (pure_l, sum_l, pure_r, sum_r):
        copy.wait_recv()
    add_rows(out, [blocks.at[at[axis]], last.at[0], last.at[1]], 2 * half)


def ring_sum_scratch(rows, width):
    return [
        pltpu.VMEM((2, rows // 2, width), bf16),
        pltpu.VMEM((2, rows, width), bf16),
        pltpu.VMEM((2, rows // 2, width), bf16),
    ]


def row_sum_steps(wires, at, c_ref, out, held, crossed, mid, last, near):
    other = shift(at, "c", 1)
    sibling = peer(at, "c", 1)
    rows = out.shape[0]
    crossing, kept = {}, {}
    for by in (2, 1, 3, 0):
        i = shift(at, "x", by)
        crossing[by] = wires.send(c_ref.at[i, other], crossed.at[i], sibling)
        kept[by] = wires.keep(c_ref.at[i, at["c"]], held.at[i])
    yield
    for by in (2, 1, 3, 0):
        i = shift(at, "x", by)
        kept[by].wait()
        crossing[by].wait_recv()
        add_rows(held.at[i], [held.at[i], crossed.at[i]], rows)
        if by == 3:
            ring = ring_sum_steps(wires, at, "x", held, out, mid, last, near)
            next(ring)
    yield
    yield from ring


ROW_SUM_COPIES = 4 + 6


def row_sum_scratch(rows, width):
    return [pltpu.VMEM((4, rows, width), bf16)] * 2 + ring_sum_scratch(rows, width)


def matrix_steps(wires, at, order, pack, out, crossed, one, two, three, sum1, sum2):
    axis, after, end = order
    crossing = wires.send(
        pack.at[:, :, shift(at, "c", 1)], crossed, peer(at, "c", 1)
    )

    def own(by):
        return pack.at[index(at, "xyz", **{axis: shift(at, axis, by)})]

    def later(by):
        rest = "xyz".replace(axis, "")
        return sum1.at[tuple(shift(at, a, by) if a == after else slice(None) for a in rest)]

    def total(out, parts, count):
        def body(i, carry):
            value = parts[0][i].astype(f32)
            for part in parts[1:]:
                value = value + part[i].astype(f32)
            out[i] = value.astype(out.dtype)
            return carry

        lax.fori_loop(0, count, body, 0)

    def spread(parts, slots, along):
        return [wires.send(parts(by), slots.at[by - 1], peer(at, along, by)) for by in (2, 1, 3)]

    yield
    crossing.wait_recv()

    def body(i, carry):
        spot = (i // 4, i % 4)
        mine = pack[spot + (at["c"],)].astype(f32) + crossed[spot].astype(f32)
        pack[spot + (at["c"],)] = mine.astype(bf16)
        return carry

    lax.fori_loop(0, 16, body, 0)
    copies = spread(own, one, axis)
    yield
    for copy in copies:
        copy.wait_recv()
    total(sum1, [own(0)] + [one.at[k] for k in range(3)], 4)
    copies = spread(later, two, after)
    yield
    for copy in copies:
        copy.wait_recv()
    total(sum2, [later(0)] + [two.at[k] for k in range(3)], 4)
    copies = spread(lambda by: sum2.at[shift(at, end, by)], three, end)
    yield
    for copy in copies:
        copy.wait_recv()
    value = sum2[at[end]].astype(f32)
    for k in range(3):
        value = value + three[k].astype(f32)
    out[...] = value


MATRIX_COPIES = 10
RING_SUM_COPIES = 6


def matrix_scratch(width):
    leads = ((4, 4, 2, 4), (4, 4, 4), (3, 4, 4), (3, 4), (3,), (4, 4), (4,))
    return [pltpu.VMEM(lead + (16, width), bf16) for lead in leads]


D = 1024
HEADS = 16
KV_HEADS = 8
HEAD_DIM = 64
EXPERTS = 32
FF_E = 512
STEP = 10
CAP = 96
TOK = 256


norm_epsilon = 1e-06
beta_first = 0.9
beta_second = 0.95
adam_epsilon = 1e-08
masked_score = -1e30


def rotary_tables(positions, half_width):
    freqs = 10000.0 ** (-jnp.arange(half_width, dtype=jnp.float32) / half_width)
    angles = positions.astype(jnp.float32)[:, None] * freqs[None, :]
    cosines = jnp.cos(angles)
    sines = jnp.sin(angles)
    return (jnp.concatenate([cosines, cosines], 1), jnp.concatenate([sines, sines], 1))


def rotate(values, cosines, sines):
    half_width = values.shape[-1] // 2
    turned = jnp.concatenate([-values[..., half_width:], values[..., :half_width]], -1)
    return values * cosines[:, None, :] + turned * sines[:, None, :]


def rotate_back(grads, cosines, sines):
    half_width = grads.shape[-1] // 2
    scaled = grads * sines[:, None, :]
    return grads * cosines[:, None, :] + jnp.concatenate(
        [scaled[..., half_width:], -scaled[..., :half_width]], -1
    )


def rms_scale(values):
    return lax.rsqrt(jnp.mean(values * values, axis=-1, keepdims=True) + norm_epsilon)


def norm_back(values, scale, gain, dnormed):
    scaled = values * scale
    dgain = jnp.sum(dnormed * scaled, axis=0)
    dscaled = dnormed * gain
    dvalues = scale * (dscaled - scaled * jnp.mean(dscaled * scaled, axis=-1, keepdims=True))
    return (dvalues, dgain)


def masked_scores(grouped, whole_kv, positions, length):
    key_count = whole_kv.shape[0]
    key_width = whole_kv.shape[1] // 2
    heads_kv = grouped.shape[1]
    head_size = grouped.shape[3]
    all_keys = whole_kv[:, :key_width].reshape(key_count, heads_kv, head_size)
    all_values = whole_kv[:, key_width:].reshape(key_count, heads_kv, head_size)
    raw_scores = jnp.einsum(
        "qkgd,pkd->kgqp", grouped, all_keys, preferred_element_type=jnp.float32
    ) * head_size ** (-0.5)
    key_pos = jnp.arange(key_count, dtype=jnp.int32)
    allowed = (key_pos[None, :] <= positions[:, None]) & (key_pos[None, :] < length)
    return (jnp.where(allowed, raw_scores, masked_score), all_keys, all_values)


def adamw(weight, grad, first, second, rate, decay):
    first_new = beta_first * first + (1.0 - beta_first) * grad
    second_new = beta_second * second + (1.0 - beta_second) * grad * grad
    update = (
        first_new
        / (1.0 - beta_first**STEP)
        / (jnp.sqrt(second_new / (1.0 - beta_second**STEP)) + adam_epsilon)
    )
    return (weight - rate * (update + decay * weight), first_new, second_new)


SOURCES = 8
HOSTED = 4
SLOTS = SOURCES * CAP
OUT_BLOCKS = 2


def matmul(a, b, contract):
    return lax.dot_general(
        a, b, (((contract[0],), (contract[1],)), ((), ())), preferred_element_type=f32
    )


def expert_kernel(n_ref, g_ref, w_ref, dn_ref, out_ref, dw_ref, xs, ds, zs, gates):
    step = pl.program_id(0)
    base = lax.axis_index("x") * 8 + lax.axis_index("c")

    @pl.when(step == 0)
    def _():
        lane = lax.broadcasted_iota(jnp.int32, (16, 128), 1)
        sub = lax.broadcasted_iota(jnp.int32, (16, 128), 0)
        wanted = base + 2 * lax.rem(sub, HOSTED) + EXPERTS * (sub // HOSTED)
        choose = jnp.where((lane == wanted) & (sub < 3 * HOSTED), 1.0, 0.0).astype(bf16)
        slot = lax.broadcasted_iota(jnp.int32, (CAP, TOK), 0).astype(f32)

        def source(b, carry):
            fields = matmul(choose, n_ref[b, :, D:], (1, 1))
            hots = []
            for j in range(HOSTED):
                hot = slot == fields[j : j + 1]
                gate = fields[HOSTED + j : HOSTED + j + 1] + fields[2 * HOSTED + j : 2 * HOSTED + j + 1]
                span = pl.ds(pl.multiple_of(j * SLOTS + b * CAP, CAP), CAP)
                gates[span, :] = jnp.broadcast_to(
                    jnp.sum(jnp.where(hot, gate, 0.0), axis=1, keepdims=True), (CAP, 128)
                )
                hots.append(jnp.where(hot, 1.0, 0.0).astype(bf16))
            hots = jnp.concatenate(hots, axis=0)
            x = matmul(hots, n_ref[b, :, :D], (1, 0)).astype(bf16)
            d = matmul(hots, g_ref[b], (1, 0)).astype(bf16)
            for j in range(HOSTED):
                span = pl.ds(pl.multiple_of(j * SLOTS + b * CAP, CAP), CAP)
                xs[span, :] = x[j * CAP : (j + 1) * CAP]
                ds[span, :] = d[j * CAP : (j + 1) * CAP]
            return carry

        lax.fori_loop(0, SOURCES, source, 0)

    @pl.when(step < HOSTED)
    def _():
        expert = base + 2 * step
        rows = pl.ds(pl.multiple_of(step * SLOTS, SLOTS), SLOTS)
        gate = gates[rows, :][:, :1]
        w_gu = w_ref[0, :, : D // 4, :].reshape(D, 2 * FF_E)
        w_d = w_ref[0, :, D // 4 :, :].reshape(FF_E, D)
        gu = matmul(xs[rows, :], w_gu, (1, 0))
        g_part, u_part = gu[:, :FF_E], gu[:, FF_E:]
        sig = 1.0 / (1.0 + jnp.exp(-g_part))
        act = g_part * sig
        hid = (act * u_part).astype(bf16)
        y = matmul(hid, w_d, (1, 0)).astype(bf16).astype(f32)
        dout = ds[rows, :].astype(f32)
        dgate = jnp.sum(y * dout, axis=1, keepdims=True)
        dy = (gate * dout).astype(bf16)
        ds[rows, :] = (gate * y).astype(bf16)
        dh = matmul(dy, w_d, (1, 1))
        da_g = dh * u_part * (sig * (1.0 + g_part * (1.0 - sig)))
        da = jnp.concatenate([da_g, dh * act], axis=1).astype(bf16)
        dw_ref[0, :, D // 4 :, :] = (
            matmul(hid, dy, (0, 0)).astype(bf16).reshape(4, FF_E // 4, D)
        )
        dw_ref[0, :, : D // 4, :] = (
            matmul(xs[rows, :], da, (0, 0)).astype(bf16).reshape(4, D // 4, 2 * FF_E)
        )
        xs[rows, :] = matmul(da, w_gu, (1, 1)).astype(bf16)
        lane = lax.broadcasted_iota(jnp.int32, (SLOTS, 128), 1)
        high = dgate.astype(bf16).astype(f32)
        fields = jnp.where(lane == expert + EXPERTS, dgate - high, 0.0)
        zs[rows, :] = jnp.where(lane == expert, high, fields).astype(bf16)

    @pl.when(step >= HOSTED)
    def _():
        slot = lax.broadcasted_iota(jnp.int32, (TOK, HOSTED * CAP), 1)
        lane = lax.broadcasted_iota(jnp.int32, (TOK, 128), 1)
        for i in range(OUT_BLOCKS):
            b = (step - HOSTED) * OUT_BLOCKS + i
            meta = n_ref[b, :, D:].astype(f32)
            target = jnp.full((TOK, HOSTED * CAP), -1.0, f32)
            for j in reversed(range(HOSTED)):
                mine = lane == base + 2 * j
                rank = jnp.sum(jnp.where(mine, meta, 0.0), axis=1, keepdims=True)
                rank = jnp.where(rank < 0.0, -1.0, rank + j * CAP)
                target = jnp.where(slot < (j + 1) * CAP, rank, target)
            spread = jnp.where(slot.astype(f32) == target, 1.0, 0.0).astype(bf16)
            spans = [pl.ds(pl.multiple_of(j * SLOTS + b * CAP, CAP), CAP) for j in range(HOSTED)]
            for ref, out in ((xs, dn_ref.at[i, :, :D]), (zs, dn_ref.at[i, :, D:]), (ds, out_ref.at[i])):
                rows = jnp.concatenate([ref[span, :] for span in spans], axis=0)
                out[...] = matmul(spread, rows, (1, 0)).astype(bf16)


def experts(n_all, g_all, weights):
    wide = n_all.shape[2]
    slots = HOSTED * SLOTS

    def block(width):
        return pl.BlockSpec(
            (OUT_BLOCKS, TOK, width), lambda i: (jnp.maximum(i - HOSTED, 0), 0, 0)
        )

    def fixed(shape):
        return pl.BlockSpec(shape, lambda i: (0, 0, 0), pipeline_mode=pl.Buffered(1))

    def one(shape):
        return pl.BlockSpec((1,) + shape[1:], lambda i: (jnp.minimum(i, HOSTED - 1), 0, 0, 0))

    return pl.pallas_call(
        expert_kernel,
        grid=(HOSTED + SOURCES // OUT_BLOCKS,),
        out_shape=[
            jax.ShapeDtypeStruct(n_all.shape, bf16),
            jax.ShapeDtypeStruct(g_all.shape, bf16),
            jax.ShapeDtypeStruct(weights.shape, bf16),
        ],
        in_specs=[fixed(n_all.shape), fixed(g_all.shape), one(weights.shape)],
        out_specs=[block(wide), block(D), one(weights.shape)],
        scratch_shapes=[
            pltpu.VMEM((slots, D), bf16),
            pltpu.VMEM((slots, D), bf16),
            pltpu.VMEM((slots, 128), bf16),
            pltpu.VMEM((slots, 128), f32),
        ],
        compiler_params=pltpu.CompilerParams(
            dimension_semantics=("arbitrary",), vmem_limit_bytes=62 * 1024 * 1024
        ),
        cost_estimate=pl.CostEstimate(
            flops=slots * D * FF_E * 18, bytes_accessed=45_000_000, transcendentals=0
        ),
        name="experts",
    )(n_all, g_all, weights)


def turned_rows(u, cos, sin, back):
    lane = lax.broadcasted_iota(jnp.int32, (1, 128), 1)
    first = lax.rem(lane, HEAD_DIM) < HEAD_DIM // 2
    pieces = []
    for j in range(u.shape[1] // 128):
        v = u[:, j * 128 : (j + 1) * 128]
        w = v * sin if back else v
        ahead = pltpu.roll(w, 128 - HEAD_DIM // 2, 1)
        behind = pltpu.roll(w, HEAD_DIM // 2, 1)
        if back:
            pieces.append(v * cos + jnp.where(first, ahead, -behind))
        else:
            pieces.append(v * cos + jnp.where(first, -ahead, behind) * sin)
    return jnp.concatenate(pieces, axis=1)


def unpack_into(out, packed):
    def chunk(i, carry):
        x = packed[pl.ds(i * 16, 16), :, :512].astype(f32)
        rows = pl.ds(pl.multiple_of(i * 128, 128), 128)
        out[rows, :512] = x[:, :8].reshape(128, 512).astype(bf16)
        out[rows, 512:] = x[:, 8:].reshape(128, 512).astype(bf16)
        return carry

    lax.fori_loop(0, 8, chunk, 0)


def gain_rows(small):
    lane = lax.broadcasted_iota(jnp.int32, (8, 128), 1)
    sub = lax.broadcasted_iota(jnp.int32, (8, 128), 0)
    choose = (lane == EXPERTS + sub).astype(f32).astype(bf16)
    return matmul(choose, small, (1, 1))


def fill_bias(bias, length, first_row):
    rows = lax.broadcasted_iota(jnp.int32, bias.shape, 0) + first_row
    keys = lax.broadcasted_iota(jnp.int32, bias.shape, 1)
    bias[...] = jnp.where((keys <= rows) & (keys < length), 0.0, masked_score)


def front_steps(
    z, length, need, wq_p, wkv_p, wo_p, tok, routes, cos, sin, outs, n_held, bias
):
    need, keep = need
    n_out, n1, q_out, kv_out, lse_out, ho_out, r_out, gate_out, wq, wkv, wo, small_out = outs
    width = KV_HEADS * HEAD_DIM
    need("k")
    unpack_into(wkv, wkv_p)

    def small_chunk(i, carry):
        x = wkv_p[pl.ds(i * 16, 16), :, 512:].astype(f32)
        rows = pl.ds(pl.multiple_of(i * 128, 128), 128)
        small_out[rows, :] = x[:, :8].reshape(128, 128).astype(bf16)
        return carry

    lax.fori_loop(0, 8, small_chunk, 0)
    keep("wkv")
    gains = gain_rows(small_out[...])

    def block(by):
        b = lax.rem(z + by, 4)
        x = tok[b].astype(f32)
        normed = (x * rms_scale(x) * gains[0:1]).astype(bf16)
        rows = pl.ds(pl.multiple_of(b * TOK, TOK), TOK)
        n1[rows, :] = normed
        kv = matmul(normed, wkv[...], (1, 0))
        kv_out[rows, :width] = turned_rows(
            kv[:, :width], cos[rows, :], sin[rows, :], False
        ).astype(bf16)
        kv_out[rows, width:] = kv[:, width:].astype(bf16)

    block(0)
    yield
    fill_bias(bias, length[0], z * TOK)
    need("q")
    unpack_into(wq, wq_p)
    keep("wq")
    own = pl.ds(pl.multiple_of(z * TOK, TOK), TOK)
    q = matmul(n1[own, :], wq[...], (1, 0))
    q = turned_rows(q, cos[own, :], sin[own, :], False).astype(bf16)
    q_out[...] = q * jnp.asarray(HEAD_DIM ** (-0.5), bf16)
    lse_out[...] = jnp.zeros_like(lse_out)
    lane = lax.broadcasted_iota(jnp.int32, (TOK, 128), 1)
    yield
    need("t")
    for by in (1, 3, 2):
        block(by)
        yield
    keep("n1")
    keep("kv")

    def heads(j):
        keys = kv_out[:, pl.ds(j * 128, 128)]
        values = kv_out[:, pl.ds(width + j * 128, 128)]
        for g in (0, 1):
            span = pl.ds(j * 256 + g * 128, 128)
            qs = q_out[:, span]
            key = keys[:, g * HEAD_DIM : (g + 1) * HEAD_DIM]
            value = values[:, g * HEAD_DIM : (g + 1) * HEAD_DIM]
            mixed = []
            for h in (0, 1):
                s = matmul(qs[:, h * HEAD_DIM : (h + 1) * HEAD_DIM], key, (1, 1)) + bias[...]
                top = jnp.max(s, axis=1, keepdims=True)
                p = jnp.exp(s - top)
                total = jnp.sum(p, axis=1, keepdims=True)
                p = (p * (1.0 / total)).astype(bf16)
                mixed.append(matmul(p, value, (1, 0)))
                head = j * 4 + g * 2 + h
                lse_out[...] = jnp.where(lane == head, top + jnp.log(total), lse_out[...])
            ho_out[:, span] = jnp.concatenate(mixed, axis=1).astype(bf16)

    for j in range(4):
        heads(j)
        yield
    need("o")
    unpack_into(wo, wo_p)
    keep("wo")
    r = tok[z].astype(f32) + matmul(ho_out[...], wo[...], (1, 0))
    r_out[...] = r
    n2 = (r * rms_scale(r) * gains[1:2]).astype(bf16)
    n_out[:, :D] = n2
    n_held[:, :D] = n2
    logits = matmul(n2, small_out[...], (1, 0))
    hits = lane == routes[:, 0:1]
    for k in range(1, routes.shape[1]):
        hits = hits | (lane == routes[:, k : k + 1])
    lifted = jnp.where(hits, logits, masked_score)
    lifted = jnp.where(hits, jnp.exp(lifted - jnp.max(lifted, axis=1, keepdims=True)), 0.0)
    gate = lifted / jnp.sum(lifted, axis=1, keepdims=True)
    gate_out[...] = gate
    row = lax.broadcasted_iota(jnp.int32, (TOK, TOK), 0)
    col = lax.broadcasted_iota(jnp.int32, (TOK, TOK), 1)
    earlier = jnp.where(col < row, 1.0, 0.0).astype(bf16)
    ranks = matmul(earlier, jnp.where(hits, 1.0, 0.0).astype(bf16), (1, 0))
    high = gate.astype(bf16).astype(f32)
    meta = jnp.where(hits, ranks, jnp.where(lane < EXPERTS, -1.0, 0.0))
    meta = meta + pltpu.roll(high, EXPERTS, 1) + pltpu.roll(gate - high, 2 * EXPERTS, 1)
    meta = meta.astype(bf16)
    n_out[:, D:] = meta
    n_held[:, D:] = meta


GATHER_ORDERS = {"k": "zyx", "q": "zyx", "o": "zxy"}
FRONT_SCHEDULE = "kqtokqokqotkqokqotfdqofdffodffffdffff"


def front_kernel(
    length, tok, dout, w_kv, w_q, w_o, small, routes, cos, sin,
    n_out, q_out, lse_out, ho_out, r_out, gate_out, small_out,
    n1_far, kv_far, wq_far, wkv_far, wo_far, tok_far, dout_far, n_all,
    n1, kv, wq, wkv, wo,
    wkv_p, wq_p, wo_p, tok_held, dout_held, n_held, bias, *sems,
):
    at = place()
    wires = Wires(*sems)
    own_tok = wires.keep(tok, tok_held.at[at["z"]])
    own_dout = wires.keep(dout, dout_held.at[at["x"], at["c"]])
    steps = {}
    for name, src, out in (("k", w_kv, wkv_p), ("q", w_q, wq_p), ("o", w_o, wo_p)):
        block = out.at[index(at, "")]
        block[:, :512] = jnp.concatenate([src[:, :512], src[:, 512:]], axis=0).astype(bf16)
        if name == "k":
            block[:, 512:] = small[...].astype(bf16)
        steps[name] = weight_steps(wires, at, [(out, GATHER_ORDERS[name])])
    steps["t"] = token_steps(wires, at, tok_held)
    steps["d"] = row_steps(wires, at, dout_held, dout_far)
    flat = [p.reshape(128, *p.shape[-2:]) for p in (wq_p, wkv_p, wo_p)]
    outs = (n_out, n1, q_out, kv, lse_out, ho_out, r_out, gate_out, wq, wkv, wo, small_out)
    kept = []
    results = {
        "n1": (n1, n1_far),
        "kv": (kv, kv_far),
        "wq": (wq, wq_far),
        "wkv": (wkv, wkv_far),
        "wo": (wo, wo_far),
    }

    def need(name):
        for _ in steps[name]:
            pass
        if name == "t":
            kept.append(wires.keep(tok_held, tok_far))

    def keep(name):
        kept.append(wires.keep(*results[name]))

    steps["f"] = front_steps(
        at["z"], length, (need, keep), *flat, tok_held, routes, cos, sin, outs,
        n_held.at[at["x"], at["c"]], bias,
    )
    greet(at, "xyzc")
    own_tok.wait()
    own_dout.wait()
    in_order(FRONT_SCHEDULE, **steps)
    in_order("", n=row_steps(wires, at, n_held, n_all))
    for copy in kept:
        copy.wait()
    wires.finish()


def front(length, w_kv, w_q, w_o, small, tok, dout, routes, cos, sin):
    vmem = pl.BlockSpec(memory_space=pltpu.VMEM)
    far = pl.BlockSpec(memory_space=pltpu.HBM)
    rows = jax.ShapeDtypeStruct((TOK, D), bf16)
    lanes = jax.ShapeDtypeStruct((TOK, 128), f32)
    lead = (4, 4, 2, 4)
    copies = WEIGHT_COPIES + TOKEN_COPIES + 2 * ROW_COPIES
    return pl.pallas_call(
        front_kernel,
        out_shape=[
            jax.ShapeDtypeStruct((TOK, D + 128), bf16),
            rows,
            lanes,
            rows,
            jax.ShapeDtypeStruct((TOK, D), f32),
            lanes,
            jax.ShapeDtypeStruct((D, 128), bf16),
        ]
        + [pltpu.HBM((D, D), bf16)] * 5
        + [
            pltpu.HBM((4, TOK, D), bf16),
            pltpu.HBM((4, 2, TOK, D), bf16),
            pltpu.HBM((4, 2, TOK, D + 128), bf16),
        ],
        in_specs=[pl.BlockSpec(memory_space=pltpu.SMEM)] + [far] * 2 + [vmem] * 7,
        out_specs=[vmem] * 7 + [far] * 8,
        scratch_shapes=[pltpu.VMEM((D, D), bf16)] * 5
        + [
            pltpu.VMEM(lead + (16, 512 + 128), bf16),
            pltpu.VMEM(lead + (16, 512), bf16),
            pltpu.VMEM(lead + (16, 512), bf16),
            pltpu.VMEM((4, TOK, D), bf16),
            pltpu.VMEM((4, 2, TOK, D), bf16),
            pltpu.VMEM((4, 2, TOK, D + 128), bf16),
            pltpu.VMEM((TOK, 4 * TOK), f32),
        ]
        + wire_sems(copies, 2 + 6 + 2 * ROW_KEPT),
        compiler_params=pltpu.CompilerParams(
            collective_id=1, has_side_effects=True, vmem_limit_bytes=60 * 1024 * 1024
        ),
        cost_estimate=pl.CostEstimate(
            flops=10**10, bytes_accessed=30_000_000, transcendentals=5_000_000
        ),
        name="front",
    )(length, *hbm(tok, dout), w_kv, w_q, w_o, small, routes, cos, sin)


def rms_back(values, scale, gain, dnormed):
    scaled = values * scale
    dscaled = dnormed * gain
    dvalues = scale * (dscaled - scaled * jnp.mean(dscaled * scaled, axis=-1, keepdims=True))
    return dvalues, jnp.sum(dnormed * scaled, axis=0, keepdims=True)


def pack_into(out, value):
    def chunk(i, carry):
        rows = pl.ds(pl.multiple_of(i * 128, 128), 128)
        left = value[rows, :512].reshape(16, 8, 512)
        right = value[rows, 512:].reshape(16, 8, 512)
        out[pl.ds(i * 16, 16), :, :512] = jnp.concatenate([left, right], axis=1).astype(bf16)
        return carry

    lax.fori_loop(0, 8, chunk, 0)


def back_steps(
    z, length, sums, dout, n_ext, r_ref, gate_ref, ho, q_ref, kv, lse, n1, wo, small,
    cos, sin, cos_t, sin_t, late,
    dwq_p, dwkv_p, dwo_p, dg_p, dn1_out, dr_out,
    bias, square, dq_s, do_s, dkv_s,
):
    own = pl.ds(pl.multiple_of(z * TOK, TOK), TOK)
    gains = gain_rows(small[...])
    lane = lax.broadcasted_iota(jnp.int32, (TOK, 128), 1)
    gate = gate_ref[...]
    fields = sums[:, D:]
    dgate = fields + pltpu.roll(fields, 128 - EXPERTS, 1)
    mean = jnp.sum(gate * dgate, axis=1, keepdims=True)
    dlogits = (gate * (dgate - mean)).astype(bf16)
    dn2 = sums[:, :D] + matmul(dlogits, small[...], (1, 1))
    r = r_ref[...]
    dr, dg2 = rms_back(r, rms_scale(r), gains[1:2], dn2)
    dr = dr + dout[...].astype(f32)
    dr_out[...] = dr
    d_att = dr.astype(bf16)
    square[...] = matmul(ho[...], d_att, (0, 0))
    pack_into(dwo_p, square)
    spread_gain(dwo_p.at[:, :, 512:], dg2, EXPERTS, matmul(n_ext[:, :D], dlogits, (0, 0)))
    yield
    do_s[...] = matmul(d_att, wo[...], (1, 1)).astype(bf16)
    fill_bias(bias, length[0], z * TOK)
    width = KV_HEADS * HEAD_DIM
    scale = HEAD_DIM ** (-0.5)
    dkv_t = square

    def heads(j):
        keys = kv[:, pl.ds(j * 128, 128)]
        values = kv[:, pl.ds(width + j * 128, 128)]
        for g in (0, 1):
            span = pl.ds(j * 256 + g * 128, 128)
            qs, dos = q_ref[:, span], do_s[:, span]
            prods = dos.astype(f32) * ho[:, span].astype(f32)
            key = keys[:, g * HEAD_DIM : (g + 1) * HEAD_DIM]
            value = values[:, g * HEAD_DIM : (g + 1) * HEAD_DIM]
            dqs = []
            dk_t, dv_t = 0.0, 0.0
            for h in (0, 1):
                part = slice(h * HEAD_DIM, (h + 1) * HEAD_DIM)
                head = j * 4 + g * 2 + h
                shift_by = jnp.sum(jnp.where(lane == head, lse[...], 0.0), axis=1, keepdims=True)
                mine = (lane >= h * HEAD_DIM) & (lane < (h + 1) * HEAD_DIM)
                delta = jnp.sum(jnp.where(mine, prods, 0.0), axis=1, keepdims=True)
                p = jnp.exp(matmul(qs[:, part], key, (1, 1)) + bias[...] - shift_by)
                dp = matmul(dos[:, part], value, (1, 1))
                ds = (p * (dp - delta)).astype(bf16)
                dqs.append(matmul(ds, key, (1, 0)) * scale)
                dk_t = dk_t + matmul(qs[:, part], ds, (0, 0))
                dv_t = dv_t + matmul(dos[:, part], p.astype(bf16), (0, 0))
            dq_s[:, span] = jnp.concatenate(dqs, axis=1)
            half = HEAD_DIM // 2
            wave = dk_t * sin_t[...]
            dk_t = dk_t * cos_t[...] + jnp.concatenate([wave[half:], -wave[:half]], axis=0)
            at = j * 128 + g * HEAD_DIM
            dkv_t[pl.ds(at, HEAD_DIM), :] = dk_t
            dkv_t[pl.ds(width + at, HEAD_DIM), :] = dv_t

    for j in range(4):
        heads(j)
        yield

    def flip(i, carry):
        at = pl.ds(pl.multiple_of(i * 128, 128), 128)
        dkv_s[:, at] = jnp.transpose(dkv_t[at, :]).astype(bf16)
        return carry

    lax.fori_loop(0, 8, flip, 0)
    square[...] = matmul(n1[...], dkv_s[...], (0, 0))
    pack_into(dwkv_p, square)
    yield
    dq = turned_rows(dq_s[...], cos[...], sin[...], True).astype(bf16)
    square[...] = matmul(n1[own, :], dq, (0, 0))
    pack_into(dwq_p, square)
    yield
    wq, wkv, tok = late()
    for b in range(4):
        columns = slice(b * TOK, (b + 1) * TOK)
        square[:, columns] = matmul(dkv_s[...], wkv[b, :, :D], (1, 1))
        square[own, columns] += matmul(dq, wq[b, :, :D], (1, 1))
    for b in range(4):
        dn1_out[b] = square[b * TOK : (b + 1) * TOK, :].astype(bf16)
    yield
    dg1 = jnp.zeros((1, D), f32)
    for b in range(4):
        x = tok[b, :, :D].astype(f32)
        dn1 = square[b * TOK : (b + 1) * TOK, :]
        dg1 = dg1 + jnp.sum(dn1 * (x * rms_scale(x)), axis=0, keepdims=True)
    spread_gain(dg_p, dg1, 0, None)


def spread_gain(out, row, lane, rest):
    sub = lax.broadcasted_iota(jnp.int32, (8, D), 0)
    rows = jnp.where(sub == 0, row, 0.0)
    high = rows.astype(bf16)
    low = (rows - high.astype(f32)).astype(bf16)
    place_lane = lax.broadcasted_iota(jnp.int32, (8, 128), 1)
    place_sub = lax.broadcasted_iota(jnp.int32, (8, 128), 0)
    spread = jnp.where((place_lane == lane) & (place_sub == 0), 1.0, 0.0).astype(bf16)
    value = matmul(high, spread, (0, 0)) + matmul(low, spread, (0, 0))
    if rest is not None:
        value = value + rest
    value = value.reshape(128, 8, 128)
    out[...] = jnp.concatenate([value, jnp.zeros_like(value)], axis=1).astype(bf16)


BACK_INPUTS = 15
BACK_ORDERS = {"a": "xyz", "k": "xzy", "o": "xyz", "g": "xyz"}


def back_kernel(length, dn_parts, out_parts, wq, wkv, tok, *refs):
    loaded = refs[:BACK_INPUTS]
    refs = refs[BACK_INPUTS:]
    g_q, g_kv, g_o, g_g, dn1_sum, mixed, dr_out = refs[:7]
    sums, dn1, bias, square, dq_s, do_s, dkv_s = refs[7:14]
    dn_bufs, out_bufs, dn1_bufs = refs[14:19], refs[19:24], refs[24:27]
    q_bufs, kv_bufs, o_bufs, g_bufs = (refs[27 + 7 * i : 34 + 7 * i] for i in range(4))
    inputs = refs[55 : 55 + BACK_INPUTS]
    at = place()
    wires = Wires(*refs[55 + BACK_INPUTS :])
    greet(at, "xyzc")

    def backward():
        for copy in arriving:
            copy.wait()
        wires.finish()
        yield from back_steps(
            at["z"], length, sums, *inputs, late,
            *(bufs[0].reshape(128, *bufs[0].shape[-2:]) for bufs in (q_bufs, kv_bufs, o_bufs, g_bufs)),
            dn1, dr_out, bias, square, dq_s, do_s, dkv_s,
        )

    late_spots = (out_bufs[1], dn_bufs[0], dn_bufs[1])
    late_copies = []

    def load_late():
        for src, dst in ((wkv, dn_bufs[0]), (tok, dn_bufs[1]), (wq, out_bufs[1])):
            late_copies.append(wires.keep(src, dst.at[:, :, pl.ds(0, D)]))
        yield

    def late():
        for copy in late_copies:
            copy.wait()
        return late_spots

    steps = {
        "n": row_sum_steps(wires, at, dn_parts, sums, *dn_bufs),
        "l": row_sum_steps(wires, at, out_parts, mixed, *out_bufs),
        "z": ring_sum_steps(wires, at, "z", dn1, dn1_sum, *dn1_bufs),
        "a": matrix_steps(wires, at, BACK_ORDERS["a"], q_bufs[0], g_q, *q_bufs[1:]),
        "k": matrix_steps(wires, at, BACK_ORDERS["k"], kv_bufs[0], g_kv, *kv_bufs[1:]),
        "o": matrix_steps(wires, at, BACK_ORDERS["o"], o_bufs[0], g_o, *o_bufs[1:]),
        "g": matrix_steps(wires, at, BACK_ORDERS["g"], g_bufs[0], g_g, *g_bufs[1:]),
        "e": load_late(),
        "b": backward(),
    }
    next(steps["n"])
    own = pl.ds(pl.multiple_of(at["z"] * TOK, TOK), TOK)
    arriving = [
        wires.keep(src.at[own] if src.shape != dst.shape else src, dst)
        for src, dst in zip(loaded, inputs)
    ]
    in_order(BACK_SCHEDULE, **steps)
    wires.finish()


BACK_SCHEDULE = "l" + "nnnn" + "bo" + "le" + "bo" + "b" + "b" + "bl" + "bk" + "bak" + "bzao" + "bg" + "zkgkoagakgolz"


def back(length, dn_parts, out_parts, wq, wkv, tok, *inputs):
    vmem = pl.BlockSpec(memory_space=pltpu.VMEM)
    far = pl.BlockSpec(memory_space=pltpu.HBM)
    wide = dn_parts.shape[-1]
    widths = (512, 512, 640, 128)
    copies = 2 * ROW_SUM_COPIES + RING_SUM_COPIES + 4 * MATRIX_COPIES
    scratch = [
        pltpu.VMEM((TOK, wide), f32),
        pltpu.VMEM((4, TOK, D), bf16),
        pltpu.VMEM((TOK, 4 * TOK), f32),
        pltpu.VMEM((D, D), f32),
        pltpu.VMEM((TOK, D), f32),
        pltpu.VMEM((TOK, D), bf16),
        pltpu.VMEM((D, D), bf16),
    ]
    scratch += row_sum_scratch(TOK, wide) + row_sum_scratch(TOK, D) + ring_sum_scratch(TOK, D)
    for width in widths:
        scratch += matrix_scratch(width)
    scratch += [
        pltpu.VMEM((TOK, 128) if v.shape == (4 * TOK, 128) and v.dtype == f32 else v.shape, v.dtype)
        for v in inputs
    ]
    return pl.pallas_call(
        back_kernel,
        out_shape=[jax.ShapeDtypeStruct((16, width), f32) for width in widths]
        + [jax.ShapeDtypeStruct((TOK, D), f32)] * 3,
        in_specs=[pl.BlockSpec(memory_space=pltpu.SMEM)] + [far] * (5 + BACK_INPUTS),
        out_specs=[vmem] * 7,
        scratch_shapes=scratch + wire_sems(copies, 8 + 3 + BACK_INPUTS),
        compiler_params=pltpu.CompilerParams(
            collective_id=4, has_side_effects=True, vmem_limit_bytes=63 * 1024 * 1024
        ),
        cost_estimate=pl.CostEstimate(
            flops=2 * 10**10, bytes_accessed=40_000_000, transcendentals=5_000_000
        ),
        name="back",
    )(length, *hbm(dn_parts, out_parts, wq, wkv, tok, *inputs))


def rotary_constants(count):
    half = HEAD_DIM // 2
    freqs = (10000.0 ** (-np.arange(half, dtype=np.float64) / half)).astype(np.float32)
    angles = np.arange(count, dtype=np.float32)[:, None] * freqs[None, :]
    tables = np.cos(angles.astype(np.float64)), np.sin(angles.astype(np.float64))
    return tuple(np.concatenate([t, t], 1).astype(np.float32) for t in tables)


def unpack_matrix(packed):
    return jnp.concatenate([packed[:8], packed[8:]], axis=1)


def body(
    tokens, routes, lengths, out_grad,
    query_weight, query_mean, query_square,
    keyval_weight, keyval_mean, keyval_square,
    output_weight, output_mean, output_square,
    router_weight, router_mean, router_square,
    norm_gains, gains_mean, gains_square,
    gateup_weight, gateup_mean, gateup_square,
    down_weight, down_mean, down_square,
):
    row_count = tokens.shape[0]
    seq_len = row_count * 4
    query_width = HEADS * HEAD_DIM

    expert_b = lax.all_gather(
        jnp.concatenate([gateup_weight[0], down_weight[0]], axis=0).astype(bf16),
        ("y", "z"),
        axis=0,
    )
    small = jnp.concatenate(
        [router_weight, norm_gains.T, jnp.zeros((8, 128 - EXPERTS - 2), f32)], axis=1
    )
    small = jnp.concatenate([small, jnp.zeros((8, 128), f32)], axis=0)
    cos, sin = rotary_constants(seq_len)
    cos2, sin2, cos_t, sin_t = (
        jnp.asarray(table)
        for table in (np.tile(cos, (1, 2)), np.tile(sin, (1, 2)), cos.T.copy(), sin.T.copy())
    )
    (
        n_ext, q, lse, ho, residual, gate, small_b,
        n1, kv, query_b, keyval_b, output_b, all_tokens, dout_all, n_all,
    ) = front(
        lengths,
        keyval_weight,
        query_weight,
        output_weight,
        small,
        tokens,
        out_grad,
        routes,
        cos2,
        sin2,
    )
    wide = n_all.shape[-1]
    n_all = n_all.reshape(SOURCES, row_count, wide)
    dn_parts, out_parts, d_expert = experts(
        n_all,
        dout_all.reshape(SOURCES, row_count, D),
        expert_b.reshape((4,) + (4, D // 4 + FF_E // 4, D)),
    )
    grad_expert = lax.psum_scatter(
        d_expert.reshape((16,) + d_expert.shape[2:]),
        ("y", "z"),
        scatter_dimension=0,
        tiled=False,
    ).astype(f32)
    g_query, g_keyval, g_output, g_gain, dn1_sum, mixed_out, dresidual = back(
        lengths,
        dn_parts.reshape(4, 2, row_count, wide),
        out_parts.reshape(4, 2, row_count, D),
        query_b.reshape(4, row_count, D),
        keyval_b.reshape(4, row_count, D),
        all_tokens,
        out_grad, n_ext, residual, gate, ho, q, kv, lse, n1, output_b, small_b,
        cos2, sin2, cos_t, sin_t,
    )
    layer_out = (residual + mixed_out).astype(bf16)
    grad_query, grad_keyval, grad_output = (
        unpack_matrix(g) for g in (g_query, g_keyval, g_output[:, :512])
    )
    grad_router = g_output[:8, 512 : 512 + EXPERTS]
    grad_gains = jnp.stack([g_gain[:8, 0], g_output[:8, 512 + EXPERTS]])
    inputs = tokens.astype(f32)
    gain_one = small_b[:, EXPERTS].astype(f32)
    dnorm_one, _ = norm_back(inputs, rms_scale(inputs), gain_one, dn1_sum)
    tokens_grad = dresidual + dnorm_one

    rate = 0.5
    query_new = adamw(query_weight, grad_query, query_mean, query_square, rate * D ** (-0.5), 0.1)
    keyval_new = adamw(
        keyval_weight, grad_keyval, keyval_mean, keyval_square, rate * D ** (-0.5), 0.1
    )
    output_new = adamw(
        output_weight,
        grad_output,
        output_mean,
        output_square,
        rate * max(1, 2 * query_width // seq_len) ** (-0.5),
        0.1,
    )
    router_new = adamw(
        router_weight, grad_router, router_mean, router_square, rate * (4 * D) ** (-0.5), 0.1
    )
    gains_new = adamw(norm_gains, grad_gains, gains_mean, gains_square, 0.6, 0.0)
    gateup_new = adamw(
        gateup_weight,
        grad_expert[None, : D // 4],
        gateup_mean,
        gateup_square,
        rate * D ** (-0.5),
        0.1,
    )
    down_new = adamw(
        down_weight,
        grad_expert[None, D // 4 :],
        down_mean,
        down_square,
        rate * (FF_E // 8) ** (-0.5),
        0.1,
    )
    return (
        (layer_out, tokens_grad)
        + query_new
        + keyval_new
        + output_new
        + router_new
        + gains_new
        + gateup_new
        + down_new
    )


def solution(mesh):
    devices = jax.sharding.Mesh(mesh.devices.reshape(4, 4, 2, 4), ("x", "y", "c", "z"))
    every = ("x", "y", "c", "z")
    rows = P(every, None)
    gains = P(None, every)
    shard = P(("x", "y", "c"), "z", None)
    return jax.shard_map(
        body,
        mesh=devices,
        in_specs=(rows, rows, P(("x", "y", "c")), rows)
        + (rows,) * 12
        + (gains,) * 3
        + (shard,) * 6,
        out_specs=(rows, rows) + (rows,) * 12 + (gains,) * 3 + (shard,) * 6,
        check_vma=False,
    )
```

```python
import jax
import jax.numpy as jnp
import numpy as np
from jax import lax
from jax.experimental import pallas as pl
from jax.experimental.pallas import tpu as pltpu
from jax.sharding import PartitionSpec as P

MESH = pl.DeviceIdType.MESH
bf16 = jnp.bfloat16
f32 = jnp.float32
AXES = "xycz"
STRIP = 16


def place():
    return {a: lax.axis_index(a) for a in AXES}


def device(at):
    return tuple(at[a] for a in AXES)


def shift(at, axis, by):
    size = 2 if axis == "c" else 4
    return lax.rem(at[axis] + by, size)


def peer(at, axis, by):
    return device({**at, axis: shift(at, axis, by)})


def greet(at, axes):
    barrier = pltpu.get_barrier_semaphore()
    count = 0
    for axis in axes:
        for by in (1,) if axis == "c" else (1, 2, 3):
            pl.semaphore_signal(
                barrier, inc=1, device_id=peer(at, axis, by), device_id_type=MESH
            )
            count += 1
    pl.semaphore_wait(barrier, count)


class Wires:
    def __init__(self, send_sems, recv_sems, local_sems):
        self.send_sems, self.recv_sems, self.local_sems = send_sems, recv_sems, local_sems
        self.copies, self.sent, self.local = [], 0, 0

    def send(self, src, dst, target):
        at = self.sent
        self.sent += 1
        copy = pltpu.make_async_remote_copy(
            src_ref=src,
            dst_ref=dst,
            send_sem=self.send_sems.at[at],
            recv_sem=self.recv_sems.at[at],
            device_id=target,
            device_id_type=MESH,
        )
        copy.start()
        self.copies.append(copy)
        return copy

    def keep(self, src, dst):
        copy = pltpu.make_async_copy(src, dst, self.local_sems.at[self.local])
        copy.start()
        self.local += 1
        return copy

    def finish(self):
        for copy in self.copies:
            copy.wait_send()
        self.copies = []


def wire_sems(copies, kept):
    return [
        pltpu.SemaphoreType.DMA((copies,)),
        pltpu.SemaphoreType.DMA((copies,)),
        pltpu.SemaphoreType.DMA((kept,)),
    ]


def in_order(order, **steps):
    for letter in order:
        next(steps[letter], None)
    for step in steps.values():
        for _ in step:
            pass


def hbm(*arrays):
    return [pltpu.with_memory_space_constraint(v, pltpu.HBM) for v in arrays]


def ring_steps(wires, at, axis, spot, hand_on):
    right, left = peer(at, axis, 1), peer(at, axis, 3)
    to_right = {k: wires.send(spot(0, k), spot(0, k), right) for k in (0, 1)}
    to_left = {k: wires.send(spot(0, k), spot(0, k), left) for k in (1, 0)}
    for k in (0, 1):
        hand_on(0, k)
    yield
    to_right[0].wait_recv()
    far_right = wires.send(spot(3, 0), spot(3, 0), right)
    hand_on(3, 0)
    to_left[1].wait_recv()
    far_left = wires.send(spot(1, 1), spot(1, 1), left)
    hand_on(1, 1)
    yield
    to_right[1].wait_recv()
    hand_on(3, 1)
    to_left[0].wait_recv()
    hand_on(1, 0)
    yield
    far_right.wait_recv()
    hand_on(2, 0)
    far_left.wait_recv()
    hand_on(2, 1)


def row_steps(wires, at, held, out):
    half = held.shape[2] // 2
    sibling = peer(at, "c", 1)
    other = shift(at, "c", 1)
    across, kept = [], []

    def hand_on(by, part):
        rows = pl.ds(part * half, half)
        unit, theirs = (
            (shift(at, "x", by), c, rows) for c in (at["c"], other)
        )
        across.append((theirs, wires.send(held.at[unit], held.at[unit], sibling)))
        kept.append(wires.keep(held.at[unit], out.at[unit]))

    def spot(by, part):
        return held.at[shift(at, "x", by), at["c"], pl.ds(part * half, half)]

    yield from ring_steps(wires, at, "x", spot, hand_on)
    yield
    for unit, copy in across:
        copy.wait_recv()
        kept.append(wires.keep(held.at[unit], out.at[unit]))
    for copy in kept:
        copy.wait()


ROW_KEPT = 16
ROW_COPIES = 6 + 8


def token_steps(wires, at, held):
    half = held.shape[1] // 2

    def spot(by, part):
        return held.at[shift(at, "z", by), pl.ds(part * half, half)]

    yield from ring_steps(wires, at, "z", spot, lambda by, part: None)


TOKEN_COPIES = 6


def index(at, whole, **fixed):
    spots = {**at, **{a: slice(None) for a in whole}, **fixed}
    return tuple(spots[axis] for axis in AXES)


def weight_steps(wires, at, parts):
    arrivals = {}
    for p, (o, order) in enumerate(parts):
        own = o.at[index(at, "")]
        for by in (1, 3, 2):
            arrivals[p, by] = wires.send(own, own, peer(at, order[0], by))
    yield
    later = {}
    for p, (o, order) in enumerate(parts):
        for by in (1, 3, 2):
            arrivals[p, by].wait_recv()
        spot = index(at, order[0])
        for by in (1, 3, 2):
            later[p, by] = wires.send(o.at[spot], o.at[spot], peer(at, order[1], by))
    yield
    sibling = peer(at, "c", 1)
    across, rings = [], []
    for p, (o, order) in enumerate(parts):
        for by in (1, 3, 2):
            later[p, by].wait_recv()

        def spot(by, part, o=o, order=order):
            pieces = {order[1]: pl.ds(2 * part, 2), order[2]: shift(at, order[2], by)}
            return o.at[index(at, order[0], **pieces)]

        def hand_on(by, part, spot=spot):
            across.append(wires.send(spot(by, part), spot(by, part), sibling))

        ring = ring_steps(wires, at, order[2], spot, hand_on)
        next(ring)
        rings.append(ring)
    yield
    for _ in range(3):
        for ring in rings:
            next(ring, None)
        yield
    for copy in across:
        copy.wait_recv()


WEIGHT_COPIES = 3 * (3 + 3 + 6 + 8)


def add_rows(out, parts, rows):
    def strip(i, carry):
        span = pl.ds(pl.multiple_of(i * STRIP, STRIP), STRIP)
        total = parts[0][span].astype(f32)
        for part in parts[1:]:
            total = total + part[span].astype(f32)
        out[span] = total.astype(out.dtype)
        return carry

    lax.fori_loop(0, rows // STRIP, strip, 0)


def ring_sum_steps(wires, at, axis, blocks, out, mid, last, near):
    half = out.shape[0] // 2
    low, high = pl.ds(0, half), pl.ds(half, half)
    ahead, back, far = (blocks.at[shift(at, axis, by)] for by in (1, 3, 2))
    right, left = peer(at, axis, 1), peer(at, axis, 3)
    near_l = wires.send(far.at[low], near.at[0], right)
    near_r = wires.send(far.at[high], near.at[1], left)
    pure_l = wires.send(ahead.at[high], last.at[0, high], right)
    pure_r = wires.send(back.at[low], last.at[1, low], left)
    yield
    near_l.wait_recv()
    add_rows(mid.at[0], [ahead.at[low], near.at[0]], half)
    sum_l = wires.send(mid.at[0], last.at[0, low], right)
    near_r.wait_recv()
    add_rows(mid.at[1], [back.at[high], near.at[1]], half)
    sum_r = wires.send(mid.at[1], last.at[1, high], left)
    yield
    for copy in (pure_l, sum_l, pure_r, sum_r):
        copy.wait_recv()
    add_rows(out, [blocks.at[at[axis]], last.at[0], last.at[1]], 2 * half)


def ring_sum_scratch(rows, width):
    return [
        pltpu.VMEM((2, rows // 2, width), bf16),
        pltpu.VMEM((2, rows, width), bf16),
        pltpu.VMEM((2, rows // 2, width), bf16),
    ]


def row_sum_steps(wires, at, c_ref, out, held, crossed, mid, last, near):
    other = shift(at, "c", 1)
    sibling = peer(at, "c", 1)
    rows = out.shape[0]
    crossing, kept = {}, {}
    for by in (2, 1, 3, 0):
        i = shift(at, "x", by)
        crossing[by] = wires.send(c_ref.at[i, other], crossed.at[i], sibling)
        kept[by] = wires.keep(c_ref.at[i, at["c"]], held.at[i])
    yield
    for by in (2, 1, 3, 0):
        i = shift(at, "x", by)
        kept[by].wait()
        crossing[by].wait_recv()
        add_rows(held.at[i], [held.at[i], crossed.at[i]], rows)
        if by == 3:
            ring = ring_sum_steps(wires, at, "x", held, out, mid, last, near)
            next(ring)
    yield
    yield from ring


ROW_SUM_COPIES = 4 + 6


def row_sum_scratch(rows, width):
    return [pltpu.VMEM((4, rows, width), bf16)] * 2 + ring_sum_scratch(rows, width)


def matrix_steps(wires, at, order, pack, write, crossed, one, two, three, sum1, sum2):
    axis, after, end = order
    crossing = wires.send(
        pack.at[:, :, shift(at, "c", 1)], crossed, peer(at, "c", 1)
    )

    def own(by):
        return pack.at[index(at, "xyz", **{axis: shift(at, axis, by)})]

    def later(by):
        rest = "xyz".replace(axis, "")
        return sum1.at[tuple(shift(at, a, by) if a == after else slice(None) for a in rest)]

    def total(out, parts, count):
        def body(i, carry):
            value = parts[0][i].astype(f32)
            for part in parts[1:]:
                value = value + part[i].astype(f32)
            out[i] = value.astype(out.dtype)
            return carry

        lax.fori_loop(0, count, body, 0)

    def spread(parts, slots, along):
        return [wires.send(parts(by), slots.at[by - 1], peer(at, along, by)) for by in (2, 1, 3)]

    yield
    crossing.wait_recv()

    def body(i, carry):
        spot = (i // 4, i % 4)
        mine = pack[spot + (at["c"],)].astype(f32) + crossed[spot].astype(f32)
        pack[spot + (at["c"],)] = mine.astype(bf16)
        return carry

    lax.fori_loop(0, 16, body, 0)
    copies = spread(own, one, axis)
    yield
    for copy in copies:
        copy.wait_recv()
    total(sum1, [own(0)] + [one.at[k] for k in range(3)], 4)
    copies = spread(later, two, after)
    yield
    for copy in copies:
        copy.wait_recv()
    total(sum2, [later(0)] + [two.at[k] for k in range(3)], 4)
    copies = spread(lambda by: sum2.at[shift(at, end, by)], three, end)
    yield
    for copy in copies:
        copy.wait_recv()
    value = sum2[at[end]].astype(f32)
    for k in range(3):
        value = value + three[k].astype(f32)
    write(value)


MATRIX_COPIES = 10
RING_SUM_COPIES = 6


def matrix_scratch(width):
    leads = ((4, 4, 2, 4), (4, 4, 4), (3, 4, 4), (3, 4), (3,), (4, 4), (4,))
    return [pltpu.VMEM(lead + (16, width), bf16) for lead in leads]


D = 1024
HEADS = 16
KV_HEADS = 8
HEAD_DIM = 64
EXPERTS = 32
FF_E = 512
STEP = 10
CAP = 96
TOK = 256


norm_epsilon = 1e-06
beta_first = 0.9
beta_second = 0.95
adam_epsilon = 1e-08
masked_score = -1e30


def rotary_tables(positions, half_width):
    freqs = 10000.0 ** (-jnp.arange(half_width, dtype=jnp.float32) / half_width)
    angles = positions.astype(jnp.float32)[:, None] * freqs[None, :]
    cosines = jnp.cos(angles)
    sines = jnp.sin(angles)
    return (jnp.concatenate([cosines, cosines], 1), jnp.concatenate([sines, sines], 1))


def rotate(values, cosines, sines):
    half_width = values.shape[-1] // 2
    turned = jnp.concatenate([-values[..., half_width:], values[..., :half_width]], -1)
    return values * cosines[:, None, :] + turned * sines[:, None, :]


def rotate_back(grads, cosines, sines):
    half_width = grads.shape[-1] // 2
    scaled = grads * sines[:, None, :]
    return grads * cosines[:, None, :] + jnp.concatenate(
        [scaled[..., half_width:], -scaled[..., :half_width]], -1
    )


def rms_scale(values):
    return lax.rsqrt(jnp.mean(values * values, axis=-1, keepdims=True) + norm_epsilon)


def norm_back(values, scale, gain, dnormed):
    scaled = values * scale
    dgain = jnp.sum(dnormed * scaled, axis=0)
    dscaled = dnormed * gain
    dvalues = scale * (dscaled - scaled * jnp.mean(dscaled * scaled, axis=-1, keepdims=True))
    return (dvalues, dgain)


def masked_scores(grouped, whole_kv, positions, length):
    key_count = whole_kv.shape[0]
    key_width = whole_kv.shape[1] // 2
    heads_kv = grouped.shape[1]
    head_size = grouped.shape[3]
    all_keys = whole_kv[:, :key_width].reshape(key_count, heads_kv, head_size)
    all_values = whole_kv[:, key_width:].reshape(key_count, heads_kv, head_size)
    raw_scores = jnp.einsum(
        "qkgd,pkd->kgqp", grouped, all_keys, preferred_element_type=jnp.float32
    ) * head_size ** (-0.5)
    key_pos = jnp.arange(key_count, dtype=jnp.int32)
    allowed = (key_pos[None, :] <= positions[:, None]) & (key_pos[None, :] < length)
    return (jnp.where(allowed, raw_scores, masked_score), all_keys, all_values)


def adamw(weight, grad, first, second, rate, decay):
    first_new = beta_first * first + (1.0 - beta_first) * grad
    second_new = beta_second * second + (1.0 - beta_second) * grad * grad
    update = (
        first_new
        / (1.0 - beta_first**STEP)
        / (jnp.sqrt(second_new / (1.0 - beta_second**STEP)) + adam_epsilon)
    )
    return (weight - rate * (update + decay * weight), first_new, second_new)


SOURCES = 8
HOSTED = 4
SLOTS = SOURCES * CAP
OUT_BLOCKS = 2


def matmul(a, b, contract):
    return lax.dot_general(
        a, b, (((contract[0],), (contract[1],)), ((), ())), preferred_element_type=f32
    )


def expert_kernel(n_ref, g_ref, w_ref, dn_ref, out_ref, dw_ref, xs, ds, zs, gates):
    step = pl.program_id(0)
    base = lax.axis_index("x") * 8 + lax.axis_index("c")

    @pl.when(step == 0)
    def _():
        lane = lax.broadcasted_iota(jnp.int32, (16, 128), 1)
        sub = lax.broadcasted_iota(jnp.int32, (16, 128), 0)
        wanted = base + 2 * lax.rem(sub, HOSTED) + EXPERTS * (sub // HOSTED)
        choose = jnp.where((lane == wanted) & (sub < 3 * HOSTED), 1.0, 0.0).astype(bf16)
        slot = lax.broadcasted_iota(jnp.int32, (CAP, TOK), 0).astype(f32)

        def source(b, carry):
            fields = matmul(choose, n_ref[b, :, D:], (1, 1))
            hots = []
            for j in range(HOSTED):
                hot = slot == fields[j : j + 1]
                gate = fields[HOSTED + j : HOSTED + j + 1] + fields[2 * HOSTED + j : 2 * HOSTED + j + 1]
                span = pl.ds(pl.multiple_of(j * SLOTS + b * CAP, CAP), CAP)
                gates[span, :] = jnp.broadcast_to(
                    jnp.sum(jnp.where(hot, gate, 0.0), axis=1, keepdims=True), (CAP, 128)
                )
                hots.append(jnp.where(hot, 1.0, 0.0).astype(bf16))
            hots = jnp.concatenate(hots, axis=0)
            x = matmul(hots, n_ref[b, :, :D], (1, 0)).astype(bf16)
            d = matmul(hots, g_ref[b], (1, 0)).astype(bf16)
            for j in range(HOSTED):
                span = pl.ds(pl.multiple_of(j * SLOTS + b * CAP, CAP), CAP)
                xs[span, :] = x[j * CAP : (j + 1) * CAP]
                ds[span, :] = d[j * CAP : (j + 1) * CAP]
            return carry

        lax.fori_loop(0, SOURCES, source, 0)

    @pl.when(step < HOSTED)
    def _():
        expert = base + 2 * step
        rows = pl.ds(pl.multiple_of(step * SLOTS, SLOTS), SLOTS)
        gate = gates[rows, :][:, :1]
        w_gu = w_ref[0, :, : D // 4, :].reshape(D, 2 * FF_E)
        w_d = w_ref[0, :, D // 4 :, :].reshape(FF_E, D)
        gu = matmul(xs[rows, :], w_gu, (1, 0))
        g_part, u_part = gu[:, :FF_E], gu[:, FF_E:]
        sig = 1.0 / (1.0 + jnp.exp(-g_part))
        act = g_part * sig
        hid = (act * u_part).astype(bf16)
        y = matmul(hid, w_d, (1, 0)).astype(bf16).astype(f32)
        dout = ds[rows, :].astype(f32)
        dgate = jnp.sum(y * dout, axis=1, keepdims=True)
        dy = (gate * dout).astype(bf16)
        ds[rows, :] = (gate * y).astype(bf16)
        dh = matmul(dy, w_d, (1, 1))
        da_g = dh * u_part * (sig * (1.0 + g_part * (1.0 - sig)))
        da = jnp.concatenate([da_g, dh * act], axis=1).astype(bf16)
        dw_ref[0, :, D // 4 :, :] = (
            matmul(hid, dy, (0, 0)).astype(bf16).reshape(4, FF_E // 4, D)
        )
        dw_ref[0, :, : D // 4, :] = (
            matmul(xs[rows, :], da, (0, 0)).astype(bf16).reshape(4, D // 4, 2 * FF_E)
        )
        xs[rows, :] = matmul(da, w_gu, (1, 1)).astype(bf16)
        lane = lax.broadcasted_iota(jnp.int32, (SLOTS, 128), 1)
        high = dgate.astype(bf16).astype(f32)
        fields = jnp.where(lane == expert + EXPERTS, dgate - high, 0.0)
        zs[rows, :] = jnp.where(lane == expert, high, fields).astype(bf16)

    @pl.when(step >= HOSTED)
    def _():
        slot = lax.broadcasted_iota(jnp.int32, (TOK, HOSTED * CAP), 1)
        lane = lax.broadcasted_iota(jnp.int32, (TOK, 128), 1)
        for i in range(OUT_BLOCKS):
            b = (step - HOSTED) * OUT_BLOCKS + i
            meta = n_ref[b, :, D:].astype(f32)
            target = jnp.full((TOK, HOSTED * CAP), -1.0, f32)
            for j in reversed(range(HOSTED)):
                mine = lane == base + 2 * j
                rank = jnp.sum(jnp.where(mine, meta, 0.0), axis=1, keepdims=True)
                rank = jnp.where(rank < 0.0, -1.0, rank + j * CAP)
                target = jnp.where(slot < (j + 1) * CAP, rank, target)
            spread = jnp.where(slot.astype(f32) == target, 1.0, 0.0).astype(bf16)
            spans = [pl.ds(pl.multiple_of(j * SLOTS + b * CAP, CAP), CAP) for j in range(HOSTED)]
            for ref, out in ((xs, dn_ref.at[i, :, :D]), (zs, dn_ref.at[i, :, D:]), (ds, out_ref.at[i])):
                rows = jnp.concatenate([ref[span, :] for span in spans], axis=0)
                out[...] = matmul(spread, rows, (1, 0)).astype(bf16)


def experts(n_all, g_all, weights):
    wide = n_all.shape[2]
    slots = HOSTED * SLOTS

    def block(width):
        return pl.BlockSpec(
            (OUT_BLOCKS, TOK, width), lambda i: (jnp.maximum(i - HOSTED, 0), 0, 0)
        )

    def fixed(shape):
        return pl.BlockSpec(shape, lambda i: (0, 0, 0), pipeline_mode=pl.Buffered(1))

    def one(shape):
        return pl.BlockSpec((1,) + shape[1:], lambda i: (jnp.minimum(i, HOSTED - 1), 0, 0, 0))

    return pl.pallas_call(
        expert_kernel,
        grid=(HOSTED + SOURCES // OUT_BLOCKS,),
        out_shape=[
            jax.ShapeDtypeStruct(n_all.shape, bf16),
            jax.ShapeDtypeStruct(g_all.shape, bf16),
            jax.ShapeDtypeStruct(weights.shape, bf16),
        ],
        in_specs=[fixed(n_all.shape), fixed(g_all.shape), one(weights.shape)],
        out_specs=[block(wide), block(D), one(weights.shape)],
        scratch_shapes=[
            pltpu.VMEM((slots, D), bf16),
            pltpu.VMEM((slots, D), bf16),
            pltpu.VMEM((slots, 128), bf16),
            pltpu.VMEM((slots, 128), f32),
        ],
        compiler_params=pltpu.CompilerParams(
            dimension_semantics=("arbitrary",), vmem_limit_bytes=62 * 1024 * 1024
        ),
        cost_estimate=pl.CostEstimate(
            flops=slots * D * FF_E * 18, bytes_accessed=45_000_000, transcendentals=0
        ),
        name="experts",
    )(n_all, g_all, weights)


def turned_rows(u, cos, sin, back):
    lane = lax.broadcasted_iota(jnp.int32, (1, 128), 1)
    first = lax.rem(lane, HEAD_DIM) < HEAD_DIM // 2
    pieces = []
    for j in range(u.shape[1] // 128):
        v = u[:, j * 128 : (j + 1) * 128]
        w = v * sin if back else v
        ahead = pltpu.roll(w, 128 - HEAD_DIM // 2, 1)
        behind = pltpu.roll(w, HEAD_DIM // 2, 1)
        if back:
            pieces.append(v * cos + jnp.where(first, ahead, -behind))
        else:
            pieces.append(v * cos + jnp.where(first, -ahead, behind) * sin)
    return jnp.concatenate(pieces, axis=1)


def unpack_into(out, packed):
    def chunk(i, carry):
        x = packed[pl.ds(i * 16, 16), :, :512].astype(f32)
        rows = pl.ds(pl.multiple_of(i * 128, 128), 128)
        out[rows, :512] = x[:, :8].reshape(128, 512).astype(bf16)
        out[rows, 512:] = x[:, 8:].reshape(128, 512).astype(bf16)
        return carry

    lax.fori_loop(0, 8, chunk, 0)


def gain_rows(small):
    lane = lax.broadcasted_iota(jnp.int32, (8, 128), 1)
    sub = lax.broadcasted_iota(jnp.int32, (8, 128), 0)
    choose = (lane == EXPERTS + sub).astype(f32).astype(bf16)
    return matmul(choose, small, (1, 1))


def fill_bias(bias, length, first_row):
    rows = lax.broadcasted_iota(jnp.int32, bias.shape, 0) + first_row
    keys = lax.broadcasted_iota(jnp.int32, bias.shape, 1)
    bias[...] = jnp.where((keys <= rows) & (keys < length), 0.0, masked_score)


def front_steps(
    z, length, need, wq_p, wkv_p, wo_p, tok, routes, cos, sin, outs, n_held, bias
):
    need, keep = need
    n_out, n1, q_out, kv_out, lse_out, ho_out, r_out, gate_out, wq, wkv, wo, small_out = outs
    width = KV_HEADS * HEAD_DIM
    need("k")
    unpack_into(wkv, wkv_p)

    def small_chunk(i, carry):
        x = wkv_p[pl.ds(i * 16, 16), :, 512:].astype(f32)
        rows = pl.ds(pl.multiple_of(i * 128, 128), 128)
        small_out[rows, :] = x[:, :8].reshape(128, 128).astype(bf16)
        return carry

    lax.fori_loop(0, 8, small_chunk, 0)
    keep("wkv")
    gains = gain_rows(small_out[...])

    def block(by):
        b = lax.rem(z + by, 4)
        x = tok[b].astype(f32)
        normed = (x * rms_scale(x) * gains[0:1]).astype(bf16)
        rows = pl.ds(pl.multiple_of(b * TOK, TOK), TOK)
        n1[rows, :] = normed
        kv = matmul(normed, wkv[...], (1, 0))
        kv_out[rows, :width] = turned_rows(
            kv[:, :width], cos[rows, :], sin[rows, :], False
        ).astype(bf16)
        kv_out[rows, width:] = kv[:, width:].astype(bf16)

    block(0)
    yield
    fill_bias(bias, length[0], z * TOK)
    need("q")
    unpack_into(wq, wq_p)
    keep("wq")
    own = pl.ds(pl.multiple_of(z * TOK, TOK), TOK)
    q = matmul(n1[own, :], wq[...], (1, 0))
    q = turned_rows(q, cos[own, :], sin[own, :], False).astype(bf16)
    q_out[...] = q * jnp.asarray(HEAD_DIM ** (-0.5), bf16)
    lse_out[...] = jnp.zeros_like(lse_out)
    lane = lax.broadcasted_iota(jnp.int32, (TOK, 128), 1)
    yield
    need("t")
    for by in (1, 3, 2):
        block(by)
        yield
    keep("n1")
    keep("kv")

    def heads(j):
        keys = kv_out[:, pl.ds(j * 128, 128)]
        values = kv_out[:, pl.ds(width + j * 128, 128)]
        for g in (0, 1):
            span = pl.ds(j * 256 + g * 128, 128)
            qs = q_out[:, span]
            key = keys[:, g * HEAD_DIM : (g + 1) * HEAD_DIM]
            value = values[:, g * HEAD_DIM : (g + 1) * HEAD_DIM]
            mixed = []
            for h in (0, 1):
                s = matmul(qs[:, h * HEAD_DIM : (h + 1) * HEAD_DIM], key, (1, 1)) + bias[...]
                top = jnp.max(s, axis=1, keepdims=True)
                p = jnp.exp(s - top)
                total = jnp.sum(p, axis=1, keepdims=True)
                p = (p * (1.0 / total)).astype(bf16)
                mixed.append(matmul(p, value, (1, 0)))
                head = j * 4 + g * 2 + h
                lse_out[...] = jnp.where(lane == head, top + jnp.log(total), lse_out[...])
            ho_out[:, span] = jnp.concatenate(mixed, axis=1).astype(bf16)

    for j in range(4):
        heads(j)
        yield
    need("o")
    unpack_into(wo, wo_p)
    keep("wo")
    r = tok[z].astype(f32) + matmul(ho_out[...], wo[...], (1, 0))
    r_out[...] = r
    n2 = (r * rms_scale(r) * gains[1:2]).astype(bf16)
    n_out[:, :D] = n2
    n_held[:, :D] = n2
    logits = matmul(n2, small_out[...], (1, 0))
    hits = lane == routes[:, 0:1]
    for k in range(1, routes.shape[1]):
        hits = hits | (lane == routes[:, k : k + 1])
    lifted = jnp.where(hits, logits, masked_score)
    lifted = jnp.where(hits, jnp.exp(lifted - jnp.max(lifted, axis=1, keepdims=True)), 0.0)
    gate = lifted / jnp.sum(lifted, axis=1, keepdims=True)
    gate_out[...] = gate
    row = lax.broadcasted_iota(jnp.int32, (TOK, TOK), 0)
    col = lax.broadcasted_iota(jnp.int32, (TOK, TOK), 1)
    earlier = jnp.where(col < row, 1.0, 0.0).astype(bf16)
    ranks = matmul(earlier, jnp.where(hits, 1.0, 0.0).astype(bf16), (1, 0))
    high = gate.astype(bf16).astype(f32)
    meta = jnp.where(hits, ranks, jnp.where(lane < EXPERTS, -1.0, 0.0))
    meta = meta + pltpu.roll(high, EXPERTS, 1) + pltpu.roll(gate - high, 2 * EXPERTS, 1)
    meta = meta.astype(bf16)
    n_out[:, D:] = meta
    n_held[:, D:] = meta


GATHER_ORDERS = {"k": "zyx", "q": "zxy", "o": "zyx"}
FRONT_SCHEDULE = "kqtodkqokqotkqdokqotdfqofdffodffffdffff"


def front_kernel(
    length, tok, dout, w_kv, w_q, w_o, small, routes, cos, sin,
    n_out, q_out, lse_out, ho_out, r_out, gate_out, small_out,
    n1_far, kv_far, wq_far, wkv_far, wo_far, tok_far, dout_far, n_all,
    n1, kv, wq, wkv, wo,
    wkv_p, wq_p, wo_p, tok_held, dout_held, n_held, bias, *sems,
):
    at = place()
    wires = Wires(*sems)
    own_tok = wires.keep(tok, tok_held.at[at["z"]])
    own_dout = wires.keep(dout, dout_held.at[at["x"], at["c"]])
    steps = {}
    for name, src, out in (("k", w_kv, wkv_p), ("q", w_q, wq_p), ("o", w_o, wo_p)):
        block = out.at[index(at, "")]
        block[:, :512] = jnp.concatenate([src[:, :512], src[:, 512:]], axis=0).astype(bf16)
        if name == "k":
            block[:, 512:] = small[...].astype(bf16)
        steps[name] = weight_steps(wires, at, [(out, GATHER_ORDERS[name])])
    steps["t"] = token_steps(wires, at, tok_held)
    steps["d"] = row_steps(wires, at, dout_held, dout_far)
    flat = [p.reshape(128, *p.shape[-2:]) for p in (wq_p, wkv_p, wo_p)]
    outs = (n_out, n1, q_out, kv, lse_out, ho_out, r_out, gate_out, wq, wkv, wo, small_out)
    kept = []
    results = {
        "n1": (n1, n1_far),
        "kv": (kv, kv_far),
        "wq": (wq, wq_far),
        "wkv": (wkv, wkv_far),
        "wo": (wo, wo_far),
    }

    def need(name):
        for _ in steps[name]:
            pass
        if name == "t":
            kept.append(wires.keep(tok_held, tok_far))

    def keep(name):
        kept.append(wires.keep(*results[name]))

    steps["f"] = front_steps(
        at["z"], length, (need, keep), *flat, tok_held, routes, cos, sin, outs,
        n_held.at[at["x"], at["c"]], bias,
    )
    greet(at, "xyzc")
    own_tok.wait()
    own_dout.wait()
    in_order(FRONT_SCHEDULE, **steps)
    in_order("", n=row_steps(wires, at, n_held, n_all))
    for copy in kept:
        copy.wait()
    wires.finish()


def front(length, w_kv, w_q, w_o, small, tok, dout, routes, cos, sin):
    vmem = pl.BlockSpec(memory_space=pltpu.VMEM)
    far = pl.BlockSpec(memory_space=pltpu.HBM)
    rows = jax.ShapeDtypeStruct((TOK, D), bf16)
    lanes = jax.ShapeDtypeStruct((TOK, 128), f32)
    lead = (4, 4, 2, 4)
    copies = WEIGHT_COPIES + TOKEN_COPIES + 2 * ROW_COPIES
    return pl.pallas_call(
        front_kernel,
        out_shape=[
            jax.ShapeDtypeStruct((TOK, D + 128), bf16),
            rows,
            lanes,
            rows,
            jax.ShapeDtypeStruct((TOK, D), f32),
            lanes,
            jax.ShapeDtypeStruct((D, 128), bf16),
        ]
        + [pltpu.HBM((D, D), bf16)] * 5
        + [
            pltpu.HBM((4, TOK, D), bf16),
            pltpu.HBM((4, 2, TOK, D), bf16),
            pltpu.HBM((4, 2, TOK, D + 128), bf16),
        ],
        in_specs=[pl.BlockSpec(memory_space=pltpu.SMEM)] + [far] * 2 + [vmem] * 7,
        out_specs=[vmem] * 7 + [far] * 8,
        scratch_shapes=[pltpu.VMEM((D, D), bf16)] * 5
        + [
            pltpu.VMEM(lead + (16, 512 + 128), bf16),
            pltpu.VMEM(lead + (16, 512), bf16),
            pltpu.VMEM(lead + (16, 512), bf16),
            pltpu.VMEM((4, TOK, D), bf16),
            pltpu.VMEM((4, 2, TOK, D), bf16),
            pltpu.VMEM((4, 2, TOK, D + 128), bf16),
            pltpu.VMEM((TOK, 4 * TOK), f32),
        ]
        + wire_sems(copies, 2 + 6 + 2 * ROW_KEPT),
        compiler_params=pltpu.CompilerParams(
            collective_id=1, has_side_effects=True, vmem_limit_bytes=60 * 1024 * 1024
        ),
        cost_estimate=pl.CostEstimate(
            flops=10**10, bytes_accessed=30_000_000, transcendentals=5_000_000
        ),
        name="front",
    )(length, *hbm(tok, dout), w_kv, w_q, w_o, small, routes, cos, sin)


def rms_back(values, scale, gain, dnormed):
    scaled = values * scale
    dscaled = dnormed * gain
    dvalues = scale * (dscaled - scaled * jnp.mean(dscaled * scaled, axis=-1, keepdims=True))
    return dvalues, jnp.sum(dnormed * scaled, axis=0, keepdims=True)


def pack_into(out, value):
    def chunk(i, carry):
        rows = pl.ds(pl.multiple_of(i * 128, 128), 128)
        left = value[rows, :512].reshape(16, 8, 512)
        right = value[rows, 512:].reshape(16, 8, 512)
        out[pl.ds(i * 16, 16), :, :512] = jnp.concatenate([left, right], axis=1).astype(bf16)
        return carry

    lax.fori_loop(0, 8, chunk, 0)


def back_steps(
    z, length, sums, dout, n_ext, r_ref, gate_ref, ho, q_ref, kv, lse, n1, wo, small,
    cos, sin, cos_t, sin_t, late,
    dwq_p, dwkv_p, dwo_p, dg_p, dn1_out, dr_out,
    bias, square, dq_s, do_s, dkv_s,
):
    own = pl.ds(pl.multiple_of(z * TOK, TOK), TOK)
    gains = gain_rows(small[...])
    lane = lax.broadcasted_iota(jnp.int32, (TOK, 128), 1)
    gate = gate_ref[...]
    fields = sums[:, D:]
    dgate = fields + pltpu.roll(fields, 128 - EXPERTS, 1)
    mean = jnp.sum(gate * dgate, axis=1, keepdims=True)
    dlogits = (gate * (dgate - mean)).astype(bf16)
    dn2 = sums[:, :D] + matmul(dlogits, small[...], (1, 1))
    r = r_ref[...]
    dr, dg2 = rms_back(r, rms_scale(r), gains[1:2], dn2)
    dr = dr + dout[...].astype(f32)
    dr_out[...] = dr
    d_att = dr.astype(bf16)
    square[...] = matmul(ho[...], d_att, (0, 0))
    pack_into(dwo_p, square)
    spread_gain(dwo_p.at[:, :, 512:], dg2, EXPERTS, matmul(n_ext[:, :D], dlogits, (0, 0)))
    yield
    do_s[...] = matmul(d_att, wo[...], (1, 1)).astype(bf16)
    fill_bias(bias, length[0], z * TOK)
    width = KV_HEADS * HEAD_DIM
    scale = HEAD_DIM ** (-0.5)
    dkv_t = square

    def heads(j):
        keys = kv[:, pl.ds(j * 128, 128)]
        values = kv[:, pl.ds(width + j * 128, 128)]
        for g in (0, 1):
            span = pl.ds(j * 256 + g * 128, 128)
            qs, dos = q_ref[:, span], do_s[:, span]
            prods = dos.astype(f32) * ho[:, span].astype(f32)
            key = keys[:, g * HEAD_DIM : (g + 1) * HEAD_DIM]
            value = values[:, g * HEAD_DIM : (g + 1) * HEAD_DIM]
            dqs = []
            dk_t, dv_t = 0.0, 0.0
            for h in (0, 1):
                part = slice(h * HEAD_DIM, (h + 1) * HEAD_DIM)
                head = j * 4 + g * 2 + h
                shift_by = jnp.sum(jnp.where(lane == head, lse[...], 0.0), axis=1, keepdims=True)
                mine = (lane >= h * HEAD_DIM) & (lane < (h + 1) * HEAD_DIM)
                delta = jnp.sum(jnp.where(mine, prods, 0.0), axis=1, keepdims=True)
                p = jnp.exp(matmul(qs[:, part], key, (1, 1)) + bias[...] - shift_by)
                dp = matmul(dos[:, part], value, (1, 1))
                ds = (p * (dp - delta)).astype(bf16)
                dqs.append(matmul(ds, key, (1, 0)) * scale)
                dk_t = dk_t + matmul(qs[:, part], ds, (0, 0))
                dv_t = dv_t + matmul(dos[:, part], p.astype(bf16), (0, 0))
            dq_s[:, span] = jnp.concatenate(dqs, axis=1)
            half = HEAD_DIM // 2
            wave = dk_t * sin_t[...]
            dk_t = dk_t * cos_t[...] + jnp.concatenate([wave[half:], -wave[:half]], axis=0)
            at = j * 128 + g * HEAD_DIM
            dkv_t[pl.ds(at, HEAD_DIM), :] = dk_t
            dkv_t[pl.ds(width + at, HEAD_DIM), :] = dv_t

    for j in range(4):
        heads(j)
        yield

    def flip(i, carry):
        at = pl.ds(pl.multiple_of(i * 128, 128), 128)
        dkv_s[:, at] = jnp.transpose(dkv_t[at, :]).astype(bf16)
        return carry

    lax.fori_loop(0, 8, flip, 0)
    square[...] = matmul(n1[...], dkv_s[...], (0, 0))
    pack_into(dwkv_p, square)
    yield
    dq = turned_rows(dq_s[...], cos[...], sin[...], True).astype(bf16)
    square[...] = matmul(n1[own, :], dq, (0, 0))
    pack_into(dwq_p, square)
    yield
    wq, wkv, tok = late()
    for b in range(4):
        columns = slice(b * TOK, (b + 1) * TOK)
        square[:, columns] = matmul(dkv_s[...], wkv[b, :, :D], (1, 1))
        square[own, columns] += matmul(dq, wq[b, :, :D], (1, 1))
    for b in range(4):
        dn1_out[b] = square[b * TOK : (b + 1) * TOK, :].astype(bf16)
    yield
    dg1 = jnp.zeros((1, D), f32)
    for b in range(4):
        x = tok[b, :, :D].astype(f32)
        dn1 = square[b * TOK : (b + 1) * TOK, :]
        dg1 = dg1 + jnp.sum(dn1 * (x * rms_scale(x)), axis=0, keepdims=True)
    spread_gain(dg_p, dg1, 0, None)


def spread_gain(out, row, lane, rest):
    sub = lax.broadcasted_iota(jnp.int32, (8, D), 0)
    rows = jnp.where(sub == 0, row, 0.0)
    high = rows.astype(bf16)
    low = (rows - high.astype(f32)).astype(bf16)
    place_lane = lax.broadcasted_iota(jnp.int32, (8, 128), 1)
    place_sub = lax.broadcasted_iota(jnp.int32, (8, 128), 0)
    spread = jnp.where((place_lane == lane) & (place_sub == 0), 1.0, 0.0).astype(bf16)
    value = matmul(high, spread, (0, 0)) + matmul(low, spread, (0, 0))
    if rest is not None:
        value = value + rest
    value = value.reshape(128, 8, 128)
    out[...] = jnp.concatenate([value, jnp.zeros_like(value)], axis=1).astype(bf16)


BACK_INPUTS = 15
BACK_ORDERS = {"a": "xyz", "k": "xzy", "o": "xyz", "g": "xyz"}


def back_kernel(length, dn_parts, out_parts, wq, wkv, tok, *refs):
    loaded = refs[:BACK_INPUTS]
    refs = refs[BACK_INPUTS:]
    g_q, g_kv, g_o, g_small, g_g, dr_out, layer_out = refs[:7]
    sums, dn1, bias, square, dq_s, do_s, dkv_s = refs[7:14]
    mixed = sums.at[:, pl.ds(0, D)]
    dn_bufs, out_bufs, dn1_bufs = refs[14:19], refs[19:24], refs[24:27]
    q_bufs, kv_bufs, o_bufs, g_bufs = (refs[27 + 7 * i : 34 + 7 * i] for i in range(4))
    inputs = refs[55 : 55 + BACK_INPUTS]
    dn1_sum = refs[55 + BACK_INPUTS]
    at = place()
    wires = Wires(*refs[56 + BACK_INPUTS :])

    def unpacked(out, small=None):
        def write(value):
            out[:, :512] = value[:8, :512]
            out[:, 512:] = value[8:, :512]
            if small is not None:
                small[...] = value[:8, 512:]

        return write

    def gain_column(value):
        g_g[...] = value[:8]
    greet(at, "xyzc")

    def backward():
        for copy in arriving:
            copy.wait()
        wires.finish()
        yield from back_steps(
            at["z"], length, sums, *inputs, late,
            *(bufs[0].reshape(128, *bufs[0].shape[-2:]) for bufs in (q_bufs, kv_bufs, o_bufs, g_bufs)),
            dn1, dr_out, bias, square, dq_s, do_s, dkv_s,
        )

    late_spots = (out_bufs[1], dn_bufs[0], dn_bufs[1])
    late_copies = []

    def load_late():
        for src, dst in ((wkv, dn_bufs[0]), (tok, dn_bufs[1]), (wq, out_bufs[1])):
            late_copies.append(wires.keep(src, dst.at[:, :, pl.ds(0, D)]))
        yield

    def late():
        for copy in late_copies:
            copy.wait()
        return late_spots

    steps = {
        "n": row_sum_steps(wires, at, dn_parts, sums, *dn_bufs),
        "l": row_sum_steps(wires, at, out_parts, mixed, *out_bufs),
        "z": ring_sum_steps(wires, at, "z", dn1, dn1_sum, *dn1_bufs),
        "a": matrix_steps(wires, at, BACK_ORDERS["a"], q_bufs[0], unpacked(g_q), *q_bufs[1:]),
        "k": matrix_steps(wires, at, BACK_ORDERS["k"], kv_bufs[0], unpacked(g_kv), *kv_bufs[1:]),
        "o": matrix_steps(wires, at, BACK_ORDERS["o"], o_bufs[0], unpacked(g_o, g_small), *o_bufs[1:]),
        "g": matrix_steps(wires, at, BACK_ORDERS["g"], g_bufs[0], gain_column, *g_bufs[1:]),
        "e": load_late(),
        "b": backward(),
    }
    next(steps["n"])
    own = pl.ds(pl.multiple_of(at["z"] * TOK, TOK), TOK)
    arriving = [
        wires.keep(src.at[own] if src.shape != dst.shape else src, dst)
        for src, dst in zip(loaded, inputs)
    ]
    in_order(BACK_SCHEDULE, **steps)
    residual, small = inputs[2], inputs[10]
    layer_out[...] = (residual[...] + mixed[...]).astype(bf16)
    x = late_spots[2][at["z"], :, :D].astype(f32)
    dx, _ = rms_back(x, rms_scale(x), gain_rows(small[...])[0:1], dn1_sum[...])
    dr_out[...] += dx
    wires.finish()


BACK_SCHEDULE = "l" + "nnnn" + "bo" + "le" + "bo" + "b" + "b" + "bl" + "bk" + "bak" + "bzao" + "bg" + "zkgkoagakgolz"


def back(length, dn_parts, out_parts, wq, wkv, tok, *inputs):
    vmem = pl.BlockSpec(memory_space=pltpu.VMEM)
    far = pl.BlockSpec(memory_space=pltpu.HBM)
    wide = dn_parts.shape[-1]
    widths = (512, 512, 640, 128)
    copies = 2 * ROW_SUM_COPIES + RING_SUM_COPIES + 4 * MATRIX_COPIES
    scratch = [
        pltpu.VMEM((TOK, wide), f32),
        pltpu.VMEM((4, TOK, D), bf16),
        pltpu.VMEM((TOK, 4 * TOK), f32),
        pltpu.VMEM((D, D), f32),
        pltpu.VMEM((TOK, D), f32),
        pltpu.VMEM((TOK, D), bf16),
        pltpu.VMEM((D, D), bf16),
    ]
    scratch += row_sum_scratch(TOK, wide) + row_sum_scratch(TOK, D) + ring_sum_scratch(TOK, D)
    for width in widths:
        scratch += matrix_scratch(width)
    scratch += [
        pltpu.VMEM((TOK, 128) if v.shape == (4 * TOK, 128) and v.dtype == f32 else v.shape, v.dtype)
        for v in inputs
    ]
    scratch.append(pltpu.VMEM((TOK, D), f32))
    return pl.pallas_call(
        back_kernel,
        out_shape=[jax.ShapeDtypeStruct((8, D), f32)] * 3
        + [jax.ShapeDtypeStruct((8, 128), f32)] * 2
        + [jax.ShapeDtypeStruct((TOK, D), f32), jax.ShapeDtypeStruct((TOK, D), bf16)],
        in_specs=[pl.BlockSpec(memory_space=pltpu.SMEM)] + [far] * (5 + BACK_INPUTS),
        out_specs=[vmem] * 7,
        scratch_shapes=scratch + wire_sems(copies, 8 + 3 + BACK_INPUTS),
        compiler_params=pltpu.CompilerParams(
            collective_id=4, has_side_effects=True, vmem_limit_bytes=63 * 1024 * 1024
        ),
        cost_estimate=pl.CostEstimate(
            flops=2 * 10**10, bytes_accessed=40_000_000, transcendentals=5_000_000
        ),
        name="back",
    )(length, *hbm(dn_parts, out_parts, wq, wkv, tok, *inputs))


def rotary_constants(count):
    half = HEAD_DIM // 2
    freqs = (10000.0 ** (-np.arange(half, dtype=np.float64) / half)).astype(np.float32)
    angles = np.arange(count, dtype=np.float32)[:, None] * freqs[None, :]
    tables = np.cos(angles.astype(np.float64)), np.sin(angles.astype(np.float64))
    return tuple(np.concatenate([t, t], 1).astype(np.float32) for t in tables)


def body(
    tokens, routes, lengths, out_grad,
    query_weight, query_mean, query_square,
    keyval_weight, keyval_mean, keyval_square,
    output_weight, output_mean, output_square,
    router_weight, router_mean, router_square,
    norm_gains, gains_mean, gains_square,
    gateup_weight, gateup_mean, gateup_square,
    down_weight, down_mean, down_square,
):
    row_count = tokens.shape[0]
    seq_len = row_count * 4
    query_width = HEADS * HEAD_DIM

    expert_b = lax.all_gather(
        jnp.concatenate([gateup_weight[0], down_weight[0]], axis=0).astype(bf16),
        ("y", "z"),
        axis=0,
    )
    small = jnp.concatenate(
        [router_weight, norm_gains.T, jnp.zeros((8, 128 - EXPERTS - 2), f32)], axis=1
    )
    small = jnp.concatenate([small, jnp.zeros((8, 128), f32)], axis=0)
    cos, sin = rotary_constants(seq_len)
    cos2, sin2, cos_t, sin_t = (
        jnp.asarray(table)
        for table in (np.tile(cos, (1, 2)), np.tile(sin, (1, 2)), cos.T.copy(), sin.T.copy())
    )
    (
        n_ext, q, lse, ho, residual, gate, small_b,
        n1, kv, query_b, keyval_b, output_b, all_tokens, dout_all, n_all,
    ) = front(
        lengths,
        keyval_weight,
        query_weight,
        output_weight,
        small,
        tokens,
        out_grad,
        routes,
        cos2,
        sin2,
    )
    wide = n_all.shape[-1]
    n_all = n_all.reshape(SOURCES, row_count, wide)
    dn_parts, out_parts, d_expert = experts(
        n_all,
        dout_all.reshape(SOURCES, row_count, D),
        expert_b.reshape((4,) + (4, D // 4 + FF_E // 4, D)),
    )
    grad_expert = lax.psum_scatter(
        d_expert.reshape((16,) + d_expert.shape[2:]),
        ("y", "z"),
        scatter_dimension=0,
        tiled=False,
    ).astype(f32)
    grad_query, grad_keyval, grad_output, g_small, g_gain, tokens_grad, layer_out = back(
        lengths,
        dn_parts.reshape(4, 2, row_count, wide),
        out_parts.reshape(4, 2, row_count, D),
        query_b.reshape(4, row_count, D),
        keyval_b.reshape(4, row_count, D),
        all_tokens,
        out_grad, n_ext, residual, gate, ho, q, kv, lse, n1, output_b, small_b,
        cos2, sin2, cos_t, sin_t,
    )
    grad_router = g_small[:, :EXPERTS]
    grad_gains = jnp.stack([g_gain[:, 0], g_small[:, EXPERTS]])

    rate = 0.5
    query_new = adamw(query_weight, grad_query, query_mean, query_square, rate * D ** (-0.5), 0.1)
    keyval_new = adamw(
        keyval_weight, grad_keyval, keyval_mean, keyval_square, rate * D ** (-0.5), 0.1
    )
    output_new = adamw(
        output_weight,
        grad_output,
        output_mean,
        output_square,
        rate * max(1, 2 * query_width // seq_len) ** (-0.5),
        0.1,
    )
    router_new = adamw(
        router_weight, grad_router, router_mean, router_square, rate * (4 * D) ** (-0.5), 0.1
    )
    gains_new = adamw(norm_gains, grad_gains, gains_mean, gains_square, 0.6, 0.0)
    gateup_new = adamw(
        gateup_weight,
        grad_expert[None, : D // 4],
        gateup_mean,
        gateup_square,
        rate * D ** (-0.5),
        0.1,
    )
    down_new = adamw(
        down_weight,
        grad_expert[None, D // 4 :],
        down_mean,
        down_square,
        rate * (FF_E // 8) ** (-0.5),
        0.1,
    )
    return (
        (layer_out, tokens_grad)
        + query_new
        + keyval_new
        + output_new
        + router_new
        + gains_new
        + gateup_new
        + down_new
    )


def solution(mesh):
    devices = jax.sharding.Mesh(mesh.devices.reshape(4, 4, 2, 4), ("x", "y", "c", "z"))
    every = ("x", "y", "c", "z")
    rows = P(every, None)
    gains = P(None, every)
    shard = P(("x", "y", "c"), "z", None)
    return jax.shard_map(
        body,
        mesh=devices,
        in_specs=(rows, rows, P(("x", "y", "c")), rows)
        + (rows,) * 12
        + (gains,) * 3
        + (shard,) * 6,
        out_specs=(rows, rows) + (rows,) * 12 + (gains,) * 3 + (shard,) * 6,
        check_vma=False,
    )
```

```python
import jax
import jax.numpy as jnp
import numpy as np
from jax import lax
from jax.experimental import pallas as pl
from jax.experimental.pallas import tpu as pltpu
from jax.sharding import PartitionSpec as P

MESH = pl.DeviceIdType.MESH
bf16 = jnp.bfloat16
f32 = jnp.float32
AXES = "xycz"
STRIP = 16


def place():
    return {a: lax.axis_index(a) for a in AXES}


def device(at):
    return tuple(at[a] for a in AXES)


def shift(at, axis, by):
    size = 2 if axis == "c" else 4
    return lax.rem(at[axis] + by, size)


def peer(at, axis, by):
    return device({**at, axis: shift(at, axis, by)})


def greet(at, axes):
    barrier = pltpu.get_barrier_semaphore()
    count = 0
    for axis in axes:
        for by in (1,) if axis == "c" else (1, 2, 3):
            pl.semaphore_signal(
                barrier, inc=1, device_id=peer(at, axis, by), device_id_type=MESH
            )
            count += 1
    pl.semaphore_wait(barrier, count)


class Wires:
    def __init__(self, send_sems, recv_sems, local_sems):
        self.send_sems, self.recv_sems, self.local_sems = send_sems, recv_sems, local_sems
        self.copies, self.sent, self.local = [], 0, 0

    def send(self, src, dst, target):
        at = self.sent
        self.sent += 1
        copy = pltpu.make_async_remote_copy(
            src_ref=src,
            dst_ref=dst,
            send_sem=self.send_sems.at[at],
            recv_sem=self.recv_sems.at[at],
            device_id=target,
            device_id_type=MESH,
        )
        copy.start()
        self.copies.append(copy)
        return copy

    def keep(self, src, dst):
        copy = pltpu.make_async_copy(src, dst, self.local_sems.at[self.local])
        copy.start()
        self.local += 1
        return copy

    def let_go(self, *copies):
        for copy in copies:
            copy.wait_send()
        self.copies = [c for c in self.copies if all(c is not copy for copy in copies)]

    def finish(self):
        for copy in self.copies:
            copy.wait_send()
        self.copies = []


def wire_sems(copies, kept):
    return [
        pltpu.SemaphoreType.DMA((copies,)),
        pltpu.SemaphoreType.DMA((copies,)),
        pltpu.SemaphoreType.DMA((kept,)),
    ]


def in_order(order, **steps):
    for letter in order:
        next(steps[letter], None)
    for step in steps.values():
        for _ in step:
            pass


def hbm(*arrays):
    return [pltpu.with_memory_space_constraint(v, pltpu.HBM) for v in arrays]


def ring_steps(wires, at, axis, spot, hand_on, patient=False):
    right, left = peer(at, axis, 1), peer(at, axis, 3)
    to_right = {0: wires.send(spot(0, 0), spot(0, 0), right)}
    to_left = {1: wires.send(spot(0, 1), spot(0, 1), left)}
    for k in (0, 1):
        hand_on(0, k)
    if patient:
        wires.let_go(to_right[0], to_left[1])
    to_right[1] = wires.send(spot(0, 1), spot(0, 1), right)
    to_left[0] = wires.send(spot(0, 0), spot(0, 0), left)
    yield
    to_right[0].wait_recv()
    far_right = wires.send(spot(3, 0), spot(3, 0), right)
    hand_on(3, 0)
    to_left[1].wait_recv()
    far_left = wires.send(spot(1, 1), spot(1, 1), left)
    hand_on(1, 1)
    yield
    to_right[1].wait_recv()
    hand_on(3, 1)
    to_left[0].wait_recv()
    hand_on(1, 0)
    yield
    far_right.wait_recv()
    hand_on(2, 0)
    far_left.wait_recv()
    hand_on(2, 1)


def row_steps(wires, at, held, out, patient=False):
    half = held.shape[2] // 2
    sibling = peer(at, "c", 1)
    other = shift(at, "c", 1)
    across, kept = [], []

    def hand_on(by, part):
        rows = pl.ds(part * half, half)
        unit, theirs = (
            (shift(at, "x", by), c, rows) for c in (at["c"], other)
        )
        across.append((theirs, wires.send(held.at[unit], held.at[unit], sibling)))
        kept.append(wires.keep(held.at[unit], out.at[unit]))

    def spot(by, part):
        return held.at[shift(at, "x", by), at["c"], pl.ds(part * half, half)]

    yield from ring_steps(wires, at, "x", spot, hand_on, patient)
    yield
    for unit, copy in across:
        copy.wait_recv()
        kept.append(wires.keep(held.at[unit], out.at[unit]))
    for copy in kept:
        copy.wait()


ROW_KEPT = 16
ROW_COPIES = 6 + 8


def token_steps(wires, at, held):
    half = held.shape[1] // 2

    def spot(by, part):
        return held.at[shift(at, "z", by), pl.ds(part * half, half)]

    yield from ring_steps(wires, at, "z", spot, lambda by, part: None)


TOKEN_COPIES = 6


def index(at, whole, **fixed):
    spots = {**at, **{a: slice(None) for a in whole}, **fixed}
    return tuple(spots[axis] for axis in AXES)


def weight_steps(wires, at, parts):
    arrivals = {}
    for p, (o, order) in enumerate(parts):
        own = o.at[index(at, "")]
        for by in (1, 3, 2):
            arrivals[p, by] = wires.send(own, own, peer(at, order[0], by))
    yield
    later = {}
    for p, (o, order) in enumerate(parts):
        for by in (1, 3, 2):
            arrivals[p, by].wait_recv()
        spot = index(at, order[0])
        for by in (1, 3, 2):
            later[p, by] = wires.send(o.at[spot], o.at[spot], peer(at, order[1], by))
    yield
    sibling = peer(at, "c", 1)
    across, rings = [], []
    for p, (o, order) in enumerate(parts):
        for by in (1, 3, 2):
            later[p, by].wait_recv()

        def spot(by, part, o=o, order=order):
            pieces = {order[1]: pl.ds(2 * part, 2), order[2]: shift(at, order[2], by)}
            return o.at[index(at, order[0], **pieces)]

        def hand_on(by, part, spot=spot):
            across.append(wires.send(spot(by, part), spot(by, part), sibling))

        ring = ring_steps(wires, at, order[2], spot, hand_on)
        next(ring)
        rings.append(ring)
    yield
    for _ in range(3):
        for ring in rings:
            next(ring, None)
        yield
    for copy in across:
        copy.wait_recv()


WEIGHT_COPIES = 3 * (3 + 3 + 6 + 8)


def add_rows(out, parts, rows):
    def strip(i, carry):
        span = pl.ds(pl.multiple_of(i * STRIP, STRIP), STRIP)
        total = parts[0][span].astype(f32)
        for part in parts[1:]:
            total = total + part[span].astype(f32)
        out[span] = total.astype(out.dtype)
        return carry

    lax.fori_loop(0, rows // STRIP, strip, 0)


def ring_sum_steps(wires, at, axis, blocks, out, mid, last, near):
    half = out.shape[0] // 2
    low, high = pl.ds(0, half), pl.ds(half, half)
    ahead, back, far = (blocks.at[shift(at, axis, by)] for by in (1, 3, 2))
    right, left = peer(at, axis, 1), peer(at, axis, 3)
    near_l = wires.send(far.at[low], near.at[0], right)
    near_r = wires.send(far.at[high], near.at[1], left)
    yield
    pure_l = wires.send(ahead.at[high], last.at[0, high], right)
    pure_r = wires.send(back.at[low], last.at[1, low], left)
    yield
    near_l.wait_recv()
    add_rows(mid.at[0], [ahead.at[low], near.at[0]], half)
    sum_l = wires.send(mid.at[0], last.at[0, low], right)
    near_r.wait_recv()
    add_rows(mid.at[1], [back.at[high], near.at[1]], half)
    sum_r = wires.send(mid.at[1], last.at[1, high], left)
    yield
    for copy in (pure_l, sum_l, pure_r, sum_r):
        copy.wait_recv()
    add_rows(out, [blocks.at[at[axis]], last.at[0], last.at[1]], 2 * half)


def ring_sum_scratch(rows, width):
    return [
        pltpu.VMEM((2, rows // 2, width), bf16),
        pltpu.VMEM((2, rows, width), bf16),
        pltpu.VMEM((2, rows // 2, width), bf16),
    ]


def row_sum_steps(wires, at, c_ref, out, held, crossed, mid, last, near):
    other = shift(at, "c", 1)
    sibling = peer(at, "c", 1)
    rows = out.shape[0]
    crossing, kept = {}, {}
    for by in (2, 1, 3, 0):
        i = shift(at, "x", by)
        crossing[by] = wires.send(c_ref.at[i, other], crossed.at[i], sibling)
        kept[by] = wires.keep(c_ref.at[i, at["c"]], held.at[i])
    yield
    for by in (2, 1, 3, 0):
        i = shift(at, "x", by)
        kept[by].wait()
        crossing[by].wait_recv()
        add_rows(held.at[i], [held.at[i], crossed.at[i]], rows)
        if by == 2:
            ring = ring_sum_steps(wires, at, "x", held, out, mid, last, near)
        if by in (2, 3):
            next(ring)
    yield
    yield from ring


ROW_SUM_COPIES = 4 + 6


def row_sum_scratch(rows, width):
    return [pltpu.VMEM((4, rows, width), bf16)] * 2 + ring_sum_scratch(rows, width)


def matrix_steps(wires, at, order, pack, write, crossed, one, two, three, sum1, sum2):
    axis, after, end = order
    crossing = wires.send(
        pack.at[:, :, shift(at, "c", 1)], crossed, peer(at, "c", 1)
    )

    def own(by):
        return pack.at[index(at, "xyz", **{axis: shift(at, axis, by)})]

    def later(by):
        rest = "xyz".replace(axis, "")
        return sum1.at[tuple(shift(at, a, by) if a == after else slice(None) for a in rest)]

    def total(out, parts, count):
        def body(i, carry):
            value = parts[0][i].astype(f32)
            for part in parts[1:]:
                value = value + part[i].astype(f32)
            out[i] = value.astype(out.dtype)
            return carry

        lax.fori_loop(0, count, body, 0)

    def spread(parts, slots, along):
        return [wires.send(parts(by), slots.at[by - 1], peer(at, along, by)) for by in (2, 1, 3)]

    yield
    crossing.wait_recv()

    def body(i, carry):
        spot = (i // 4, i % 4)
        mine = pack[spot + (at["c"],)].astype(f32) + crossed[spot].astype(f32)
        pack[spot + (at["c"],)] = mine.astype(bf16)
        return carry

    lax.fori_loop(0, 16, body, 0)
    copies = spread(own, one, axis)
    yield
    for copy in copies:
        copy.wait_recv()
    total(sum1, [own(0)] + [one.at[k] for k in range(3)], 4)
    copies = spread(later, two, after)
    yield
    for copy in copies:
        copy.wait_recv()
    total(sum2, [later(0)] + [two.at[k] for k in range(3)], 4)
    copies = spread(lambda by: sum2.at[shift(at, end, by)], three, end)
    yield
    for copy in copies:
        copy.wait_recv()
    value = sum2[at[end]].astype(f32)
    for k in range(3):
        value = value + three[k].astype(f32)
    write(value)


MATRIX_COPIES = 10
RING_SUM_COPIES = 6


def matrix_scratch(width):
    leads = ((4, 4, 2, 4), (4, 4, 4), (3, 4, 4), (3, 4), (3,), (4, 4), (4,))
    return [pltpu.VMEM(lead + (16, width), bf16) for lead in leads]


D = 1024
HEADS = 16
KV_HEADS = 8
HEAD_DIM = 64
EXPERTS = 32
FF_E = 512
STEP = 10
CAP = 96
TOK = 256


norm_epsilon = 1e-06
beta_first = 0.9
beta_second = 0.95
adam_epsilon = 1e-08
masked_score = -1e30


def rotary_tables(positions, half_width):
    freqs = 10000.0 ** (-jnp.arange(half_width, dtype=jnp.float32) / half_width)
    angles = positions.astype(jnp.float32)[:, None] * freqs[None, :]
    cosines = jnp.cos(angles)
    sines = jnp.sin(angles)
    return (jnp.concatenate([cosines, cosines], 1), jnp.concatenate([sines, sines], 1))


def rotate(values, cosines, sines):
    half_width = values.shape[-1] // 2
    turned = jnp.concatenate([-values[..., half_width:], values[..., :half_width]], -1)
    return values * cosines[:, None, :] + turned * sines[:, None, :]


def rotate_back(grads, cosines, sines):
    half_width = grads.shape[-1] // 2
    scaled = grads * sines[:, None, :]
    return grads * cosines[:, None, :] + jnp.concatenate(
        [scaled[..., half_width:], -scaled[..., :half_width]], -1
    )


def rms_scale(values):
    return lax.rsqrt(jnp.mean(values * values, axis=-1, keepdims=True) + norm_epsilon)


def norm_back(values, scale, gain, dnormed):
    scaled = values * scale
    dgain = jnp.sum(dnormed * scaled, axis=0)
    dscaled = dnormed * gain
    dvalues = scale * (dscaled - scaled * jnp.mean(dscaled * scaled, axis=-1, keepdims=True))
    return (dvalues, dgain)


def masked_scores(grouped, whole_kv, positions, length):
    key_count = whole_kv.shape[0]
    key_width = whole_kv.shape[1] // 2
    heads_kv = grouped.shape[1]
    head_size = grouped.shape[3]
    all_keys = whole_kv[:, :key_width].reshape(key_count, heads_kv, head_size)
    all_values = whole_kv[:, key_width:].reshape(key_count, heads_kv, head_size)
    raw_scores = jnp.einsum(
        "qkgd,pkd->kgqp", grouped, all_keys, preferred_element_type=jnp.float32
    ) * head_size ** (-0.5)
    key_pos = jnp.arange(key_count, dtype=jnp.int32)
    allowed = (key_pos[None, :] <= positions[:, None]) & (key_pos[None, :] < length)
    return (jnp.where(allowed, raw_scores, masked_score), all_keys, all_values)


def adamw(weight, grad, first, second, rate, decay):
    first_new = beta_first * first + (1.0 - beta_first) * grad
    second_new = beta_second * second + (1.0 - beta_second) * grad * grad
    update = (
        first_new
        / (1.0 - beta_first**STEP)
        / (jnp.sqrt(second_new / (1.0 - beta_second**STEP)) + adam_epsilon)
    )
    return (weight - rate * (update + decay * weight), first_new, second_new)


SOURCES = 8
HOSTED = 4
SLOTS = SOURCES * CAP
OUT_BLOCKS = 2


def matmul(a, b, contract):
    return lax.dot_general(
        a, b, (((contract[0],), (contract[1],)), ((), ())), preferred_element_type=f32
    )


def expert_kernel(n_ref, g_ref, w_ref, dn_ref, out_ref, dw_ref, xs, ds, zs, gates):
    step = pl.program_id(0)
    base = lax.axis_index("x") * 8 + lax.axis_index("c")

    @pl.when(step == 0)
    def _():
        lane = lax.broadcasted_iota(jnp.int32, (16, 128), 1)
        sub = lax.broadcasted_iota(jnp.int32, (16, 128), 0)
        wanted = base + 2 * lax.rem(sub, HOSTED) + EXPERTS * (sub // HOSTED)
        choose = jnp.where((lane == wanted) & (sub < 3 * HOSTED), 1.0, 0.0).astype(bf16)
        slot = lax.broadcasted_iota(jnp.int32, (CAP, TOK), 0).astype(f32)

        def source(b, carry):
            fields = matmul(choose, n_ref[b, :, D:], (1, 1))
            hots = []
            for j in range(HOSTED):
                hot = slot == fields[j : j + 1]
                gate = fields[HOSTED + j : HOSTED + j + 1] + fields[2 * HOSTED + j : 2 * HOSTED + j + 1]
                span = pl.ds(pl.multiple_of(j * SLOTS + b * CAP, CAP), CAP)
                gates[span, :] = jnp.broadcast_to(
                    jnp.sum(jnp.where(hot, gate, 0.0), axis=1, keepdims=True), (CAP, 128)
                )
                hots.append(jnp.where(hot, 1.0, 0.0).astype(bf16))
            hots = jnp.concatenate(hots, axis=0)
            x = matmul(hots, n_ref[b, :, :D], (1, 0)).astype(bf16)
            d = matmul(hots, g_ref[b], (1, 0)).astype(bf16)
            for j in range(HOSTED):
                span = pl.ds(pl.multiple_of(j * SLOTS + b * CAP, CAP), CAP)
                xs[span, :] = x[j * CAP : (j + 1) * CAP]
                ds[span, :] = d[j * CAP : (j + 1) * CAP]
            return carry

        lax.fori_loop(0, SOURCES, source, 0)

    @pl.when(step < HOSTED)
    def _():
        expert = base + 2 * step
        rows = pl.ds(pl.multiple_of(step * SLOTS, SLOTS), SLOTS)
        gate = gates[rows, :][:, :1]
        w_gu = w_ref[0, :, : D // 4, :].reshape(D, 2 * FF_E)
        w_d = w_ref[0, :, D // 4 :, :].reshape(FF_E, D)
        gu = matmul(xs[rows, :], w_gu, (1, 0))
        g_part, u_part = gu[:, :FF_E], gu[:, FF_E:]
        sig = 1.0 / (1.0 + jnp.exp(-g_part))
        act = g_part * sig
        hid = (act * u_part).astype(bf16)
        y = matmul(hid, w_d, (1, 0)).astype(bf16).astype(f32)
        dout = ds[rows, :].astype(f32)
        dgate = jnp.sum(y * dout, axis=1, keepdims=True)
        dy = (gate * dout).astype(bf16)
        ds[rows, :] = (gate * y).astype(bf16)
        dh = matmul(dy, w_d, (1, 1))
        da_g = dh * u_part * (sig * (1.0 + g_part * (1.0 - sig)))
        da = jnp.concatenate([da_g, dh * act], axis=1).astype(bf16)
        dw_ref[0, :, D // 4 :, :] = (
            matmul(hid, dy, (0, 0)).astype(bf16).reshape(4, FF_E // 4, D)
        )
        dw_ref[0, :, : D // 4, :] = (
            matmul(xs[rows, :], da, (0, 0)).astype(bf16).reshape(4, D // 4, 2 * FF_E)
        )
        xs[rows, :] = matmul(da, w_gu, (1, 1)).astype(bf16)
        lane = lax.broadcasted_iota(jnp.int32, (SLOTS, 128), 1)
        high = dgate.astype(bf16).astype(f32)
        fields = jnp.where(lane == expert + EXPERTS, dgate - high, 0.0)
        zs[rows, :] = jnp.where(lane == expert, high, fields).astype(bf16)

    @pl.when(step >= HOSTED)
    def _():
        slot = lax.broadcasted_iota(jnp.int32, (TOK, HOSTED * CAP), 1)
        lane = lax.broadcasted_iota(jnp.int32, (TOK, 128), 1)
        for i in range(OUT_BLOCKS):
            b = (step - HOSTED) * OUT_BLOCKS + i
            meta = n_ref[b, :, D:].astype(f32)
            target = jnp.full((TOK, HOSTED * CAP), -1.0, f32)
            for j in reversed(range(HOSTED)):
                mine = lane == base + 2 * j
                rank = jnp.sum(jnp.where(mine, meta, 0.0), axis=1, keepdims=True)
                rank = jnp.where(rank < 0.0, -1.0, rank + j * CAP)
                target = jnp.where(slot < (j + 1) * CAP, rank, target)
            spread = jnp.where(slot.astype(f32) == target, 1.0, 0.0).astype(bf16)
            spans = [pl.ds(pl.multiple_of(j * SLOTS + b * CAP, CAP), CAP) for j in range(HOSTED)]
            for ref, out in ((xs, dn_ref.at[i, :, :D]), (zs, dn_ref.at[i, :, D:]), (ds, out_ref.at[i])):
                rows = jnp.concatenate([ref[span, :] for span in spans], axis=0)
                out[...] = matmul(spread, rows, (1, 0)).astype(bf16)


def experts(n_all, g_all, weights):
    wide = n_all.shape[2]
    slots = HOSTED * SLOTS

    def block(width):
        return pl.BlockSpec(
            (OUT_BLOCKS, TOK, width), lambda i: (jnp.maximum(i - HOSTED, 0), 0, 0)
        )

    def fixed(shape):
        return pl.BlockSpec(shape, lambda i: (0, 0, 0), pipeline_mode=pl.Buffered(1))

    def one(shape):
        return pl.BlockSpec((1,) + shape[1:], lambda i: (jnp.minimum(i, HOSTED - 1), 0, 0, 0))

    return pl.pallas_call(
        expert_kernel,
        grid=(HOSTED + SOURCES // OUT_BLOCKS,),
        out_shape=[
            jax.ShapeDtypeStruct(n_all.shape, bf16),
            jax.ShapeDtypeStruct(g_all.shape, bf16),
            jax.ShapeDtypeStruct(weights.shape, bf16),
        ],
        in_specs=[fixed(n_all.shape), fixed(g_all.shape), one(weights.shape)],
        out_specs=[block(wide), block(D), one(weights.shape)],
        scratch_shapes=[
            pltpu.VMEM((slots, D), bf16),
            pltpu.VMEM((slots, D), bf16),
            pltpu.VMEM((slots, 128), bf16),
            pltpu.VMEM((slots, 128), f32),
        ],
        compiler_params=pltpu.CompilerParams(
            dimension_semantics=("arbitrary",), vmem_limit_bytes=62 * 1024 * 1024
        ),
        cost_estimate=pl.CostEstimate(
            flops=slots * D * FF_E * 18, bytes_accessed=45_000_000, transcendentals=0
        ),
        name="experts",
    )(n_all, g_all, weights)


def turned_rows(u, cos, sin, back):
    lane = lax.broadcasted_iota(jnp.int32, (1, 128), 1)
    first = lax.rem(lane, HEAD_DIM) < HEAD_DIM // 2
    pieces = []
    for j in range(u.shape[1] // 128):
        v = u[:, j * 128 : (j + 1) * 128]
        w = v * sin if back else v
        ahead = pltpu.roll(w, 128 - HEAD_DIM // 2, 1)
        behind = pltpu.roll(w, HEAD_DIM // 2, 1)
        if back:
            pieces.append(v * cos + jnp.where(first, ahead, -behind))
        else:
            pieces.append(v * cos + jnp.where(first, -ahead, behind) * sin)
    return jnp.concatenate(pieces, axis=1)


def unpack_into(out, packed):
    def chunk(i, carry):
        x = packed[pl.ds(i * 16, 16), :, :512].astype(f32)
        rows = pl.ds(pl.multiple_of(i * 128, 128), 128)
        out[rows, :512] = x[:, :8].reshape(128, 512).astype(bf16)
        out[rows, 512:] = x[:, 8:].reshape(128, 512).astype(bf16)
        return carry

    lax.fori_loop(0, 8, chunk, 0)


def gain_rows(small):
    lane = lax.broadcasted_iota(jnp.int32, (8, 128), 1)
    sub = lax.broadcasted_iota(jnp.int32, (8, 128), 0)
    choose = (lane == EXPERTS + sub).astype(f32).astype(bf16)
    return matmul(choose, small, (1, 1))


def fill_bias(bias, length, first_row):
    rows = lax.broadcasted_iota(jnp.int32, bias.shape, 0) + first_row
    keys = lax.broadcasted_iota(jnp.int32, bias.shape, 1)
    bias[...] = jnp.where((keys <= rows) & (keys < length), 0.0, masked_score)


def front_steps(
    z, length, need, wq_p, wkv_p, wo_p, tok, routes, cos, sin, outs, n_held, bias
):
    need, keep = need
    n_out, n1, q_out, kv_out, lse_out, ho_out, r_out, gate_out, wq, wkv, wo, small_out = outs
    width = KV_HEADS * HEAD_DIM
    need("k")
    unpack_into(wkv, wkv_p)

    def small_chunk(i, carry):
        x = wkv_p[pl.ds(i * 16, 16), :, 512:].astype(f32)
        rows = pl.ds(pl.multiple_of(i * 128, 128), 128)
        small_out[rows, :] = x[:, :8].reshape(128, 128).astype(bf16)
        return carry

    lax.fori_loop(0, 8, small_chunk, 0)
    keep("wkv")
    gains = gain_rows(small_out[...])

    def block(by):
        b = lax.rem(z + by, 4)
        x = tok[b].astype(f32)
        normed = (x * rms_scale(x) * gains[0:1]).astype(bf16)
        rows = pl.ds(pl.multiple_of(b * TOK, TOK), TOK)
        n1[rows, :] = normed
        kv = matmul(normed, wkv[...], (1, 0))
        kv_out[rows, :width] = turned_rows(
            kv[:, :width], cos[rows, :], sin[rows, :], False
        ).astype(bf16)
        kv_out[rows, width:] = kv[:, width:].astype(bf16)

    block(0)
    yield
    fill_bias(bias, length[0], z * TOK)
    need("q")
    unpack_into(wq, wq_p)
    keep("wq")
    own = pl.ds(pl.multiple_of(z * TOK, TOK), TOK)
    q = matmul(n1[own, :], wq[...], (1, 0))
    q = turned_rows(q, cos[own, :], sin[own, :], False).astype(bf16)
    q_out[...] = q * jnp.asarray(HEAD_DIM ** (-0.5), bf16)
    lse_out[...] = jnp.zeros_like(lse_out)
    lane = lax.broadcasted_iota(jnp.int32, (TOK, 128), 1)
    yield
    need("t")
    for by in (1, 3, 2):
        block(by)
        yield
    keep("n1")
    keep("kv")

    def heads(j):
        keys = kv_out[:, pl.ds(j * 128, 128)]
        values = kv_out[:, pl.ds(width + j * 128, 128)]
        for g in (0, 1):
            span = pl.ds(j * 256 + g * 128, 128)
            qs = q_out[:, span]
            key = keys[:, g * HEAD_DIM : (g + 1) * HEAD_DIM]
            value = values[:, g * HEAD_DIM : (g + 1) * HEAD_DIM]
            mixed = []
            for h in (0, 1):
                s = matmul(qs[:, h * HEAD_DIM : (h + 1) * HEAD_DIM], key, (1, 1)) + bias[...]
                top = jnp.max(s, axis=1, keepdims=True)
                p = jnp.exp(s - top)
                total = jnp.sum(p, axis=1, keepdims=True)
                p = (p * (1.0 / total)).astype(bf16)
                mixed.append(matmul(p, value, (1, 0)))
                head = j * 4 + g * 2 + h
                lse_out[...] = jnp.where(lane == head, top + jnp.log(total), lse_out[...])
            ho_out[:, span] = jnp.concatenate(mixed, axis=1).astype(bf16)

    for j in range(4):
        heads(j)
        yield
    need("o")
    unpack_into(wo, wo_p)
    keep("wo")
    r = tok[z].astype(f32) + matmul(ho_out[...], wo[...], (1, 0))
    r_out[...] = r
    n2 = (r * rms_scale(r) * gains[1:2]).astype(bf16)
    n_out[:, :D] = n2
    n_held[:, :D] = n2
    logits = matmul(n2, small_out[...], (1, 0))
    hits = lane == routes[:, 0:1]
    for k in range(1, routes.shape[1]):
        hits = hits | (lane == routes[:, k : k + 1])
    lifted = jnp.where(hits, logits, masked_score)
    lifted = jnp.where(hits, jnp.exp(lifted - jnp.max(lifted, axis=1, keepdims=True)), 0.0)
    gate = lifted / jnp.sum(lifted, axis=1, keepdims=True)
    gate_out[...] = gate
    row = lax.broadcasted_iota(jnp.int32, (TOK, TOK), 0)
    col = lax.broadcasted_iota(jnp.int32, (TOK, TOK), 1)
    earlier = jnp.where(col < row, 1.0, 0.0).astype(bf16)
    ranks = matmul(earlier, jnp.where(hits, 1.0, 0.0).astype(bf16), (1, 0))
    high = gate.astype(bf16).astype(f32)
    meta = jnp.where(hits, ranks, jnp.where(lane < EXPERTS, -1.0, 0.0))
    meta = meta + pltpu.roll(high, EXPERTS, 1) + pltpu.roll(gate - high, 2 * EXPERTS, 1)
    meta = meta.astype(bf16)
    n_out[:, D:] = meta
    n_held[:, D:] = meta


GATHER_ORDERS = {"k": "zyx", "q": "zxy", "o": "zyx"}
FRONT_SCHEDULE = "kqtodkqokqotkqdokqotdfqofdffodffffdffff"


def front_kernel(
    length, tok, dout, w_kv, w_q, w_o, small, routes, cos, sin,
    n_out, q_out, lse_out, ho_out, r_out, gate_out, small_out,
    n1_far, kv_far, wq_far, wkv_far, wo_far, tok_far, dout_far, n_all,
    n1, kv, wq, wkv, wo,
    wkv_p, wq_p, wo_p, tok_held, dout_held, n_held, bias, *sems,
):
    at = place()
    wires = Wires(*sems)
    own_tok = wires.keep(tok, tok_held.at[at["z"]])
    own_dout = wires.keep(dout, dout_held.at[at["x"], at["c"]])
    steps = {}
    for name, src, out in (("k", w_kv, wkv_p), ("q", w_q, wq_p), ("o", w_o, wo_p)):
        block = out.at[index(at, "")]
        block[:, :512] = jnp.concatenate([src[:, :512], src[:, 512:]], axis=0).astype(bf16)
        if name == "k":
            block[:, 512:] = small[...].astype(bf16)
        steps[name] = weight_steps(wires, at, [(out, GATHER_ORDERS[name])])
    steps["t"] = token_steps(wires, at, tok_held)
    steps["d"] = row_steps(wires, at, dout_held, dout_far)
    flat = [p.reshape(128, *p.shape[-2:]) for p in (wq_p, wkv_p, wo_p)]
    outs = (n_out, n1, q_out, kv, lse_out, ho_out, r_out, gate_out, wq, wkv, wo, small_out)
    kept = []
    results = {
        "n1": (n1, n1_far),
        "kv": (kv, kv_far),
        "wq": (wq, wq_far),
        "wkv": (wkv, wkv_far),
        "wo": (wo, wo_far),
    }

    def need(name):
        for _ in steps[name]:
            pass
        if name == "t":
            kept.append(wires.keep(tok_held, tok_far))

    def keep(name):
        kept.append(wires.keep(*results[name]))

    steps["f"] = front_steps(
        at["z"], length, (need, keep), *flat, tok_held, routes, cos, sin, outs,
        n_held.at[at["x"], at["c"]], bias,
    )
    greet(at, "xyzc")
    own_tok.wait()
    own_dout.wait()
    in_order(FRONT_SCHEDULE, **steps)
    in_order("", n=row_steps(wires, at, n_held, n_all, True))
    for copy in kept:
        copy.wait()
    wires.finish()


def front(length, w_kv, w_q, w_o, small, tok, dout, routes, cos, sin):
    vmem = pl.BlockSpec(memory_space=pltpu.VMEM)
    far = pl.BlockSpec(memory_space=pltpu.HBM)
    rows = jax.ShapeDtypeStruct((TOK, D), bf16)
    lanes = jax.ShapeDtypeStruct((TOK, 128), f32)
    lead = (4, 4, 2, 4)
    copies = WEIGHT_COPIES + TOKEN_COPIES + 2 * ROW_COPIES
    return pl.pallas_call(
        front_kernel,
        out_shape=[
            jax.ShapeDtypeStruct((TOK, D + 128), bf16),
            rows,
            lanes,
            rows,
            jax.ShapeDtypeStruct((TOK, D), f32),
            lanes,
            jax.ShapeDtypeStruct((D, 128), bf16),
        ]
        + [pltpu.HBM((D, D), bf16)] * 5
        + [
            pltpu.HBM((4, TOK, D), bf16),
            pltpu.HBM((4, 2, TOK, D), bf16),
            pltpu.HBM((4, 2, TOK, D + 128), bf16),
        ],
        in_specs=[pl.BlockSpec(memory_space=pltpu.SMEM)] + [far] * 2 + [vmem] * 7,
        out_specs=[vmem] * 7 + [far] * 8,
        scratch_shapes=[pltpu.VMEM((D, D), bf16)] * 5
        + [
            pltpu.VMEM(lead + (16, 512 + 128), bf16),
            pltpu.VMEM(lead + (16, 512), bf16),
            pltpu.VMEM(lead + (16, 512), bf16),
            pltpu.VMEM((4, TOK, D), bf16),
            pltpu.VMEM((4, 2, TOK, D), bf16),
            pltpu.VMEM((4, 2, TOK, D + 128), bf16),
            pltpu.VMEM((TOK, 4 * TOK), f32),
        ]
        + wire_sems(copies, 2 + 6 + 2 * ROW_KEPT),
        compiler_params=pltpu.CompilerParams(
            collective_id=1, has_side_effects=True, vmem_limit_bytes=60 * 1024 * 1024
        ),
        cost_estimate=pl.CostEstimate(
            flops=10**10, bytes_accessed=30_000_000, transcendentals=5_000_000
        ),
        name="front",
    )(length, *hbm(tok, dout), w_kv, w_q, w_o, small, routes, cos, sin)


def rms_back(values, scale, gain, dnormed):
    scaled = values * scale
    dscaled = dnormed * gain
    dvalues = scale * (dscaled - scaled * jnp.mean(dscaled * scaled, axis=-1, keepdims=True))
    return dvalues, jnp.sum(dnormed * scaled, axis=0, keepdims=True)


def pack_into(out, value):
    def chunk(i, carry):
        rows = pl.ds(pl.multiple_of(i * 128, 128), 128)
        left = value[rows, :512].reshape(16, 8, 512)
        right = value[rows, 512:].reshape(16, 8, 512)
        out[pl.ds(i * 16, 16), :, :512] = jnp.concatenate([left, right], axis=1).astype(bf16)
        return carry

    lax.fori_loop(0, 8, chunk, 0)


def back_steps(
    z, length, sums, dout, n_ext, r_ref, gate_ref, ho, q_ref, kv, lse, n1, wo, small,
    cos, sin, cos_t, sin_t, late,
    dwq_p, dwkv_p, dwo_p, dg_p, dn1_out, dr_out,
    bias, square, dq_s, do_s, dkv_s,
):
    own = pl.ds(pl.multiple_of(z * TOK, TOK), TOK)
    gains = gain_rows(small[...])
    lane = lax.broadcasted_iota(jnp.int32, (TOK, 128), 1)
    gate = gate_ref[...]
    fields = sums[:, D:]
    dgate = fields + pltpu.roll(fields, 128 - EXPERTS, 1)
    mean = jnp.sum(gate * dgate, axis=1, keepdims=True)
    dlogits = (gate * (dgate - mean)).astype(bf16)
    dn2 = sums[:, :D] + matmul(dlogits, small[...], (1, 1))
    r = r_ref[...]
    dr, dg2 = rms_back(r, rms_scale(r), gains[1:2], dn2)
    dr = dr + dout[...].astype(f32)
    dr_out[...] = dr
    d_att = dr.astype(bf16)
    square[...] = matmul(ho[...], d_att, (0, 0))
    pack_into(dwo_p, square)
    spread_gain(dwo_p.at[:, :, 512:], dg2, EXPERTS, matmul(n_ext[:, :D], dlogits, (0, 0)))
    yield
    do_s[...] = matmul(d_att, wo[...], (1, 1)).astype(bf16)
    fill_bias(bias, length[0], z * TOK)
    width = KV_HEADS * HEAD_DIM
    scale = HEAD_DIM ** (-0.5)
    dkv_t = square

    def heads(j):
        keys = kv[:, pl.ds(j * 128, 128)]
        values = kv[:, pl.ds(width + j * 128, 128)]
        for g in (0, 1):
            span = pl.ds(j * 256 + g * 128, 128)
            qs, dos = q_ref[:, span], do_s[:, span]
            prods = dos.astype(f32) * ho[:, span].astype(f32)
            key = keys[:, g * HEAD_DIM : (g + 1) * HEAD_DIM]
            value = values[:, g * HEAD_DIM : (g + 1) * HEAD_DIM]
            dqs = []
            dk_t, dv_t = 0.0, 0.0
            for h in (0, 1):
                part = slice(h * HEAD_DIM, (h + 1) * HEAD_DIM)
                head = j * 4 + g * 2 + h
                shift_by = jnp.sum(jnp.where(lane == head, lse[...], 0.0), axis=1, keepdims=True)
                mine = (lane >= h * HEAD_DIM) & (lane < (h + 1) * HEAD_DIM)
                delta = jnp.sum(jnp.where(mine, prods, 0.0), axis=1, keepdims=True)
                p = jnp.exp(matmul(qs[:, part], key, (1, 1)) + bias[...] - shift_by)
                dp = matmul(dos[:, part], value, (1, 1))
                ds = (p * (dp - delta)).astype(bf16)
                dqs.append(matmul(ds, key, (1, 0)) * scale)
                dk_t = dk_t + matmul(qs[:, part], ds, (0, 0))
                dv_t = dv_t + matmul(dos[:, part], p.astype(bf16), (0, 0))
            dq_s[:, span] = jnp.concatenate(dqs, axis=1)
            half = HEAD_DIM // 2
            wave = dk_t * sin_t[...]
            dk_t = dk_t * cos_t[...] + jnp.concatenate([wave[half:], -wave[:half]], axis=0)
            at = j * 128 + g * HEAD_DIM
            dkv_t[pl.ds(at, HEAD_DIM), :] = dk_t
            dkv_t[pl.ds(width + at, HEAD_DIM), :] = dv_t

    for j in range(4):
        heads(j)
        yield

    def flip(i, carry):
        at = pl.ds(pl.multiple_of(i * 128, 128), 128)
        dkv_s[:, at] = jnp.transpose(dkv_t[at, :]).astype(bf16)
        return carry

    lax.fori_loop(0, 8, flip, 0)
    square[...] = matmul(n1[...], dkv_s[...], (0, 0))
    pack_into(dwkv_p, square)
    yield
    dq = turned_rows(dq_s[...], cos[...], sin[...], True).astype(bf16)
    square[...] = matmul(n1[own, :], dq, (0, 0))
    pack_into(dwq_p, square)
    yield
    wq, wkv, tok = late()
    for b in range(4):
        columns = slice(b * TOK, (b + 1) * TOK)
        square[:, columns] = matmul(dkv_s[...], wkv[b, :, :D], (1, 1))
        square[own, columns] += matmul(dq, wq[b, :, :D], (1, 1))
    for b in range(4):
        dn1_out[b] = square[b * TOK : (b + 1) * TOK, :].astype(bf16)
    yield
    dg1 = jnp.zeros((1, D), f32)
    for b in range(4):
        x = tok[b, :, :D].astype(f32)
        dn1 = square[b * TOK : (b + 1) * TOK, :]
        dg1 = dg1 + jnp.sum(dn1 * (x * rms_scale(x)), axis=0, keepdims=True)
    spread_gain(dg_p, dg1, 0, None)


def spread_gain(out, row, lane, rest):
    sub = lax.broadcasted_iota(jnp.int32, (8, D), 0)
    rows = jnp.where(sub == 0, row, 0.0)
    high = rows.astype(bf16)
    low = (rows - high.astype(f32)).astype(bf16)
    place_lane = lax.broadcasted_iota(jnp.int32, (8, 128), 1)
    place_sub = lax.broadcasted_iota(jnp.int32, (8, 128), 0)
    spread = jnp.where((place_lane == lane) & (place_sub == 0), 1.0, 0.0).astype(bf16)
    value = matmul(high, spread, (0, 0)) + matmul(low, spread, (0, 0))
    if rest is not None:
        value = value + rest
    value = value.reshape(128, 8, 128)
    out[...] = jnp.concatenate([value, jnp.zeros_like(value)], axis=1).astype(bf16)


BACK_INPUTS = 15
BACK_ORDERS = {"a": "xyz", "k": "xzy", "o": "xyz", "g": "xyz"}


def back_kernel(length, dn_parts, out_parts, wq, wkv, tok, *refs):
    loaded = refs[:BACK_INPUTS]
    refs = refs[BACK_INPUTS:]
    g_q, g_kv, g_o, g_small, g_g, dr_out, layer_out = refs[:7]
    sums, dn1, bias, square, dq_s, do_s, dkv_s = refs[7:14]
    mixed = sums.at[:, pl.ds(0, D)]
    dn_bufs, out_bufs, dn1_bufs = refs[14:19], refs[19:24], refs[24:27]
    q_bufs, kv_bufs, o_bufs, g_bufs = (refs[27 + 7 * i : 34 + 7 * i] for i in range(4))
    inputs = refs[55 : 55 + BACK_INPUTS]
    dn1_sum = refs[55 + BACK_INPUTS]
    at = place()
    wires = Wires(*refs[56 + BACK_INPUTS :])

    def unpacked(out, small=None):
        def write(value):
            out[:, :512] = value[:8, :512]
            out[:, 512:] = value[8:, :512]
            if small is not None:
                small[...] = value[:8, 512:]

        return write

    def gain_column(value):
        g_g[...] = value[:8]
    greet(at, "xyzc")

    def backward():
        for copy in arriving:
            copy.wait()
        wires.finish()
        yield from back_steps(
            at["z"], length, sums, *inputs, late,
            *(bufs[0].reshape(128, *bufs[0].shape[-2:]) for bufs in (q_bufs, kv_bufs, o_bufs, g_bufs)),
            dn1, dr_out, bias, square, dq_s, do_s, dkv_s,
        )

    late_spots = (out_bufs[1], dn_bufs[0], dn_bufs[1])
    late_copies = []

    def load_late():
        for src, dst in ((wkv, dn_bufs[0]), (tok, dn_bufs[1]), (wq, out_bufs[1])):
            late_copies.append(wires.keep(src, dst.at[:, :, pl.ds(0, D)]))
        yield

    def late():
        for copy in late_copies:
            copy.wait()
        return late_spots

    steps = {
        "n": row_sum_steps(wires, at, dn_parts, sums, *dn_bufs),
        "l": row_sum_steps(wires, at, out_parts, mixed, *out_bufs),
        "z": ring_sum_steps(wires, at, "z", dn1, dn1_sum, *dn1_bufs),
        "a": matrix_steps(wires, at, BACK_ORDERS["a"], q_bufs[0], unpacked(g_q), *q_bufs[1:]),
        "k": matrix_steps(wires, at, BACK_ORDERS["k"], kv_bufs[0], unpacked(g_kv), *kv_bufs[1:]),
        "o": matrix_steps(wires, at, BACK_ORDERS["o"], o_bufs[0], unpacked(g_o, g_small), *o_bufs[1:]),
        "g": matrix_steps(wires, at, BACK_ORDERS["g"], g_bufs[0], gain_column, *g_bufs[1:]),
        "e": load_late(),
        "b": backward(),
    }
    next(steps["n"])
    own = pl.ds(pl.multiple_of(at["z"] * TOK, TOK), TOK)
    arriving = [
        wires.keep(src.at[own] if src.shape != dst.shape else src, dst)
        for src, dst in zip(loaded, inputs)
    ]
    in_order(BACK_SCHEDULE, **steps)
    residual, small = inputs[2], inputs[10]
    layer_out[...] = (residual[...] + mixed[...]).astype(bf16)
    x = late_spots[2][at["z"], :, :D].astype(f32)
    dx, _ = rms_back(x, rms_scale(x), gain_rows(small[...])[0:1], dn1_sum[...])
    dr_out[...] += dx
    wires.finish()


BACK_SCHEDULE = "l" + "nnnn" + "bo" + "le" + "bo" + "b" + "b" + "bl" + "bk" + "bak" + "bzzao" + "bg" + "kzgkoagakgolz"


def back(length, dn_parts, out_parts, wq, wkv, tok, *inputs):
    vmem = pl.BlockSpec(memory_space=pltpu.VMEM)
    far = pl.BlockSpec(memory_space=pltpu.HBM)
    wide = dn_parts.shape[-1]
    widths = (512, 512, 640, 128)
    copies = 2 * ROW_SUM_COPIES + RING_SUM_COPIES + 4 * MATRIX_COPIES
    scratch = [
        pltpu.VMEM((TOK, wide), f32),
        pltpu.VMEM((4, TOK, D), bf16),
        pltpu.VMEM((TOK, 4 * TOK), f32),
        pltpu.VMEM((D, D), f32),
        pltpu.VMEM((TOK, D), f32),
        pltpu.VMEM((TOK, D), bf16),
        pltpu.VMEM((D, D), bf16),
    ]
    scratch += row_sum_scratch(TOK, wide) + row_sum_scratch(TOK, D) + ring_sum_scratch(TOK, D)
    for width in widths:
        scratch += matrix_scratch(width)
    scratch += [
        pltpu.VMEM((TOK, 128) if v.shape == (4 * TOK, 128) and v.dtype == f32 else v.shape, v.dtype)
        for v in inputs
    ]
    scratch.append(pltpu.VMEM((TOK, D), f32))
    return pl.pallas_call(
        back_kernel,
        out_shape=[jax.ShapeDtypeStruct((8, D), f32)] * 3
        + [jax.ShapeDtypeStruct((8, 128), f32)] * 2
        + [jax.ShapeDtypeStruct((TOK, D), f32), jax.ShapeDtypeStruct((TOK, D), bf16)],
        in_specs=[pl.BlockSpec(memory_space=pltpu.SMEM)] + [far] * (5 + BACK_INPUTS),
        out_specs=[vmem] * 7,
        scratch_shapes=scratch + wire_sems(copies, 8 + 3 + BACK_INPUTS),
        compiler_params=pltpu.CompilerParams(
            collective_id=4, has_side_effects=True, vmem_limit_bytes=63 * 1024 * 1024
        ),
        cost_estimate=pl.CostEstimate(
            flops=2 * 10**10, bytes_accessed=40_000_000, transcendentals=5_000_000
        ),
        name="back",
    )(length, *hbm(dn_parts, out_parts, wq, wkv, tok, *inputs))


def rotary_constants(count):
    half = HEAD_DIM // 2
    freqs = (10000.0 ** (-np.arange(half, dtype=np.float64) / half)).astype(np.float32)
    angles = np.arange(count, dtype=np.float32)[:, None] * freqs[None, :]
    tables = np.cos(angles.astype(np.float64)), np.sin(angles.astype(np.float64))
    return tuple(np.concatenate([t, t], 1).astype(np.float32) for t in tables)


def body(
    tokens, routes, lengths, out_grad,
    query_weight, query_mean, query_square,
    keyval_weight, keyval_mean, keyval_square,
    output_weight, output_mean, output_square,
    router_weight, router_mean, router_square,
    norm_gains, gains_mean, gains_square,
    gateup_weight, gateup_mean, gateup_square,
    down_weight, down_mean, down_square,
):
    row_count = tokens.shape[0]
    seq_len = row_count * 4
    query_width = HEADS * HEAD_DIM

    expert_b = lax.all_gather(
        jnp.concatenate([gateup_weight[0], down_weight[0]], axis=0).astype(bf16),
        ("y", "z"),
        axis=0,
    )
    small = jnp.concatenate(
        [router_weight, norm_gains.T, jnp.zeros((8, 128 - EXPERTS - 2), f32)], axis=1
    )
    small = jnp.concatenate([small, jnp.zeros((8, 128), f32)], axis=0)
    cos, sin = rotary_constants(seq_len)
    cos2, sin2, cos_t, sin_t = (
        jnp.asarray(table)
        for table in (np.tile(cos, (1, 2)), np.tile(sin, (1, 2)), cos.T.copy(), sin.T.copy())
    )
    (
        n_ext, q, lse, ho, residual, gate, small_b,
        n1, kv, query_b, keyval_b, output_b, all_tokens, dout_all, n_all,
    ) = front(
        lengths,
        keyval_weight,
        query_weight,
        output_weight,
        small,
        tokens,
        out_grad,
        routes,
        cos2,
        sin2,
    )
    wide = n_all.shape[-1]
    n_all = n_all.reshape(SOURCES, row_count, wide)
    dn_parts, out_parts, d_expert = experts(
        n_all,
        dout_all.reshape(SOURCES, row_count, D),
        expert_b.reshape((4,) + (4, D // 4 + FF_E // 4, D)),
    )
    grad_expert = lax.psum_scatter(
        d_expert.reshape((16,) + d_expert.shape[2:]),
        ("y", "z"),
        scatter_dimension=0,
        tiled=False,
    ).astype(f32)
    grad_query, grad_keyval, grad_output, g_small, g_gain, tokens_grad, layer_out = back(
        lengths,
        dn_parts.reshape(4, 2, row_count, wide),
        out_parts.reshape(4, 2, row_count, D),
        query_b.reshape(4, row_count, D),
        keyval_b.reshape(4, row_count, D),
        all_tokens,
        out_grad, n_ext, residual, gate, ho, q, kv, lse, n1, output_b, small_b,
        cos2, sin2, cos_t, sin_t,
    )
    grad_router = g_small[:, :EXPERTS]
    grad_gains = jnp.stack([g_gain[:, 0], g_small[:, EXPERTS]])

    rate = 0.5
    query_new = adamw(query_weight, grad_query, query_mean, query_square, rate * D ** (-0.5), 0.1)
    keyval_new = adamw(
        keyval_weight, grad_keyval, keyval_mean, keyval_square, rate * D ** (-0.5), 0.1
    )
    output_new = adamw(
        output_weight,
        grad_output,
        output_mean,
        output_square,
        rate * max(1, 2 * query_width // seq_len) ** (-0.5),
        0.1,
    )
    router_new = adamw(
        router_weight, grad_router, router_mean, router_square, rate * (4 * D) ** (-0.5), 0.1
    )
    gains_new = adamw(norm_gains, grad_gains, gains_mean, gains_square, 0.6, 0.0)
    gateup_new = adamw(
        gateup_weight,
        grad_expert[None, : D // 4],
        gateup_mean,
        gateup_square,
        rate * D ** (-0.5),
        0.1,
    )
    down_new = adamw(
        down_weight,
        grad_expert[None, D // 4 :],
        down_mean,
        down_square,
        rate * (FF_E // 8) ** (-0.5),
        0.1,
    )
    return (
        (layer_out, tokens_grad)
        + query_new
        + keyval_new
        + output_new
        + router_new
        + gains_new
        + gateup_new
        + down_new
    )


def solution(mesh):
    devices = jax.sharding.Mesh(mesh.devices.reshape(4, 4, 2, 4), ("x", "y", "c", "z"))
    every = ("x", "y", "c", "z")
    rows = P(every, None)
    gains = P(None, every)
    shard = P(("x", "y", "c"), "z", None)
    return jax.shard_map(
        body,
        mesh=devices,
        in_specs=(rows, rows, P(("x", "y", "c")), rows)
        + (rows,) * 12
        + (gains,) * 3
        + (shard,) * 6,
        out_specs=(rows, rows) + (rows,) * 12 + (gains,) * 3 + (shard,) * 6,
        check_vma=False,
    )
```
